32 devices in a mesh: groups: 2 (over y), store: 4 (over z), tensor: 4 (over x, core).
Axes of the slice: x: 2, y: 2, z: 4, core: 2. Of those that a mesh axis runs over, the one named last changes fastest.
Arguments:
- queries: bfloat16 [8, 256, 8192], P(('groups', 'store'), None, 'tensor'), parts along dimension 0, may hold values from -96 to 96
- question_kv: bfloat16 [8, 256, 2048], P(('groups', 'store'), None, 'tensor'), parts along dimension 0, may hold values from -4.2 to 4.2
- key_value_store: bfloat16 [64, 256, 2048], P(('groups', 'store'), None, 'tensor'), parts along dimension 0, may hold values from -6 to 6
- span_store_slot: int32 [64], P('groups'), parts along dimension 0, may hold values from 0 to 31, as said below
- retrieval: int32 [8, 16], P('groups'), parts along dimension 0, may hold values from 0 to 31, as said below
- recompute_rows: int32 [8, 16, 8], P(('groups', 'store')), parts along dimension 0, may hold values from 0 to 255, as said below
- recompute_hidden: bfloat16 [8, 16, 8, 8192], P(('groups', 'store')), parts along dimension 0, may hold values from -6 to 6
- kv_weight: bfloat16 [8192, 2048], P('store', 'tensor'), may hold values from -0.0625 to 0.0625
Outputs:
- attended: bfloat16 [8, 256, 8192], P(('groups', 'store'), None, 'tensor'), parts along dimension 0
- fresh_kv: bfloat16 [8, 16, 8, 2048], P(('groups', 'store'), None, None, 'tensor'), parts along dimension 0
The draws below stay inside these ranges and needn't reach their ends.
There are 2 independent parts, one for each index of `groups`. The reference program is written for one: setup_inputs(seed, part) draws one part's arguments, and reference() takes and returns one part's arrays. A program takes and returns all parts, laid end to end along the dimension named above; an argument that names none is the same for every part. Nothing has to cross between parts.
Inputs may be any that keep to these rules, and one draw needn't show every extreme that they name: A permutation: span c is kept in store slot span_store_slot[c], and slot g lies with store index g // 8. `retrieval`: span ids; the spans of one request lie on at most 4 per store index, and every request reaches that number on some store index; spans of one request are distinct. `recompute_rows`: distinct within each request's span.
All inputs are finite; a program needn't handle non-finite values.
Results may differ from the reference program's by a relative error of at most 0.0051.
Values may be sent and summed in bfloat16 or wider, within the bound.
No kernel may reach another device: no remote copies, remote signals or barrier semaphores. Data moves between devices by JAX's collectives and lax.ppermute only.
A program may use at most 128 MiB of HBM per device.

```python
import jax
import jax.numpy as jnp
from jax import lax

D = 8192
HEADS = 64
KEY_VALUE_HEADS = 8
HEAD_WIDTH = 128
QLEN = 256
SPAN_TOKENS = 256
SPANS_REQ = 16
RECOMP = 8
SLOTS = 8
REQUESTS = 4
STORE_SLOTS = 32
N_STORE = 4


def store_layout(key):
    return jax.random.permutation(jax.random.fold_in(key, 201), STORE_SLOTS).astype(jnp.int32)


def drawn_question(key):
    shape = (REQUESTS, QLEN, KEY_VALUE_HEADS, 2, HEAD_WIDTH)
    return jnp.clip(jax.random.normal(jax.random.fold_in(key, 101), shape, jnp.float32), -4.0, 4.0)


def draw_question_kv(key, part):
    rows = drawn_question(key)
    return rows.reshape(REQUESTS, QLEN, KEY_VALUE_HEADS * 2 * HEAD_WIDTH).astype(jnp.bfloat16)


def draw_queries(key, part):
    own = jax.random.fold_in(key, 7)
    base = jnp.clip(2.5 * jax.random.normal(own, (REQUESTS, QLEN, HEADS, HEAD_WIDTH), jnp.float32), -12.0, 12.0)
    return base.reshape(REQUESTS, QLEN, HEADS * HEAD_WIDTH).astype(jnp.bfloat16)


def draw_span_store_slot(key, part):
    return store_layout(key)


def draw_retrieval(key, part):
    home_slots = store_layout(key)
    own = jax.random.fold_in(key, 11)
    first, second, third = jax.random.split(own, 3)
    popular = jax.random.randint(first, (N_STORE,), 0, 3)
    score = jax.random.randint(second, (REQUESTS, N_STORE), 0, 1024) + 1024 * popular[None, :]
    score = score * N_STORE + jnp.arange(N_STORE)[None, :]
    ranked = jnp.argsort(-score, axis=1).astype(jnp.int32)
    column = jnp.arange(SPANS_REQ)
    owners = ranked[:, column % N_STORE]
    offset = jax.random.randint(third, (REQUESTS, N_STORE), 0, SLOTS)
    place = (offset[:, column % N_STORE] + column // N_STORE) % SLOTS
    global_slot = owners * SLOTS + place
    inverse = jnp.argsort(home_slots).astype(jnp.int32)
    return inverse[global_slot].astype(jnp.int32)


def draw_recompute_rows(key, part):
    own = jax.random.fold_in(key, 13)
    score = jax.random.randint(own, (REQUESTS, SPANS_REQ, SPAN_TOKENS), 0, 1 << 16) * SPAN_TOKENS + jnp.arange(SPAN_TOKENS)
    return jnp.argsort(score, axis=2)[:, :, :RECOMP].astype(jnp.int32)


def block_levels(stream_key, dims, cuts, least, high):
    level = 1.0
    for position, shards_of in cuts:
        heights = jax.random.uniform(jax.random.fold_in(jax.random.fold_in(stream_key, 6), position), (shards_of,), jnp.float32, least / len(cuts), high / len(cuts))
        level = level * jnp.repeat(jnp.exp(heights), dims[position] // shards_of).reshape((-1,) + (1,) * (len(dims) - 1 - position))
    return level


def centred(rng, extent, scale, bound, cuts=(), held_as=jnp.bfloat16):
    entries = scale * jax.random.normal(rng, extent, jnp.float32)
    if cuts:
        entries = entries * block_levels(rng, extent, cuts, -0.22, 0.18)
    return jnp.clip(entries, -bound, bound).astype(held_as)


def setup_inputs(seed: int = 0, part: int = 0) -> dict:
    key_list = jax.random.split(jax.random.key(seed), 9)
    own_keys = jax.random.split(jax.random.fold_in(key_list[8], part), 9)
    return {
        "queries": draw_queries(jax.random.fold_in(jax.random.fold_in(key_list[8], part), 71), part),
        "question_kv": draw_question_kv(jax.random.fold_in(jax.random.fold_in(key_list[8], part), 71), part),
        "key_value_store": centred(own_keys[2], (STORE_SLOTS, SPAN_TOKENS, KEY_VALUE_HEADS * 2 * HEAD_WIDTH), 1.0, 6.0, ((0, 4), (2, 4))),
        "span_store_slot": draw_span_store_slot(jax.random.fold_in(jax.random.fold_in(key_list[8], part), 71), part),
        "retrieval": draw_retrieval(jax.random.fold_in(jax.random.fold_in(key_list[8], part), 71), part),
        "recompute_rows": draw_recompute_rows(jax.random.fold_in(jax.random.fold_in(key_list[8], part), 71), part),
        "recompute_hidden": centred(own_keys[6], (REQUESTS, SPANS_REQ, RECOMP, D), 1.0, 6.0, ((0, 4),)),
        "kv_weight": centred(key_list[7], (D, KEY_VALUE_HEADS * 2 * HEAD_WIDTH), D ** -0.5, 0.0625, ((0, 4), (1, 4))),
    }


def attend_rows(query_block, key_rows, value_rows, visible, score_scale):
    scores = jnp.dot(query_block, key_rows.T, preferred_element_type=jnp.float32) * score_scale
    scores = jnp.where(visible, scores, -jnp.inf)
    highest = jnp.max(scores, axis=1, keepdims=True)
    weights = jnp.exp(scores - highest)
    row_total = jnp.sum(weights, axis=1, keepdims=True)
    blended = jnp.dot(weights.astype(jnp.bfloat16), value_rows, preferred_element_type=jnp.float32)
    return (blended / row_total).astype(jnp.bfloat16)


def reference(queries, question_kv, key_value_store, span_store_slot, retrieval, recompute_rows, recompute_hidden, kv_weight):
    kv_cols = KEY_VALUE_HEADS * 2 * HEAD_WIDTH
    fresh_kv = jnp.dot(recompute_hidden.reshape(REQUESTS * SPANS_REQ * RECOMP, D), kv_weight, preferred_element_type=jnp.float32).astype(jnp.bfloat16)
    fresh_kv = fresh_kv.reshape(REQUESTS, SPANS_REQ, RECOMP, kv_cols)
    home_slots = span_store_slot[retrieval]
    context_len = SPANS_REQ * SPAN_TOKENS
    total_len = context_len + QLEN
    key_place = jnp.arange(total_len, dtype=jnp.int32)
    query_place = jnp.arange(QLEN, dtype=jnp.int32)
    visible = (key_place[None, :] < context_len) | (key_place[None, :] - context_len <= query_place[:, None])
    group_size = HEADS // KEY_VALUE_HEADS
    span_index = jnp.arange(SPANS_REQ, dtype=jnp.int32)

    def one_request(request):
        span_kv = key_value_store[home_slots[request]]
        span_kv = span_kv.at[span_index[:, None], recompute_rows[request]].set(fresh_kv[request])
        context_kv = jnp.concatenate([span_kv.reshape(context_len, kv_cols), question_kv[request]], axis=0)
        context_kv = context_kv.reshape(total_len, KEY_VALUE_HEADS, 2, HEAD_WIDTH)
        query_rows = queries[request].reshape(QLEN, HEADS, HEAD_WIDTH)

        def one_head(head_index):
            chosen = lax.dynamic_index_in_dim(query_rows, head_index, 1, keepdims=False)
            head_kv = lax.dynamic_index_in_dim(context_kv, head_index // group_size, 1, keepdims=False)
            return attend_rows(chosen, head_kv[:, 0], head_kv[:, 1], visible, HEAD_WIDTH ** -0.5)

        outputs = lax.map(one_head, jnp.arange(HEADS, dtype=jnp.int32))
        return jnp.transpose(outputs, (1, 0, 2)).reshape(QLEN, HEADS * HEAD_WIDTH)

    attended = lax.map(one_request, jnp.arange(REQUESTS, dtype=jnp.int32))
    return attended, fresh_kv
```

```python
import functools
import math

import jax
import jax.numpy as jnp
from jax import lax
from jax.experimental import pallas as pl
from jax.experimental.pallas import tpu as pltpu
from jax.sharding import PartitionSpec as P

HEAD_WIDTH = 128
EXP_SCALE = math.log2(math.e) * HEAD_WIDTH ** (-0.5)
VMEM_LIMIT = 48 * 1024 * 1024


def any_spec():
    return pl.BlockSpec(memory_space=pl.ANY)


def smem_spec():
    return pl.BlockSpec(memory_space=pltpu.SMEM)


def pack_kernel(spans, distances, with_hidden, n_deps, *refs):
    place_ref, slot_ref, retrieval_ref, store_ref = refs[:4]
    refs = refs[4:]
    if with_hidden:
        hidden_ref, refs = refs[0], refs[1:]
    refs = refs[n_deps:]
    n_out = len(spans) * len(distances) + (len(distances) if with_hidden else 0)
    outs, sems = refs[:n_out], refs[n_out]
    myself = place_ref[0]
    slot_count = store_ref.shape[0]
    copies = []

    def send(source, target):
        copy = pltpu.make_async_copy(source, target, sems.at[len(copies)])
        copy.start()
        copies.append(copy)

    place = 0
    if with_hidden:
        for distance in distances:
            target = outs[place]
            rows, width = target.shape
            first_row = pl.multiple_of(place_ref[1] * rows, rows)
            first_column = pl.multiple_of((myself ^ distance) * width, width)
            send(hidden_ref.at[pl.ds(first_row, rows), pl.ds(first_column, width)], target)
            place += 1
    for distance in distances:
        partner = myself ^ distance
        count = jnp.int32(0)
        chosen = [jnp.int32(0) for _ in spans]
        for j in range(retrieval_ref.shape[1]):
            home = slot_ref[retrieval_ref[partner, j]]
            mine = home // slot_count == myself
            for i, span in enumerate(spans):
                chosen[i] = jnp.where(mine & (count == span), home - myself * slot_count, chosen[i])
            count = count + jnp.where(mine, 1, 0)
        for slot in chosen:
            send(store_ref.at[slot], outs[place])
            place += 1
    for copy in copies:
        copy.wait()


def pack(place, slots, retrieval, store, hidden, spans, distances, deps, hidden_shape=None):
    with_hidden = hidden is not None
    _, span_len, kv_cols = store.shape
    shapes = []
    if with_hidden:
        shapes += [jax.ShapeDtypeStruct(hidden_shape, hidden.dtype)] * len(distances)
    shapes += [jax.ShapeDtypeStruct((span_len, kv_cols), store.dtype)] * (len(spans) * len(distances))
    operands = [place, slots, retrieval, store] + ([hidden] if with_hidden else []) + list(deps)
    outs = pl.pallas_call(
        functools.partial(pack_kernel, tuple(spans), tuple(distances), with_hidden, len(deps)),
        out_shape=shapes,
        in_specs=[smem_spec()] * 3 + [any_spec()] * (len(operands) - 3),
        out_specs=[any_spec()] * len(shapes),
        scratch_shapes=[pltpu.SemaphoreType.DMA((len(shapes),))],
        name="pack_spans",
    )(*operands)
    hidden_pieces = outs[: len(distances)] if with_hidden else []
    rest = outs[len(hidden_pieces) :]
    per = len(spans)
    return list(hidden_pieces), [list(rest[i * per : (i + 1) * per]) for i in range(len(distances))]


def attend_kernel(n_pieces, with_question, with_fresh, first, last, n_deps, *refs):
    table_ref, query_ref, question_ref = refs[:3]
    refs = refs[3:]
    piece_refs, refs = refs[:n_pieces], refs[n_pieces:]
    if with_fresh:
        fresh_ref, refs = refs[0], refs[1:]
    if not first:
        blend_in, stats_in = refs[:2]
        refs = refs[2:]
    refs = refs[n_deps:]
    if last:
        out_ref, refs = refs[0], refs[1:]
    else:
        blend_out, stats_out = refs[:2]
        refs = refs[2:]
    keys, values = refs
    width = HEAD_WIDTH
    question_len = query_ref.shape[0]
    group_size = query_ref.shape[1] // width
    span_len = piece_refs[0].shape[0]
    spare_key = question_ref[0:1, :width].astype(jnp.float32)
    row = lax.broadcasted_iota(jnp.int32, (span_len, width), 0)
    for i in range(n_pieces):
        stale = row < jnp.where(table_ref[i, 0] == 0, span_len, 0)
        for column in range(1, table_ref.shape[1]):
            stale = stale | (row == table_ref[i, column])
        here = pl.ds(i * span_len, span_len)
        block = piece_refs[i][...].astype(jnp.float32)
        keys[here, :] = jnp.where(stale, spare_key, block[:, :width]).astype(keys.dtype)
        values[here, :width] = jnp.where(stale, 0.0, block[:, width:]).astype(values.dtype)
        values[here, width:] = jnp.where(stale, 0.0, 1.0).astype(values.dtype)
    base = n_pieces * span_len
    for ref in ([fresh_ref] if with_fresh else []) + ([question_ref] if with_question else []):
        here = pl.ds(base, ref.shape[0])
        keys[here, :] = ref[:, :width]
        values[here, :width] = ref[:, width:]
        values[here, width:] = jnp.ones((ref.shape[0], width), values.dtype)
        base += ref.shape[0]
    plain = base - (question_len if with_question else 0)
    pair = 2
    rows = pair * question_len
    for start in range(0, group_size, pair):
        query = jnp.concatenate(
            [query_ref[:, h * width : (h + 1) * width] for h in range(start, start + pair)], axis=0
        )
        contract = (((1,), (1,)), ((), ()))
        scores = [
            lax.dot_general(query, keys[:plain, :], contract, preferred_element_type=jnp.float32)
        ]
        if with_question:
            asked = lax.dot_general(
                query, keys[plain:, :], contract, preferred_element_type=jnp.float32
            )
            asked = asked.reshape(pair, question_len, question_len)
            q_place = lax.broadcasted_iota(jnp.int32, asked.shape, 1)
            k_place = lax.broadcasted_iota(jnp.int32, asked.shape, 2)
            asked = jnp.where(k_place <= q_place, asked, -jnp.inf)
            scores.append(asked.reshape(rows, question_len))
        highest = functools.reduce(
            jnp.maximum, [jnp.max(part, axis=1, keepdims=True) for part in scores]
        )
        here = pl.ds(start * question_len, rows)
        if not first:
            stats = stats_in[here, :]
            before = stats[:, :1]
            row_total = stats[:, width // 2 : width // 2 + 1]
            highest = jnp.maximum(highest, before)
            fade = jnp.exp2((before - highest) * EXP_SCALE)
        blend = 0.0
        offset = 0
        for part in scores:
            probs = jnp.exp2((part - highest) * EXP_SCALE).astype(jnp.bfloat16)
            blend = blend + jnp.dot(
                probs,
                values[offset : offset + part.shape[1], :],
                preferred_element_type=jnp.float32,
            )
            offset += part.shape[1]
        total = blend[:, width:]
        blend = blend[:, :width]
        if not first:
            blend = blend + blend_in[here, :] * fade
            total = total + row_total * fade
        if last:
            done = (blend / total).astype(out_ref.dtype)
            for h in range(pair):
                out_ref[:, (start + h) * width : (start + h + 1) * width] = done[
                    h * question_len : (h + 1) * question_len
                ]
        else:
            lane = lax.broadcasted_iota(jnp.int32, (rows, width), 1)
            blend_out[here, :] = blend
            stats_out[here, :] = jnp.where(lane < width // 2, highest, total)


def attend(table, queries, question, pieces, fresh, state, with_question, last, deps):
    question_len, query_cols = queries.shape
    span_len, kv_cols = pieces[0].shape
    kv_heads = kv_cols // (2 * HEAD_WIDTH)
    group_cols = query_cols // kv_heads
    group_rows = group_cols // HEAD_WIDTH * question_len
    first = state is None
    pair_cols = 2 * HEAD_WIDTH

    def by_head(rows, columns):
        return pl.BlockSpec((rows, columns), lambda k: (0, k))

    state_spec = pl.BlockSpec((group_rows, HEAD_WIDTH), lambda k: (k, 0))
    operands = [table, queries, question] + list(pieces)
    specs = [smem_spec(), by_head(question_len, group_cols), by_head(question_len, pair_cols)]
    specs += [by_head(span_len, pair_cols)] * len(pieces)
    length = len(pieces) * span_len + (question_len if with_question else 0)
    if fresh is not None:
        operands.append(fresh)
        specs.append(by_head(fresh.shape[0], pair_cols))
        length += fresh.shape[0]
    if not first:
        operands += list(state)
        specs += [state_spec] * 2
    operands += list(deps)
    specs += [any_spec()] * len(deps)
    if last:
        out_shape = jax.ShapeDtypeStruct(queries.shape, queries.dtype)
        out_specs = by_head(question_len, group_cols)
    else:
        out_shape = [jax.ShapeDtypeStruct((kv_heads * group_rows, HEAD_WIDTH), jnp.float32)] * 2
        out_specs = [state_spec] * 2
    work = query_cols // HEAD_WIDTH * question_len * length
    return pl.pallas_call(
        functools.partial(
            attend_kernel, len(pieces), with_question, fresh is not None, first, last, len(deps)
        ),
        grid=(kv_heads,),
        out_shape=out_shape,
        in_specs=specs,
        out_specs=out_specs,
        scratch_shapes=[
            pltpu.VMEM((length, HEAD_WIDTH), jnp.bfloat16),
            pltpu.VMEM((length, 2 * HEAD_WIDTH), jnp.bfloat16),
        ],
        compiler_params=pltpu.CompilerParams(vmem_limit_bytes=VMEM_LIMIT),
        cost_estimate=pl.CostEstimate(
            flops=work * 8 * HEAD_WIDTH, bytes_accessed=8 * 1024 * 1024, transcendentals=work
        ),
        name="attend_spans",
    )(*operands)


def local(
    queries,
    question_kv,
    key_value_store,
    span_store_slot,
    retrieval,
    recompute_rows,
    recompute_hidden,
    kv_weight,
):
    n_store = lax.axis_size("store")
    n_tensor = lax.axis_size("tensor")
    myself = lax.axis_index("store")
    slot_count, span_len, kv_cols = key_value_store.shape
    span_count = retrieval.shape[1]
    recomp = recompute_rows.shape[2]
    model_width = recompute_hidden.shape[3]
    per_pair = max(1, span_count // n_store)
    fresh_rows = span_count * recomp
    shard_rows = fresh_rows // n_tensor
    shard_width = model_width // n_store
    place = jnp.stack([myself, lax.axis_index("tensor")]).astype(jnp.int32)
    hidden = recompute_hidden.reshape(fresh_rows, model_width)
    question = question_kv[0]
    query_rows = queries[0]

    def exchange(piece, distance):
        if distance == 0:
            return piece
        return lax.ppermute(piece, "store", [(i, i ^ distance) for i in range(n_store)])

    away = list(range(n_store - 1, 0, -1))
    everyone = away + [0]

    owners = span_store_slot[retrieval[myself]] // slot_count
    column = jnp.arange(span_count, dtype=jnp.int32)
    earlier = (owners[:, None] == owners[None, :]) & (column[None, :] < column[:, None])
    rank = jnp.sum(earlier.astype(jnp.int32), axis=1)
    source = myself ^ jnp.arange(n_store, dtype=jnp.int32)
    match = (owners[None, None, :] == source[:, None, None]) & (
        rank[None, None, :] == jnp.arange(per_pair, dtype=jnp.int32)[None, :, None]
    )
    match = match.astype(jnp.int32)
    listed = jnp.concatenate(
        [jnp.ones((span_count, 1), jnp.int32), recompute_rows[0]], axis=1
    )
    table = jnp.sum(match[:, :, :, None] * listed[None, None], axis=2)

    def rows_of(keys):
        return jnp.stack([table[distance, span] for distance, span in keys])

    hidden_out, out = pack(
        place, span_store_slot, retrieval, key_value_store, hidden, [0], everyone, [],
        (shard_rows, shard_width),
    )
    hidden_in = [exchange(piece, d) for piece, d in zip(hidden_out, everyone)]
    rounds = [[exchange(piece[0], d) for piece, d in zip(out[: len(away)], away)]]
    own = [(0, 0, out[-1][0])]
    if per_pair > 1:
        _, out = pack(
            place, span_store_slot, retrieval, key_value_store, None, list(range(1, per_pair)), [0], []
        )
        own += [(0, span, piece) for span, piece in zip(range(1, per_pair), out[0])]
        _, out = pack(place, span_store_slot, retrieval, key_value_store, None, [1], away, [])
        rounds.append([exchange(piece[0], d) for piece, d in zip(out, away)])

    state = attend(
        rows_of([(d, s) for d, s, _ in own]), query_rows, question, [p for _, _, p in own],
        None, None, True, False, [],
    )

    gathered = lax.all_gather(jnp.stack(hidden_in[::-1]), "tensor", axis=0)
    partial = jnp.dot(
        gathered.reshape(n_tensor * n_store * shard_rows, shard_width),
        kv_weight,
        preferred_element_type=jnp.float32,
    )
    partial = partial.reshape(n_tensor, n_store, shard_rows, kv_cols)
    bits = n_store.bit_length() - 1
    partial = partial.reshape((n_tensor,) + (2,) * bits + (shard_rows, kv_cols))
    for bit in range(bits):
        axis = bits - bit
        kept, sent = lax.index_in_dim(partial, 0, axis, False), lax.index_in_dim(partial, 1, axis, False)
        partial = kept + exchange(sent.astype(jnp.bfloat16), 1 << bit).astype(jnp.float32)
    fresh = partial.reshape(fresh_rows, kv_cols).astype(jnp.bfloat16)

    for span in range(per_pair):
        arrived = rounds[span]
        deps = []
        if span + 2 < per_pair:
            _, out = pack(
                place, span_store_slot, retrieval, key_value_store, None, [span + 2], away, arrived
            )
            rounds.append([exchange(piece[0], d) for piece, d in zip(out, away)])
            deps = [out[0][0]]
        batches = [list(range(i, min(i + 4, len(away)))) for i in range(0, len(away), 4)]
        for number, batch in enumerate(batches):
            last = span == per_pair - 1 and number == len(batches) - 1
            with_fresh = span == max(0, per_pair - 2) and number == len(batches) - 1
            result = attend(
                rows_of([(away[i], span) for i in batch]), query_rows, question,
                [arrived[i] for i in batch], fresh if with_fresh else None, state, False, last, deps,
            )
            state = result
    attended = state
    return (attended[None], fresh.reshape(1, span_count, recomp, kv_cols))


def solution(mesh):
    in_specs = (
        P(("groups", "store"), None, "tensor"),
        P(("groups", "store"), None, "tensor"),
        P(("groups", "store"), None, "tensor"),
        P("groups"),
        P("groups", None),
        P(("groups", "store"), None, None),
        P(("groups", "store"), None, None, None),
        P("store", "tensor"),
    )
    out_specs = (
        P(("groups", "store"), None, "tensor"),
        P(("groups", "store"), None, None, "tensor"),
    )
    return jax.shard_map(local, mesh=mesh, in_specs=in_specs, out_specs=out_specs, check_vma=False)
```

```python
import functools
import math

import jax
import jax.numpy as jnp
from jax import lax
from jax.experimental import pallas as pl
from jax.experimental.pallas import tpu as pltpu
from jax.sharding import PartitionSpec as P

HEAD_WIDTH = 128
EXP_SCALE = math.log2(math.e) * HEAD_WIDTH ** (-0.5)
VMEM_LIMIT = 60 * 1024 * 1024


def any_spec():
    return pl.BlockSpec(memory_space=pl.ANY)


def smem_spec():
    return pl.BlockSpec(memory_space=pltpu.SMEM)


def pack_kernel(spans, distances, with_hidden, n_deps, *refs):
    place_ref, slot_ref, retrieval_ref, store_ref = refs[:4]
    refs = refs[4:]
    if with_hidden:
        hidden_ref, refs = refs[0], refs[1:]
    refs = refs[n_deps:]
    n_away = len([distance for distance in distances if distance])
    n_out = len(spans) * n_away + (len(distances) if with_hidden else 0)
    outs, bounces, sems = refs[:n_out], refs[n_out : 2 * n_out], refs[2 * n_out]
    myself = place_ref[0]
    slot_count = store_ref.shape[0]
    copies = []

    def send(source, target):
        copy = pltpu.make_async_copy(source, bounces[place], sems.at[place])
        copy.start()
        copies.append((copy, target))

    place = 0
    if with_hidden:
        for distance in distances:
            target = outs[place]
            rows, width = target.shape
            first_row = pl.multiple_of(place_ref[1] * rows, rows)
            first_column = pl.multiple_of((myself ^ distance) * width, width)
            send(hidden_ref.at[pl.ds(first_row, rows), pl.ds(first_column, width)], target)
            place += 1
    for distance in distances:
        if distance == 0:
            continue
        partner = myself ^ distance
        count = jnp.int32(0)
        chosen = [jnp.int32(0) for _ in spans]
        for j in range(retrieval_ref.shape[1]):
            home = slot_ref[retrieval_ref[partner, j]]
            mine = home // slot_count == myself
            for i, span in enumerate(spans):
                chosen[i] = jnp.where(mine & (count == span), home - myself * slot_count, chosen[i])
            count = count + jnp.where(mine, 1, 0)
        for slot in chosen:
            send(store_ref.at[slot], outs[place])
            place += 1
    leaving = []
    for i, (copy, target) in enumerate(copies):
        copy.wait()
        copy = pltpu.make_async_copy(bounces[i], target, sems.at[i])
        copy.start()
        leaving.append(copy)
    for copy in leaving:
        copy.wait()


def pack(place, slots, retrieval, store, hidden, spans, distances, deps, hidden_shape=None):
    with_hidden = hidden is not None
    _, span_len, kv_cols = store.shape
    shapes = []
    if with_hidden:
        shapes += [jax.ShapeDtypeStruct(hidden_shape, hidden.dtype)] * len(distances)
    n_away = len([distance for distance in distances if distance])
    shapes += [jax.ShapeDtypeStruct((span_len, kv_cols), store.dtype)] * (len(spans) * n_away)
    operands = [place, slots, retrieval, store] + ([hidden] if with_hidden else []) + list(deps)
    outs = pl.pallas_call(
        functools.partial(pack_kernel, tuple(spans), tuple(distances), with_hidden, len(deps)),
        out_shape=shapes,
        in_specs=[smem_spec()] * 3 + [any_spec()] * (len(operands) - 3),
        out_specs=[any_spec()] * len(shapes),
        scratch_shapes=[pltpu.VMEM(shape.shape, shape.dtype) for shape in shapes]
        + [pltpu.SemaphoreType.DMA((len(shapes),))],
        compiler_params=pltpu.CompilerParams(vmem_limit_bytes=VMEM_LIMIT),
        name="pack_spans",
    )(*operands)
    hidden_pieces = outs[: len(distances)] if with_hidden else []
    rest = outs[len(hidden_pieces) :]
    per = len(spans)
    return list(hidden_pieces), [list(rest[i * per : (i + 1) * per]) for i in range(n_away)]


def attend_kernel(n_pieces, with_question, with_fresh, first, last, n_deps, *refs):
    _, table_ref, query_ref, question_ref = refs[:4]
    refs = refs[4:]
    piece_refs, refs = refs[:n_pieces], refs[n_pieces:]
    if with_fresh:
        fresh_ref, refs = refs[0], refs[1:]
    if not first:
        blend_in, stats_in = refs[:2]
        refs = refs[2:]
    refs = refs[n_deps:]
    if last:
        out_ref, refs = refs[0], refs[1:]
    else:
        blend_out, stats_out = refs[:2]
        refs = refs[2:]
    keys, values = refs
    width = HEAD_WIDTH
    question_len = query_ref.shape[0]
    group_size = query_ref.shape[1] // width
    span_len = piece_refs[0].shape[0]
    spare_key = question_ref[0:1, :width].astype(jnp.float32)
    row = lax.broadcasted_iota(jnp.int32, (span_len, width), 0)
    for i in range(n_pieces):
        stale = row < jnp.where(table_ref[i, 0] == 0, span_len, 0)
        for column in range(1, table_ref.shape[1]):
            stale = stale | (row == table_ref[i, column])
        here = pl.ds(i * span_len, span_len)
        block = piece_refs[i][...].astype(jnp.float32)
        keys[here, :] = jnp.where(stale, spare_key, block[:, :width]).astype(keys.dtype)
        values[here, :width] = jnp.where(stale, 0.0, block[:, width:]).astype(values.dtype)
        values[here, width:] = jnp.where(stale, 0.0, 1.0).astype(values.dtype)
    base = n_pieces * span_len
    for ref in ([fresh_ref] if with_fresh else []) + ([question_ref] if with_question else []):
        here = pl.ds(base, ref.shape[0])
        keys[here, :] = ref[:, :width]
        values[here, :width] = ref[:, width:]
        values[here, width:] = jnp.ones((ref.shape[0], width), values.dtype)
        base += ref.shape[0]
    plain = base - (question_len if with_question else 0)
    pair = 2
    rows = pair * question_len
    for start in range(0, group_size, pair):
        query = jnp.concatenate(
            [query_ref[:, h * width : (h + 1) * width] for h in range(start, start + pair)], axis=0
        )
        contract = (((1,), (1,)), ((), ()))
        scores = [
            lax.dot_general(query, keys[:plain, :], contract, preferred_element_type=jnp.float32)
        ]
        if with_question:
            asked = lax.dot_general(
                query, keys[plain:, :], contract, preferred_element_type=jnp.float32
            )
            asked = asked.reshape(pair, question_len, question_len)
            q_place = lax.broadcasted_iota(jnp.int32, asked.shape, 1)
            k_place = lax.broadcasted_iota(jnp.int32, asked.shape, 2)
            asked = jnp.where(k_place <= q_place, asked, -jnp.inf)
            scores.append(asked.reshape(rows, question_len))
        highest = functools.reduce(
            jnp.maximum, [jnp.max(part, axis=1, keepdims=True) for part in scores]
        )
        here = pl.ds(start * question_len, rows)
        if not first:
            stats = stats_in[here, :]
            before = stats[:, :1]
            row_total = stats[:, width // 2 : width // 2 + 1]
            highest = jnp.maximum(highest, before)
            fade = jnp.exp2((before - highest) * EXP_SCALE)
        blend = 0.0
        offset = 0
        for part in scores:
            probs = jnp.exp2((part - highest) * EXP_SCALE).astype(jnp.bfloat16)
            blend = blend + jnp.dot(
                probs,
                values[offset : offset + part.shape[1], :],
                preferred_element_type=jnp.float32,
            )
            offset += part.shape[1]
        total = blend[:, width:]
        blend = blend[:, :width]
        if not first:
            blend = blend + blend_in[here, :] * fade
            total = total + row_total * fade
        if last:
            done = (blend / total).astype(out_ref.dtype)
            for h in range(pair):
                out_ref[:, (start + h) * width : (start + h + 1) * width] = done[
                    h * question_len : (h + 1) * question_len
                ]
        else:
            lane = lax.broadcasted_iota(jnp.int32, (rows, width), 1)
            blend_out[here, :] = blend
            stats_out[here, :] = jnp.where(lane < width // 2, highest, total)


def attend(table, queries, question, pieces, slots, fresh, state, with_question, last, deps):
    question_len, query_cols = queries.shape
    span_len, kv_cols = pieces[0].shape[-2:]
    kv_heads = kv_cols // (2 * HEAD_WIDTH)
    group_cols = query_cols // kv_heads
    group_rows = group_cols // HEAD_WIDTH * question_len
    first = state is None
    pair_cols = 2 * HEAD_WIDTH

    def by_head(rows, columns):
        return pl.BlockSpec((rows, columns), lambda k, slots: (0, k))

    def by_slot(place):
        return pl.BlockSpec((None, span_len, pair_cols), lambda k, slots: (slots[place], 0, k))

    state_spec = pl.BlockSpec((group_rows, HEAD_WIDTH), lambda k, slots: (k, 0))
    operands = [table, queries, question] + list(pieces)
    specs = [smem_spec(), by_head(question_len, group_cols), by_head(question_len, pair_cols)]
    if slots is None:
        specs += [by_head(span_len, pair_cols)] * len(pieces)
        slots = jnp.zeros((1,), jnp.int32)
    else:
        specs += [by_slot(place) for place in range(len(pieces))]
    length = len(pieces) * span_len + (question_len if with_question else 0)
    if fresh is not None:
        operands.append(fresh)
        specs.append(by_head(fresh.shape[0], pair_cols))
        length += fresh.shape[0]
    if not first:
        operands += list(state)
        specs += [state_spec] * 2
    operands += list(deps)
    specs += [any_spec()] * len(deps)
    if last:
        out_shape = jax.ShapeDtypeStruct(queries.shape, queries.dtype)
        out_specs = by_head(question_len, group_cols)
    else:
        out_shape = [jax.ShapeDtypeStruct((kv_heads * group_rows, HEAD_WIDTH), jnp.float32)] * 2
        out_specs = [state_spec] * 2
    work = query_cols // HEAD_WIDTH * question_len * length
    return pl.pallas_call(
        functools.partial(
            attend_kernel, len(pieces), with_question, fresh is not None, first, last, len(deps)
        ),
        out_shape=out_shape,
        grid_spec=pltpu.PrefetchScalarGridSpec(
            num_scalar_prefetch=1,
            grid=(kv_heads,),
            in_specs=specs,
            out_specs=out_specs,
            scratch_shapes=[
                pltpu.VMEM((length, HEAD_WIDTH), jnp.bfloat16),
                pltpu.VMEM((length, 2 * HEAD_WIDTH), jnp.bfloat16),
            ],
        ),
        compiler_params=pltpu.CompilerParams(vmem_limit_bytes=VMEM_LIMIT),
        cost_estimate=pl.CostEstimate(
            flops=work * 8 * HEAD_WIDTH, bytes_accessed=8 * 1024 * 1024, transcendentals=work
        ),
        name="attend_spans",
    )(slots, *operands)


def local(
    queries,
    question_kv,
    key_value_store,
    span_store_slot,
    retrieval,
    recompute_rows,
    recompute_hidden,
    kv_weight,
):
    n_store = lax.axis_size("store")
    n_tensor = lax.axis_size("tensor")
    myself = lax.axis_index("store")
    slot_count, span_len, kv_cols = key_value_store.shape
    span_count = retrieval.shape[1]
    recomp = recompute_rows.shape[2]
    model_width = recompute_hidden.shape[3]
    per_pair = max(1, span_count // n_store)
    fresh_rows = span_count * recomp
    shard_rows = fresh_rows // n_tensor
    shard_width = model_width // n_store
    place = jnp.stack([myself, lax.axis_index("tensor")]).astype(jnp.int32)
    hidden = recompute_hidden.reshape(fresh_rows, model_width)
    question = question_kv[0]
    query_rows = queries[0]

    def exchange(piece, distance):
        if distance == 0:
            return piece
        return lax.ppermute(piece, "store", [(i, i ^ distance) for i in range(n_store)])

    away = list(range(n_store - 1, 0, -1))
    everyone = away + [0]

    home_slots = span_store_slot[retrieval[myself]]
    owners = home_slots // slot_count
    column = jnp.arange(span_count, dtype=jnp.int32)
    earlier = (owners[:, None] == owners[None, :]) & (column[None, :] < column[:, None])
    rank = jnp.sum(earlier.astype(jnp.int32), axis=1)
    source = myself ^ jnp.arange(n_store, dtype=jnp.int32)
    match = (owners[None, None, :] == source[:, None, None]) & (
        rank[None, None, :] == jnp.arange(per_pair, dtype=jnp.int32)[None, :, None]
    )
    match = match.astype(jnp.int32)
    listed = jnp.concatenate(
        [jnp.ones((span_count, 1), jnp.int32), recompute_rows[0]], axis=1
    )
    table = jnp.sum(match[:, :, :, None] * listed[None, None], axis=2)
    own_slots = jnp.sum(match[0] * (home_slots % slot_count)[None], axis=1)

    def rows_of(keys):
        return jnp.stack([table[distance, span] for distance, span in keys])

    hidden_out, out = pack(
        place, span_store_slot, retrieval, key_value_store, hidden, [0], everyone, [],
        (shard_rows, shard_width),
    )
    hidden_in = [exchange(piece, d) for piece, d in zip(hidden_out, everyone)]
    rounds = [[exchange(piece[0], d) for piece, d in zip(out, away)]]
    if per_pair > 1:
        _, out = pack(place, span_store_slot, retrieval, key_value_store, None, [1], away, [])
        rounds.append([exchange(piece[0], d) for piece, d in zip(out, away)])

    state = attend(
        rows_of([(0, span) for span in range(per_pair)]), query_rows, question,
        [key_value_store] * per_pair, own_slots, None, None, True, False, [],
    )

    gathered = lax.all_gather(jnp.stack(hidden_in[::-1]), "tensor", axis=0)
    partial = jnp.dot(
        gathered.reshape(n_tensor * n_store * shard_rows, shard_width),
        kv_weight,
        preferred_element_type=jnp.float32,
    )
    partial = partial.reshape(n_tensor, n_store, shard_rows, kv_cols)
    bits = n_store.bit_length() - 1
    partial = partial.reshape((n_tensor,) + (2,) * bits + (shard_rows, kv_cols))
    for bit in range(bits):
        axis = bits - bit
        kept, sent = lax.index_in_dim(partial, 0, axis, False), lax.index_in_dim(partial, 1, axis, False)
        partial = kept + exchange(sent.astype(jnp.bfloat16), 1 << bit).astype(jnp.float32)
    fresh = partial.reshape(fresh_rows, kv_cols).astype(jnp.bfloat16)

    for span in range(per_pair):
        arrived = rounds[span]
        deps = []
        if span + 2 < per_pair:
            _, out = pack(
                place, span_store_slot, retrieval, key_value_store, None, [span + 2], away, arrived
            )
            rounds.append([exchange(piece[0], d) for piece, d in zip(out, away)])
            deps = [out[0][0]]
        batches = [list(range(i, min(i + 4, len(away)))) for i in range(0, len(away), 4)]
        for number, batch in enumerate(batches):
            last = span == per_pair - 1 and number == len(batches) - 1
            with_fresh = span == max(0, per_pair - 2) and number == len(batches) - 1
            result = attend(
                rows_of([(away[i], span) for i in batch]), query_rows, question,
                [arrived[i] for i in batch], None, fresh if with_fresh else None, state, False, last,
                deps,
            )
            state = result
    attended = state
    return (attended[None], fresh.reshape(1, span_count, recomp, kv_cols))


def solution(mesh):
    in_specs = (
        P(("groups", "store"), None, "tensor"),
        P(("groups", "store"), None, "tensor"),
        P(("groups", "store"), None, "tensor"),
        P("groups"),
        P("groups", None),
        P(("groups", "store"), None, None),
        P(("groups", "store"), None, None, None),
        P("store", "tensor"),
    )
    out_specs = (
        P(("groups", "store"), None, "tensor"),
        P(("groups", "store"), None, None, "tensor"),
    )
    return jax.shard_map(local, mesh=mesh, in_specs=in_specs, out_specs=out_specs, check_vma=False)
```

```python
import functools
import math

import jax
import jax.numpy as jnp
from jax import lax
from jax.experimental import pallas as pl
from jax.experimental.pallas import tpu as pltpu
from jax.sharding import PartitionSpec as P

HEAD_WIDTH = 128
EXP_SCALE = math.log2(math.e) * HEAD_WIDTH ** (-0.5)
PAIR = 2
VMEM_LIMIT = 28 * 1024 * 1024
PACK_VMEM_LIMIT = 28 * 1024 * 1024


def hbm_spec():
    return pl.BlockSpec(memory_space=pltpu.HBM)


def smem_spec():
    return pl.BlockSpec(memory_space=pltpu.SMEM)


def vmem_spec():
    return pl.BlockSpec(memory_space=pltpu.VMEM)


def after(array, *others):
    return lax.optimization_barrier((array,) + others)[0]


def pack_kernel(messages, shard, with_table, *refs):
    slot_ref, retrieval_ref, store_ref, hidden_ref = refs[:4]
    refs = refs[4:]
    if with_table:
        rows_ref, refs = refs[0], refs[1:]
    outs, refs = refs[: len(messages)], refs[len(messages) :]
    if with_table:
        table_ref, refs = refs[0], refs[1:]
    sems = refs[0]
    myself = lax.axis_index("store")
    tensor = lax.axis_index("tensor")
    slot_count, _, kv_cols = store_ref.shape
    span_count = retrieval_ref.shape[1]
    shard_rows, shard_width = shard
    copies = []

    def send(source, target):
        copy = pltpu.make_async_copy(source, target, sems.at[len(copies)])
        copy.start()
        copies.append(copy)

    for target, (distance, with_hidden, pieces) in zip(outs, messages):
        if with_hidden:
            base = sum(rows for _, _, rows in pieces)
            first_row = pl.multiple_of(tensor * shard_rows, shard_rows)
            for i in range(shard_width // kv_cols):
                column = pl.multiple_of((myself ^ distance) * shard_width + i * kv_cols, kv_cols)
                send(
                    hidden_ref.at[pl.ds(first_row, shard_rows), pl.ds(column, kv_cols)],
                    target.at[pl.ds(base + i * shard_rows, shard_rows)],
                )
    for distance in sorted({message[0] for message in messages}, reverse=True):
        wanted = []
        for target, message in zip(outs, messages):
            base = 0
            for span, start, rows in message[2] if message[0] == distance else ():
                wanted.append((span, pl.ds(start, rows), target.at[pl.ds(base, rows)]))
                base += rows
        if not wanted:
            continue
        count = jnp.int32(0)
        chosen = [jnp.int32(0) for _ in wanted]
        for j in range(span_count):
            home = slot_ref[retrieval_ref[myself ^ distance, j]]
            mine = home // slot_count == myself
            for i, (span, _, _) in enumerate(wanted):
                chosen[i] = jnp.where(mine & (count == span), home - myself * slot_count, chosen[i])
            count = count + jnp.where(mine, 1, 0)
        for slot, (_, rows, target) in zip(chosen, wanted):
            send(store_ref.at[slot, rows], target)
    if with_table:
        lines, columns = table_ref.shape
        per_pair = lines >> (lax.axis_size("store").bit_length() - 1)

        def clear(line, carry):
            for column in range(columns):
                table_ref[line, column] = 0
            return carry

        def fill(j, carry):
            home = slot_ref[retrieval_ref[myself, j]]
            owner = home // slot_count
            first = (owner ^ myself) * per_pair
            taken = jnp.int32(0)
            for span in range(per_pair):
                taken = taken + table_ref[first + span, 0]
            line = first + jnp.minimum(taken, per_pair - 1)
            table_ref[line, 0] = 1
            for column in range(rows_ref.shape[1]):
                table_ref[line, 1 + column] = rows_ref[j, column]
            table_ref[line, columns - 1] = home - owner * slot_count
            return carry

        lax.fori_loop(0, lines, clear, 0)
        lax.fori_loop(0, span_count, fill, 0)
    for copy in copies:
        copy.wait()


def pack(slots, retrieval, store, hidden, rows, messages, shard, lines):
    kv_cols = store.shape[2]
    with_table = rows is not None
    blocks = shard[1] // kv_cols
    shapes, n_copies = [], 0
    for _, with_hidden, pieces in messages:
        length = sum(rows for _, _, rows in pieces) + (blocks * shard[0] if with_hidden else 0)
        shapes.append(jax.ShapeDtypeStruct((length, kv_cols), store.dtype))
        n_copies += len(pieces) + (blocks if with_hidden else 0)
    specs = [vmem_spec()] * len(shapes)
    operands = [slots, retrieval, store, hidden]
    in_specs = [smem_spec()] * 2 + [hbm_spec()] * 2
    if with_table:
        operands.append(rows)
        in_specs.append(smem_spec())
        shapes.append(jax.ShapeDtypeStruct((lines, rows.shape[1] + 2), jnp.int32))
        specs.append(smem_spec())
    outs = pl.pallas_call(
        functools.partial(pack_kernel, messages, shard, with_table),
        out_shape=shapes,
        in_specs=in_specs,
        out_specs=specs,
        scratch_shapes=[pltpu.SemaphoreType.DMA((n_copies,))],
        compiler_params=pltpu.CompilerParams(vmem_limit_bytes=PACK_VMEM_LIMIT),
        cost_estimate=pl.CostEstimate(flops=0, bytes_accessed=0, transcendentals=0),
        name="pack_spans",
    )(*operands)
    return list(outs[: len(messages)]), outs[-1] if with_table else None


def project_kernel(shard_rows, distances, *refs):
    block_refs, (weight_ref, partial_ref, sent_ref) = refs[:-3], refs[-3:]
    n_store, group_rows, kv_cols = partial_ref.shape
    pieces = weight_ref.shape[0] // kv_cols
    total = 0.0
    for piece in range(pieces):
        rows = []
        for d in range(n_store):
            for ref in block_refs:
                length = n_store * pieces * shard_rows
                for base in range(0, ref.shape[0], length):
                    start = base + (d * pieces + piece) * shard_rows
                    rows.append(ref[start : start + shard_rows, :])
        total = total + jnp.dot(
            jnp.concatenate(rows, axis=0),
            weight_ref[piece * kv_cols : (piece + 1) * kv_cols, :],
            preferred_element_type=jnp.float32,
        )
    tensor = lax.axis_index("tensor")
    for d in range(n_store):
        for i, distance in enumerate(distances):
            base = d * group_rows + i * shard_rows
            block = total[base : base + shard_rows, :]
            row = pl.multiple_of((tensor ^ distance) * shard_rows, shard_rows)
            partial_ref[d, pl.ds(row, shard_rows), :] = block
            if d % 2:
                sent_ref[d // 2, pl.ds(row, shard_rows), :] = block.astype(sent_ref.dtype)


def project(blocks, weight, n_store, shard_rows, distances):
    group_rows = sum(block.shape[0] for block in blocks) * weight.shape[1]
    group_rows = group_rows // (n_store * weight.shape[0])
    kv_cols = weight.shape[1]
    return pl.pallas_call(
        functools.partial(project_kernel, shard_rows, tuple(distances)),
        out_shape=[
            jax.ShapeDtypeStruct((n_store, group_rows, kv_cols), jnp.float32),
            jax.ShapeDtypeStruct((n_store // 2, group_rows, kv_cols), jnp.bfloat16),
        ],
        in_specs=[vmem_spec()] * (len(blocks) + 1),
        out_specs=[vmem_spec()] * 2,
        compiler_params=pltpu.CompilerParams(vmem_limit_bytes=VMEM_LIMIT),
        cost_estimate=pl.CostEstimate(flops=0, bytes_accessed=0, transcendentals=0),
        name="project_rows",
    )(*blocks, weight)


def attend_kernel(parts, with_store, with_question, with_fresh, first, last, *refs):
    table_ref, query_ref, question_ref = refs[:3]
    refs = refs[3:]
    if with_store:
        store_ref, refs = refs[0], refs[1:]
    else:
        piece_refs, refs = refs[: len(parts)], refs[len(parts) :]
    if with_fresh:
        fresh_ref, refs = refs[0], refs[1:]
    if not first:
        blend_in, stats_in = refs[:2]
        refs = refs[2:]
    if last:
        out_ref, keys, values, out_stage, sems = refs
    else:
        blend_out, stats_out, keys, values = refs
    width = HEAD_WIDTH
    question_len, query_cols = query_ref.shape
    kv_heads = question_ref.shape[1] // (2 * width)
    group_cols = query_cols // kv_heads
    group_size = group_cols // width
    rows = PAIR * question_len
    pairs = group_size // PAIR
    contract = (((1,), (1,)), ((), ()))

    def out_copy(step, column):
        columns = pl.ds(column, PAIR * width)
        return pltpu.make_async_copy(out_stage.at[:, columns], out_ref.at[:, columns], sems.at[step])

    def one_kv_head(k, carry):
        key_at = pl.ds(pl.multiple_of(k * 2 * width, 2 * width), width)
        value_at = pl.ds(pl.multiple_of(k * 2 * width + width, width), width)
        spare_key = question_ref[0:8, key_at][0:1].astype(jnp.float32)
        base = 0
        for i, (line, start, length) in enumerate(parts):
            if with_store:
                slot = table_ref[line, table_ref.shape[1] - 1]
                key, value = store_ref[slot, :, key_at], store_ref[slot, :, value_at]
            else:
                key, value = piece_refs[i][:length, key_at], piece_refs[i][:length, value_at]
            row = start + lax.broadcasted_iota(jnp.int32, (length, width), 0)
            stale = row < jnp.where(table_ref[line, 0] == 0, start + length, 0)
            for column in range(1, table_ref.shape[1] - 1):
                stale = stale | (row == table_ref[line, column])
            here = slice(base, base + length)
            keys[here, :] = jnp.where(stale, spare_key, key.astype(jnp.float32)).astype(keys.dtype)
            values[here, :width] = jnp.where(stale, 0.0, value.astype(jnp.float32)).astype(values.dtype)
            values[here, width:] = jnp.where(stale, 0.0, 1.0).astype(values.dtype)
            base += length
        for ref in ([fresh_ref] if with_fresh else []) + ([question_ref] if with_question else []):
            here = slice(base, base + ref.shape[0])
            keys[here, :] = ref[:, key_at]
            values[here, :width] = ref[:, value_at]
            values[here, width:] = jnp.ones((ref.shape[0], width), values.dtype)
            base += ref.shape[0]
        plain = base - (question_len if with_question else 0)

        def query_columns(start):
            return pl.ds(pl.multiple_of(k * group_cols + start * width, width), width)

        def score(pair):
            query = jnp.concatenate(
                [query_ref[:, query_columns(pair * PAIR + h)] for h in range(PAIR)], axis=0
            )
            parts = [
                lax.dot_general(query, keys[:plain, :], contract, preferred_element_type=jnp.float32)
            ]
            if with_question:
                asked = lax.dot_general(
                    query, keys[plain:base, :], contract, preferred_element_type=jnp.float32
                )
                asked = asked.reshape(PAIR, question_len, question_len)
                q_place = lax.broadcasted_iota(jnp.int32, asked.shape, 1)
                k_place = lax.broadcasted_iota(jnp.int32, asked.shape, 2)
                asked = jnp.where(k_place <= q_place, asked, -jnp.inf)
                parts.append(asked.reshape(rows, question_len))
            return parts

        upcoming = score(0)
        for pair in range(pairs):
            scores = upcoming
            if pair + 1 < pairs:
                upcoming = score(pair + 1)
            highest = functools.reduce(
                jnp.maximum, [jnp.max(part, axis=1, keepdims=True) for part in scores]
            )
            here = pl.ds(pl.multiple_of((k * pairs + pair) * rows, rows), rows)
            if not first:
                stats = stats_in[here, :]
                before = stats[:, :1]
                row_total = stats[:, width // 2 : width // 2 + 1]
                highest = jnp.maximum(highest, before)
                fade = jnp.exp2((before - highest) * EXP_SCALE)
            blend = 0.0
            offset = 0
            for part in scores:
                probs = jnp.exp2((part - highest) * EXP_SCALE).astype(jnp.bfloat16)
                blend = blend + jnp.dot(
                    probs,
                    values[offset : offset + part.shape[1], :],
                    preferred_element_type=jnp.float32,
                )
                offset += part.shape[1]
            total = blend[:, width:]
            blend = blend[:, :width]
            if not first:
                blend = blend + blend_in[here, :] * fade
                total = total + row_total * fade
            if last:
                done = (blend / total).astype(out_ref.dtype)
                for h in range(PAIR):
                    out_stage[:, query_columns(pair * PAIR + h)] = done[
                        h * question_len : (h + 1) * question_len
                    ]
                out_copy(
                    k * pairs + pair,
                    pl.multiple_of(k * group_cols + pair * PAIR * width, PAIR * width),
                ).start()
            else:
                lane = lax.broadcasted_iota(jnp.int32, (rows, width), 1)
                blend_out[here, :] = blend
                stats_out[here, :] = jnp.where(lane < width // 2, highest, total)
        return carry

    lax.fori_loop(0, kv_heads, one_kv_head, 0)
    if last:
        for step in range(kv_heads * pairs):
            out_copy(step, step * PAIR * width).wait()


def attend(table, queries, question, parts, pieces, store, fresh, state, with_question, last):
    question_len, query_cols = queries.shape
    heads = query_cols // HEAD_WIDTH
    pairs = heads // PAIR
    first = state is None
    operands = [table, queries, question] + ([store] if store is not None else list(pieces))
    length = sum(rows for _, _, rows in parts) + (question_len if with_question else 0)
    if fresh is not None:
        operands.append(fresh)
        length += fresh.shape[0]
    if not first:
        operands += list(state)
    scratch = [
        pltpu.VMEM((length, HEAD_WIDTH), jnp.bfloat16),
        pltpu.VMEM((length, 2 * HEAD_WIDTH), jnp.bfloat16),
    ]
    if last:
        out_shape = jax.ShapeDtypeStruct(queries.shape, queries.dtype)
        out_specs = hbm_spec()
        scratch += [pltpu.VMEM(queries.shape, queries.dtype), pltpu.SemaphoreType.DMA((pairs,))]
    else:
        out_shape = [jax.ShapeDtypeStruct((heads * question_len, HEAD_WIDTH), jnp.float32)] * 2
        out_specs = [vmem_spec()] * 2
    return pl.pallas_call(
        functools.partial(
            attend_kernel, tuple(parts), store is not None, with_question, fresh is not None, first,
            last,
        ),
        out_shape=out_shape,
        in_specs=[smem_spec()] + [vmem_spec()] * (len(operands) - 1),
        out_specs=out_specs,
        scratch_shapes=scratch,
        compiler_params=pltpu.CompilerParams(vmem_limit_bytes=VMEM_LIMIT),
        cost_estimate=pl.CostEstimate(
            flops=heads * question_len * length * 8 * HEAD_WIDTH, bytes_accessed=0, transcendentals=0
        ),
        name="attend_spans",
    )(*operands)


def local(
    queries,
    question_kv,
    key_value_store,
    span_store_slot,
    retrieval,
    recompute_rows,
    recompute_hidden,
    kv_weight,
):
    n_store = lax.axis_size("store")
    n_tensor = lax.axis_size("tensor")
    slot_count, span_len, kv_cols = key_value_store.shape
    span_count = retrieval.shape[1]
    recomp = recompute_rows.shape[2]
    model_width = recompute_hidden.shape[3]
    shard_rows = span_count * recomp // n_tensor
    per_pair = max(1, span_count // n_store)
    fresh_rows = span_count * recomp
    hidden = recompute_hidden.reshape(fresh_rows, model_width)
    question = question_kv[0]
    query_rows = queries[0]

    def exchange(piece, distance, axis, content):
        size = lax.axis_size(axis)
        with jax.named_scope(content + str(distance)):
            return lax.ppermute(piece, axis, [(i, i ^ distance) for i in range(size)])

    shard = (shard_rows, model_width // n_store)

    def packed(messages, rows=None):
        return pack(
            span_store_slot, retrieval, key_value_store, hidden, rows, messages, shard,
            n_store * per_pair,
        )

    away = list(range(n_store - 1, 0, -1))
    stages = [[(span, 0, span_len)] for span in range(per_pair)]
    if per_pair > 1:
        half = span_len // 2
        stages[-1:] = [[(per_pair - 1, start, half)] for start in (0, half)]
    messages = [[(d, i == 0, pieces) for d in away] for i, pieces in enumerate(stages)]
    outbox, _ = packed(messages[0])
    arrived = [[exchange(piece, d, "store", "stage0_") for piece, d in zip(outbox, away)]]
    later = [message for stage in messages[1:] for message in stage]
    (hidden_own, *outbox), table = packed([(0, True, [])] + later, recompute_rows[0])

    def block(parts, pieces, state, fresh=None, last=False):
        return attend(
            table, query_rows, question, parts, pieces, None if pieces else key_value_store, fresh,
            state, not pieces, last,
        )

    def parts_of(number):
        return [(d * per_pair + span, start, rows) for d, _, p in messages[number] for span, start, rows in p]

    def behind(pieces, state):
        return list(lax.optimization_barrier((*pieces, state[1]))[:-1])

    state = block([(span, 0, span_len) for span in range(per_pair)], [], None)
    states = [state]
    arrived[0] = behind(arrived[0], state)
    for number in range(1, len(stages)):
        here, outbox = outbox[: len(away)], outbox[len(away) :]
        before = arrived[-1]
        coming = [
            exchange(after(piece, earlier), d, "store", "stage%d_" % number)
            for piece, earlier, d in zip(here, before, away)
        ]
        states.append(block(parts_of(number - 1), before, states[-1]))
        arrived.append(behind(coming, states[-1]))

    def paced(array, step):
        return after(array, *arrived[min(step, len(arrived) - 1)])

    first_row = arrived[0][0].shape[0] - hidden_own.shape[0]
    blocks = [hidden_own] + [piece[first_row:] for piece in arrived[0][::-1]]
    distances = [0]
    for step, bit in enumerate(reversed(range(n_tensor.bit_length() - 1))):
        distances += [distance ^ (1 << bit) for distance in distances]
        blocks[-1] = paced(blocks[-1], step)
        gathered = jnp.concatenate(blocks, axis=0)
        blocks = [gathered, exchange(gathered, 1 << bit, "tensor", "hidden")]
    step = n_tensor.bit_length() - 1
    blocks[-1] = paced(blocks[-1], step)
    partial, sent = project(blocks, kv_weight, n_store, shard_rows, distances)
    for bit in range(n_store.bit_length() - 1):
        if bit:
            sent = paced(partial[1::2].astype(jnp.bfloat16), step + bit)
        partial = partial[0::2] + exchange(sent, 1 << bit, "store", "partial").astype(jnp.float32)
    fresh = partial[0].astype(jnp.bfloat16)
    fresh_out = fresh.reshape(1, span_count, recomp, kv_cols)

    state, parts, size = states[-1], parts_of(len(stages) - 1), 6
    for i in range(0, len(away), size):
        last = i + size >= len(away)
        state = block(
            parts[i : i + size], arrived[-1][i : i + size], state, fresh if last else None, last
        )
    return (state[None], fresh_out)


def solution(mesh):
    in_specs = (
        P(("groups", "store"), None, "tensor"),
        P(("groups", "store"), None, "tensor"),
        P(("groups", "store"), None, "tensor"),
        P("groups"),
        P("groups", None),
        P(("groups", "store"), None, None),
        P(("groups", "store"), None, None, None),
        P("store", "tensor"),
    )
    out_specs = (
        P(("groups", "store"), None, "tensor"),
        P(("groups", "store"), None, None, "tensor"),
    )
    return jax.shard_map(local, mesh=mesh, in_specs=in_specs, out_specs=out_specs, check_vma=False)
```

```python
import functools
import math

import jax
import jax.numpy as jnp
from jax import lax
from jax.experimental import pallas as pl
from jax.experimental.pallas import tpu as pltpu
from jax.sharding import PartitionSpec as P

HEAD_WIDTH = 128
EXP_SCALE = math.log2(math.e) * HEAD_WIDTH ** (-0.5)
PAIR = 2
VMEM_LIMIT = 28 * 1024 * 1024
FIRST_VMEM_LIMIT = 60 * 1024 * 1024


def hbm_spec():
    return pl.BlockSpec(memory_space=pltpu.HBM)


def smem_spec():
    return pl.BlockSpec(memory_space=pltpu.SMEM)


def vmem_spec():
    return pl.BlockSpec(memory_space=pltpu.VMEM)


def after(array, *others):
    return lax.optimization_barrier((array,) + others)[0]


def pack_kernel(messages, shard, with_table, *refs):
    slot_ref, retrieval_ref, store_ref, hidden_ref = refs[:4]
    refs = refs[4:]
    if with_table:
        rows_ref, refs = refs[0], refs[1:]
    outs, refs = refs[: len(messages)], refs[len(messages) :]
    if with_table:
        table_ref, refs = refs[0], refs[1:]
    sems = refs[0]
    myself = lax.axis_index("store")
    tensor = lax.axis_index("tensor")
    slot_count, _, kv_cols = store_ref.shape
    span_count = retrieval_ref.shape[1]
    shard_rows, shard_width = shard
    copies = []

    def send(source, target):
        copy = pltpu.make_async_copy(source, target, sems.at[len(copies)])
        copy.start()
        copies.append(copy)

    for target, (distance, with_hidden, pieces) in zip(outs, messages):
        if with_hidden:
            base = sum(rows for _, _, rows in pieces)
            first_row = pl.multiple_of(tensor * shard_rows, shard_rows)
            for i in range(shard_width // kv_cols):
                column = pl.multiple_of((myself ^ distance) * shard_width + i * kv_cols, kv_cols)
                send(
                    hidden_ref.at[pl.ds(first_row, shard_rows), pl.ds(column, kv_cols)],
                    target.at[pl.ds(base + i * shard_rows, shard_rows)],
                )
    for distance in sorted({message[0] for message in messages}, reverse=True):
        wanted = []
        for target, message in zip(outs, messages):
            base = 0
            for span, start, rows in message[2] if message[0] == distance else ():
                wanted.append((span, pl.ds(start, rows), target.at[pl.ds(base, rows)]))
                base += rows
        if not wanted:
            continue
        count = jnp.int32(0)
        chosen = [jnp.int32(0) for _ in wanted]
        for j in range(span_count):
            home = slot_ref[retrieval_ref[myself ^ distance, j]]
            mine = home // slot_count == myself
            for i, (span, _, _) in enumerate(wanted):
                chosen[i] = jnp.where(mine & (count == span), home - myself * slot_count, chosen[i])
            count = count + jnp.where(mine, 1, 0)
        for slot, (_, rows, target) in zip(chosen, wanted):
            send(store_ref.at[slot, rows], target)
    if with_table:
        lines, columns = table_ref.shape
        per_pair = lines >> (lax.axis_size("store").bit_length() - 1)

        def clear(line, carry):
            for column in range(columns):
                table_ref[line, column] = 0
            return carry

        def fill(j, carry):
            home = slot_ref[retrieval_ref[myself, j]]
            owner = home // slot_count
            first = (owner ^ myself) * per_pair
            taken = jnp.int32(0)
            for span in range(per_pair):
                taken = taken + table_ref[first + span, 0]
            line = first + jnp.minimum(taken, per_pair - 1)
            table_ref[line, 0] = 1
            for column in range(rows_ref.shape[1]):
                table_ref[line, 1 + column] = rows_ref[j, column]
            table_ref[line, columns - 1] = home - owner * slot_count
            return carry

        lax.fori_loop(0, lines, clear, 0)
        lax.fori_loop(0, span_count, fill, 0)
    for copy in copies:
        copy.wait()


def pack(slots, retrieval, store, hidden, rows, messages, shard, lines):
    kv_cols = store.shape[2]
    with_table = rows is not None
    blocks = shard[1] // kv_cols
    shapes, n_copies = [], 0
    for _, with_hidden, pieces in messages:
        length = sum(rows for _, _, rows in pieces) + (blocks * shard[0] if with_hidden else 0)
        shapes.append(jax.ShapeDtypeStruct((length, kv_cols), store.dtype))
        n_copies += len(pieces) + (blocks if with_hidden else 0)
    specs = [vmem_spec()] * len(shapes)
    operands = [slots, retrieval, store, hidden]
    in_specs = [smem_spec()] * 2 + [hbm_spec()] * 2
    if with_table:
        operands.append(rows)
        in_specs.append(smem_spec())
        shapes.append(jax.ShapeDtypeStruct((lines, rows.shape[1] + 2), jnp.int32))
        specs.append(smem_spec())
    outs = pl.pallas_call(
        functools.partial(pack_kernel, messages, shard, with_table),
        out_shape=shapes,
        in_specs=in_specs,
        out_specs=specs,
        scratch_shapes=[pltpu.SemaphoreType.DMA((n_copies,))],
        compiler_params=pltpu.CompilerParams(vmem_limit_bytes=VMEM_LIMIT if with_table else FIRST_VMEM_LIMIT),
        cost_estimate=pl.CostEstimate(flops=0, bytes_accessed=0, transcendentals=0),
        name="pack_spans",
    )(*operands)
    return list(outs[: len(messages)]), outs[-1] if with_table else None


def project_kernel(shard_rows, distances, *refs):
    block_refs, (weight_ref, partial_ref, sent_ref) = refs[:-3], refs[-3:]
    n_store, group_rows, kv_cols = partial_ref.shape
    pieces = weight_ref.shape[0] // kv_cols
    total = 0.0
    for piece in range(pieces):
        rows = []
        for d in range(n_store):
            for ref in block_refs:
                length = n_store * pieces * shard_rows
                for base in range(0, ref.shape[0], length):
                    start = base + (d * pieces + piece) * shard_rows
                    rows.append(ref[start : start + shard_rows, :])
        total = total + jnp.dot(
            jnp.concatenate(rows, axis=0),
            weight_ref[piece * kv_cols : (piece + 1) * kv_cols, :],
            preferred_element_type=jnp.float32,
        )
    tensor = lax.axis_index("tensor")
    for d in range(n_store):
        for i, distance in enumerate(distances):
            base = d * group_rows + i * shard_rows
            block = total[base : base + shard_rows, :]
            row = pl.multiple_of((tensor ^ distance) * shard_rows, shard_rows)
            partial_ref[d, pl.ds(row, shard_rows), :] = block
            if d % 2:
                sent_ref[d // 2, pl.ds(row, shard_rows), :] = block.astype(sent_ref.dtype)


def project(blocks, weight, n_store, shard_rows, distances):
    group_rows = sum(block.shape[0] for block in blocks) * weight.shape[1]
    group_rows = group_rows // (n_store * weight.shape[0])
    kv_cols = weight.shape[1]
    return pl.pallas_call(
        functools.partial(project_kernel, shard_rows, tuple(distances)),
        out_shape=[
            jax.ShapeDtypeStruct((n_store, group_rows, kv_cols), jnp.float32),
            jax.ShapeDtypeStruct((n_store // 2, group_rows, kv_cols), jnp.bfloat16),
        ],
        in_specs=[vmem_spec()] * (len(blocks) + 1),
        out_specs=[vmem_spec()] * 2,
        compiler_params=pltpu.CompilerParams(vmem_limit_bytes=VMEM_LIMIT),
        cost_estimate=pl.CostEstimate(flops=0, bytes_accessed=0, transcendentals=0),
        name="project_rows",
    )(*blocks, weight)


def attend_kernel(parts, n_pieces, with_store, with_question, with_fresh, first, last, *refs):
    table_ref, query_ref, question_ref = refs[:3]
    refs = refs[3:]
    if with_store:
        store_ref, refs = refs[0], refs[1:]
    piece_refs, refs = refs[:n_pieces], refs[n_pieces:]
    if with_fresh:
        fresh_ref, refs = refs[0], refs[1:]
    if not first:
        blend_in, total_in, highest_in = refs[:3]
        refs = refs[3:]
    if last:
        out_ref, keys, values, live, out_stage, sems = refs
    else:
        blend_out, total_out, highest_out, keys, values, live = refs
    width = HEAD_WIDTH
    question_len, query_cols = query_ref.shape
    kv_heads = question_ref.shape[1] // (2 * width)
    group_cols = query_cols // kv_heads
    group_size = group_cols // width
    rows = PAIR * question_len
    pairs = group_size // PAIR
    contract = (((1,), (1,)), ((), ()))

    def out_copy(step, column):
        columns = pl.ds(column, PAIR * width)
        return pltpu.make_async_copy(out_stage.at[:, columns], out_ref.at[:, columns], sems.at[step])

    base = 0
    for line, start, length, _, _ in parts:
        row = start + lax.broadcasted_iota(jnp.int32, (length, width), 0)
        stale = row < jnp.where(table_ref[line, 0] == 0, start + length, 0)
        for column in range(1, table_ref.shape[1] - 1):
            stale = stale | (row == table_ref[line, column])
        live[base : base + length, :] = jnp.where(stale, 0.0, 1.0).astype(live.dtype)
        base += length
    values[:base, width:] = live[:base, :]
    if values.shape[0] > base:
        values[base:, width:] = jnp.ones((values.shape[0] - base, width), values.dtype)

    def one_kv_head(k, carry):
        key_at = pl.ds(pl.multiple_of(k * 2 * width, 2 * width), width)
        value_at = pl.ds(pl.multiple_of(k * 2 * width + width, width), width)
        spare_key = question_ref[0:8, key_at][0:1].astype(jnp.float32)
        base = 0
        for line, start, length, source, offset in parts:
            here = slice(base, base + length)
            if with_store:
                slot = table_ref[line, table_ref.shape[1] - 1]
                key, value = store_ref[slot, :, key_at], store_ref[slot, :, value_at]
            else:
                at = slice(offset, offset + length)
                key, value = piece_refs[source][at, key_at], piece_refs[source][at, value_at]
            read = live[here, :].astype(jnp.float32) > 0.5
            keys[here, :] = jnp.where(read, key.astype(jnp.float32), spare_key).astype(keys.dtype)
            values[here, :width] = jnp.where(read, value.astype(jnp.float32), 0.0).astype(values.dtype)
            base += length
        for ref in ([fresh_ref] if with_fresh else []) + ([question_ref] if with_question else []):
            here = slice(base, base + ref.shape[0])
            keys[here, :] = ref[:, key_at]
            values[here, :width] = ref[:, value_at]
            base += ref.shape[0]
        plain = base - (question_len if with_question else 0)

        def query_columns(start):
            return pl.ds(pl.multiple_of(k * group_cols + start * width, width), width)

        def score(pair):
            query = jnp.concatenate(
                [query_ref[:, query_columns(pair * PAIR + h)] for h in range(PAIR)], axis=0
            )
            parts = [
                lax.dot_general(query, keys[:plain, :], contract, preferred_element_type=jnp.float32)
            ]
            if with_question:
                asked = lax.dot_general(
                    query, keys[plain:base, :], contract, preferred_element_type=jnp.float32
                )
                asked = asked.reshape(PAIR, question_len, question_len)
                q_place = lax.broadcasted_iota(jnp.int32, asked.shape, 1)
                k_place = lax.broadcasted_iota(jnp.int32, asked.shape, 2)
                asked = jnp.where(k_place <= q_place, asked, -jnp.inf)
                parts.append(asked.reshape(rows, question_len))
            return parts

        upcoming = score(0)
        for pair in range(pairs):
            scores = upcoming
            if pair + 1 < pairs:
                upcoming = score(pair + 1)
            highest = functools.reduce(
                jnp.maximum, [jnp.max(part, axis=1, keepdims=True) for part in scores]
            )
            highest = jnp.broadcast_to(highest, (rows, width))
            here = pl.ds(pl.multiple_of((k * pairs + pair) * rows, rows), rows)
            if not first:
                before = highest_in[here, :]
                highest = jnp.maximum(highest, before)
                fade = jnp.exp2((before - highest) * EXP_SCALE)
            blend = 0.0
            offset = 0
            for part in scores:
                length = part.shape[1]
                shift = jnp.concatenate([highest] * (length // width), axis=1)
                probs = jnp.exp2((part - shift) * EXP_SCALE).astype(jnp.bfloat16)
                blend = blend + jnp.dot(
                    probs, values[offset : offset + length, :], preferred_element_type=jnp.float32
                )
                offset += length
            total = blend[:, width:]
            blend = blend[:, :width]
            if not first:
                blend = blend + blend_in[here, :] * fade
                total = total + total_in[here, :] * fade
            if last:
                done = (blend / total).astype(out_ref.dtype)
                for h in range(PAIR):
                    out_stage[:, query_columns(pair * PAIR + h)] = done[
                        h * question_len : (h + 1) * question_len
                    ]
                out_copy(
                    k * pairs + pair,
                    pl.multiple_of(k * group_cols + pair * PAIR * width, PAIR * width),
                ).start()
            else:
                blend_out[here, :] = blend
                total_out[here, :] = total
                highest_out[here, :] = highest
        return carry

    lax.fori_loop(0, kv_heads, one_kv_head, 0)
    if last:
        for step in range(kv_heads * pairs):
            out_copy(step, step * PAIR * width).wait()


def attend(table, queries, question, parts, pieces, store, fresh, state, with_question, last):
    question_len, query_cols = queries.shape
    heads = query_cols // HEAD_WIDTH
    pairs = heads // PAIR
    first = state is None
    operands = [table, queries, question] + ([store] if store is not None else []) + list(pieces)
    held = sum(part[2] for part in parts)
    length = held + (question_len if with_question else 0)
    if fresh is not None:
        operands.append(fresh)
        length += fresh.shape[0]
    if not first:
        operands += list(state)
    scratch = [
        pltpu.VMEM((length, HEAD_WIDTH), jnp.bfloat16),
        pltpu.VMEM((length, 2 * HEAD_WIDTH), jnp.bfloat16),
        pltpu.VMEM((held, HEAD_WIDTH), jnp.bfloat16),
    ]
    if last:
        out_shape = jax.ShapeDtypeStruct(queries.shape, queries.dtype)
        out_specs = hbm_spec()
        scratch += [pltpu.VMEM(queries.shape, queries.dtype), pltpu.SemaphoreType.DMA((pairs,))]
    else:
        out_shape = [jax.ShapeDtypeStruct((heads * question_len, HEAD_WIDTH), jnp.float32)] * 3
        out_specs = [vmem_spec()] * 3
    return pl.pallas_call(
        functools.partial(
            attend_kernel, tuple(parts), len(pieces), store is not None, with_question,
            fresh is not None, first, last,
        ),
        out_shape=out_shape,
        in_specs=[smem_spec()] + [vmem_spec()] * (len(operands) - 1),
        out_specs=out_specs,
        scratch_shapes=scratch,
        compiler_params=pltpu.CompilerParams(vmem_limit_bytes=VMEM_LIMIT),
        cost_estimate=pl.CostEstimate(
            flops=heads * question_len * length * 8 * HEAD_WIDTH, bytes_accessed=0, transcendentals=0
        ),
        name="attend_spans",
    )(*operands)


def local(
    queries,
    question_kv,
    key_value_store,
    span_store_slot,
    retrieval,
    recompute_rows,
    recompute_hidden,
    kv_weight,
):
    n_store = lax.axis_size("store")
    n_tensor = lax.axis_size("tensor")
    slot_count, span_len, kv_cols = key_value_store.shape
    span_count = retrieval.shape[1]
    recomp = recompute_rows.shape[2]
    model_width = recompute_hidden.shape[3]
    shard_rows = span_count * recomp // n_tensor
    per_pair = max(1, span_count // n_store)
    fresh_rows = span_count * recomp
    hidden = recompute_hidden.reshape(fresh_rows, model_width)
    question = question_kv[0]
    query_rows = queries[0]

    def exchange(piece, distance, axis, content):
        size = lax.axis_size(axis)
        with jax.named_scope(content + str(distance)):
            return lax.ppermute(piece, axis, [(i, i ^ distance) for i in range(size)])

    shard = (shard_rows, model_width // n_store)

    def packed(messages, rows=None):
        return pack(
            span_store_slot, retrieval, key_value_store, hidden, rows, messages, shard,
            n_store * per_pair,
        )

    away = list(range(n_store - 1, 0, -1))
    half = span_len // 2

    def cuts(distance):
        if per_pair == 1:
            return [span_len]
        if distance == 1:
            return [(per_pair - 1) * span_len, 0, span_len]
        if distance % 2:
            return [span_len] * (per_pair - 1) + [half] * 2
        return [span_len + half] + [span_len] * (per_pair - 3) + [half] * 3

    def pieces_of(first, length):
        pieces = []
        while length:
            span, start = divmod(first, span_len)
            rows = min(span_len - start, length)
            pieces.append((span, start, rows))
            first, length = first + rows, length - rows
        return pieces

    messages = {}
    for d in away:
        first = 0
        for number, length in enumerate(cuts(d)):
            if length:
                messages[d, number] = (d, not number, pieces_of(first, length))
            first += length
    outbox, _ = packed([messages[d, 0] for d in away])
    coming = [exchange(piece, d, "store", "spans0_") for piece, d in zip(outbox, away)]
    count = 1 + max(number for _, number in messages)
    later = [(d, number) for number in range(1, count) for d in away if (d, number) in messages]
    (hidden_own, *outbox), table = packed(
        [(0, True, [])] + [messages[key] for key in later], recompute_rows[0]
    )
    outbox = dict(zip(later, outbox))

    def behind(pieces, state):
        return [after(piece, state[2]) for piece in pieces]

    def block(keys, state, fresh=None, last=False):
        parts = []
        for source, (d, number) in enumerate(keys):
            offset = 0
            for span, start, rows in messages[d, number][2]:
                parts.append((d * per_pair + span, start, rows, source, offset))
                offset += rows
        if not keys:
            parts = [(span, 0, span_len, 0, 0) for span in range(per_pair)]
        return attend(
            table, query_rows, question, parts, [arrived[key] for key in keys],
            None if keys else key_value_store, fresh, state, not keys, last,
        )

    arrived = {}
    state = block([], None)
    arrived.update(zip([(d, 0) for d in away], behind(coming, state)))
    for number in range(1, count):
        keys = [key for key in later if key[1] == number]
        coming = [
            exchange(
                after(outbox[key], arrived[key[0] if key[0] > 1 else away[0], number - 1]),
                key[0], "store", "spans%d_" % number,
            )
            for key in keys
        ]
        state = block([(d, number - 1) for d in away if (d, number - 1) in arrived], state)
        arrived.update(zip(keys, behind(coming, state)))

    blocks = [hidden_own]
    for d in away[::-1]:
        piece = arrived[d, 0]
        blocks.append(piece[piece.shape[0] - hidden_own.shape[0] :])
    distances = [0]
    for step, bit in enumerate(reversed(range(n_tensor.bit_length() - 1))):
        distances += [distance ^ (1 << bit) for distance in distances]
        if step and per_pair > 1:
            blocks[-1] = after(blocks[-1], *[arrived[d, 1] for d in away if d > 1])
        gathered = jnp.concatenate(blocks, axis=0)
        blocks = [gathered, exchange(gathered, 1 << bit, "tensor", "hidden")]
    partial, sent = project(blocks, kv_weight, n_store, shard_rows, distances)
    for bit in range(n_store.bit_length() - 1):
        if bit:
            sent = partial[1::2].astype(jnp.bfloat16)
        partial = partial[0::2] + exchange(sent, 1 << bit, "store", "partial").astype(jnp.float32)
    fresh = partial[0].astype(jnp.bfloat16)
    fresh_out = fresh.reshape(1, span_count, recomp, kv_cols)

    keys = [(d, count - 1) for d in away if (d, count - 1) in arrived]
    size = 1 if per_pair > 1 else 6
    batches = [keys[i : i + size] for i in range(0, len(keys), size)]
    for i, keys in enumerate(batches):
        joins, last = i == max(0, len(batches) - 2), i == len(batches) - 1
        if i:
            arrived.update(zip(keys, behind([arrived[key] for key in keys], state)))
        state = block(keys, state, fresh if joins else None, last)
    return (state[None], fresh_out)


def solution(mesh):
    in_specs = (
        P(("groups", "store"), None, "tensor"),
        P(("groups", "store"), None, "tensor"),
        P(("groups", "store"), None, "tensor"),
        P("groups"),
        P("groups", None),
        P(("groups", "store"), None, None),
        P(("groups", "store"), None, None, None),
        P("store", "tensor"),
    )
    out_specs = (
        P(("groups", "store"), None, "tensor"),
        P(("groups", "store"), None, None, "tensor"),
    )
    return jax.shard_map(local, mesh=mesh, in_specs=in_specs, out_specs=out_specs, check_vma=False)
```

```python
import functools
import math

import jax
import jax.numpy as jnp
from jax import lax
from jax.experimental import pallas as pl
from jax.experimental.pallas import tpu as pltpu
from jax.sharding import PartitionSpec as P

HEAD_WIDTH = 128
EXP_SCALE = math.log2(math.e) * HEAD_WIDTH ** (-0.5)
PAIR = 2
VMEM_LIMIT = 28 * 1024 * 1024
FIRST_VMEM_LIMIT = 60 * 1024 * 1024


def hbm_spec():
    return pl.BlockSpec(memory_space=pltpu.HBM)


def smem_spec():
    return pl.BlockSpec(memory_space=pltpu.SMEM)


def vmem_spec():
    return pl.BlockSpec(memory_space=pltpu.VMEM)


def after(array, *others):
    return lax.optimization_barrier((array,) + others)[0]


def pack_kernel(messages, shard, with_table, *refs):
    slot_ref, retrieval_ref, store_ref, hidden_ref = refs[:4]
    refs = refs[4:]
    if with_table:
        rows_ref, refs = refs[0], refs[1:]
    outs, refs = refs[: len(messages)], refs[len(messages) :]
    if with_table:
        table_ref, refs = refs[0], refs[1:]
    sems = refs[0]
    myself = lax.axis_index("store")
    tensor = lax.axis_index("tensor")
    slot_count, _, kv_cols = store_ref.shape
    span_count = retrieval_ref.shape[1]
    shard_rows, shard_width = shard
    copies = []

    def send(source, target):
        copy = pltpu.make_async_copy(source, target, sems.at[len(copies)])
        copy.start()
        copies.append(copy)

    for target, (distance, with_hidden, pieces) in zip(outs, messages):
        if with_hidden:
            base = sum(rows for _, _, rows in pieces)
            first_row = pl.multiple_of(tensor * shard_rows, shard_rows)
            for i in range(shard_width // kv_cols):
                column = pl.multiple_of((myself ^ distance) * shard_width + i * kv_cols, kv_cols)
                send(
                    hidden_ref.at[pl.ds(first_row, shard_rows), pl.ds(column, kv_cols)],
                    target.at[pl.ds(base + i * shard_rows, shard_rows)],
                )
    for distance in sorted({message[0] for message in messages}, reverse=True):
        wanted = []
        for target, message in zip(outs, messages):
            base = 0
            for span, start, rows in message[2] if message[0] == distance else ():
                wanted.append((span, pl.ds(start, rows), target.at[pl.ds(base, rows)]))
                base += rows
        if not wanted:
            continue
        count = jnp.int32(0)
        chosen = [jnp.int32(0) for _ in wanted]
        for j in range(span_count):
            home = slot_ref[retrieval_ref[myself ^ distance, j]]
            mine = home // slot_count == myself
            for i, (span, _, _) in enumerate(wanted):
                chosen[i] = jnp.where(mine & (count == span), home - myself * slot_count, chosen[i])
            count = count + jnp.where(mine, 1, 0)
        for slot, (_, rows, target) in zip(chosen, wanted):
            send(store_ref.at[slot, rows], target)
    if with_table:
        lines, columns = table_ref.shape
        per_pair = lines >> (lax.axis_size("store").bit_length() - 1)

        def clear(line, carry):
            for column in range(columns):
                table_ref[line, column] = 0
            return carry

        def fill(j, carry):
            home = slot_ref[retrieval_ref[myself, j]]
            owner = home // slot_count
            first = (owner ^ myself) * per_pair
            taken = jnp.int32(0)
            for span in range(per_pair):
                taken = taken + table_ref[first + span, 0]
            line = first + jnp.minimum(taken, per_pair - 1)
            table_ref[line, 0] = 1
            for column in range(rows_ref.shape[1]):
                table_ref[line, 1 + column] = rows_ref[j, column]
            table_ref[line, columns - 1] = home - owner * slot_count
            return carry

        lax.fori_loop(0, lines, clear, 0)
        lax.fori_loop(0, span_count, fill, 0)
    for copy in copies:
        copy.wait()


def pack(slots, retrieval, store, hidden, rows, messages, shard, lines):
    kv_cols = store.shape[2]
    with_table = rows is not None
    blocks = shard[1] // kv_cols
    shapes, n_copies = [], 0
    for _, with_hidden, pieces in messages:
        length = sum(rows for _, _, rows in pieces) + (blocks * shard[0] if with_hidden else 0)
        shapes.append(jax.ShapeDtypeStruct((length, kv_cols), store.dtype))
        n_copies += len(pieces) + (blocks if with_hidden else 0)
    specs = [vmem_spec()] * len(shapes)
    operands = [slots, retrieval, store, hidden]
    in_specs = [smem_spec()] * 2 + [hbm_spec()] * 2
    if with_table:
        operands.append(rows)
        in_specs.append(smem_spec())
        shapes.append(jax.ShapeDtypeStruct((lines, rows.shape[1] + 2), jnp.int32))
        specs.append(smem_spec())
    outs = pl.pallas_call(
        functools.partial(pack_kernel, messages, shard, with_table),
        out_shape=shapes,
        in_specs=in_specs,
        out_specs=specs,
        scratch_shapes=[pltpu.SemaphoreType.DMA((n_copies,))],
        compiler_params=pltpu.CompilerParams(vmem_limit_bytes=VMEM_LIMIT if with_table else FIRST_VMEM_LIMIT),
        cost_estimate=pl.CostEstimate(flops=0, bytes_accessed=0, transcendentals=0),
        name="pack_spans",
    )(*operands)
    return list(outs[: len(messages)]), outs[-1] if with_table else None


def project_kernel(shard_rows, distances, *refs):
    block_refs, (weight_ref, partial_ref, sent_ref) = refs[:-3], refs[-3:]
    n_store, group_rows, kv_cols = partial_ref.shape
    pieces = weight_ref.shape[0] // kv_cols
    total = 0.0
    for piece in range(pieces):
        rows = []
        for d in range(n_store):
            for ref in block_refs:
                length = n_store * pieces * shard_rows
                for base in range(0, ref.shape[0], length):
                    start = base + (d * pieces + piece) * shard_rows
                    rows.append(ref[start : start + shard_rows, :])
        total = total + jnp.dot(
            jnp.concatenate(rows, axis=0),
            weight_ref[piece * kv_cols : (piece + 1) * kv_cols, :],
            preferred_element_type=jnp.float32,
        )
    tensor = lax.axis_index("tensor")
    for d in range(n_store):
        for i, distance in enumerate(distances):
            base = d * group_rows + i * shard_rows
            block = total[base : base + shard_rows, :]
            row = pl.multiple_of((tensor ^ distance) * shard_rows, shard_rows)
            partial_ref[d, pl.ds(row, shard_rows), :] = block
            if d % 2:
                sent_ref[d // 2, pl.ds(row, shard_rows), :] = block.astype(sent_ref.dtype)


def project(blocks, weight, n_store, shard_rows, distances):
    group_rows = sum(block.shape[0] for block in blocks) * weight.shape[1]
    group_rows = group_rows // (n_store * weight.shape[0])
    kv_cols = weight.shape[1]
    return pl.pallas_call(
        functools.partial(project_kernel, shard_rows, tuple(distances)),
        out_shape=[
            jax.ShapeDtypeStruct((n_store, group_rows, kv_cols), jnp.float32),
            jax.ShapeDtypeStruct((n_store // 2, group_rows, kv_cols), jnp.bfloat16),
        ],
        in_specs=[vmem_spec()] * (len(blocks) + 1),
        out_specs=[vmem_spec()] * 2,
        compiler_params=pltpu.CompilerParams(vmem_limit_bytes=VMEM_LIMIT),
        cost_estimate=pl.CostEstimate(flops=0, bytes_accessed=0, transcendentals=0),
        name="project_rows",
    )(*blocks, weight)


def attend_kernel(parts, n_pieces, with_store, with_question, with_fresh, first, last, *refs):
    table_ref, query_ref, question_ref = refs[:3]
    refs = refs[3:]
    if with_store:
        store_ref, refs = refs[0], refs[1:]
    piece_refs, refs = refs[:n_pieces], refs[n_pieces:]
    if with_fresh:
        fresh_ref, refs = refs[0], refs[1:]
    if not first:
        blend_in, total_in, highest_in = refs[:3]
        refs = refs[3:]
    if last:
        out_ref, keys, values, live, out_stage, sems = refs
    else:
        blend_out, total_out, highest_out, keys, values, live = refs
    width = HEAD_WIDTH
    question_len, query_cols = query_ref.shape
    kv_heads = question_ref.shape[1] // (2 * width)
    group_cols = query_cols // kv_heads
    group_size = group_cols // width
    rows = PAIR * question_len
    pairs = group_size // PAIR
    contract = (((1,), (1,)), ((), ()))

    def out_copy(step, column):
        columns = pl.ds(column, PAIR * width)
        return pltpu.make_async_copy(out_stage.at[:, columns], out_ref.at[:, columns], sems.at[step])

    base = 0
    for line, start, length, _, _ in parts:
        row = start + lax.broadcasted_iota(jnp.int32, (length, width), 0)
        stale = row < jnp.where(table_ref[line, 0] == 0, start + length, 0)
        for column in range(1, table_ref.shape[1] - 1):
            stale = stale | (row == table_ref[line, column])
        live[base : base + length, :] = jnp.where(stale, 0.0, 1.0).astype(live.dtype)
        base += length
    values[:base, width:] = live[:base, :]
    if values.shape[0] > base:
        values[base:, width:] = jnp.ones((values.shape[0] - base, width), values.dtype)

    def one_kv_head(k, carry):
        key_at = pl.ds(pl.multiple_of(k * 2 * width, 2 * width), width)
        value_at = pl.ds(pl.multiple_of(k * 2 * width + width, width), width)
        spare_key = question_ref[0:8, key_at][0:1].astype(jnp.float32)
        base = 0
        for line, start, length, source, offset in parts:
            here = slice(base, base + length)
            if with_store:
                slot = table_ref[line, table_ref.shape[1] - 1]
                key, value = store_ref[slot, :, key_at], store_ref[slot, :, value_at]
            else:
                at = slice(offset, offset + length)
                key, value = piece_refs[source][at, key_at], piece_refs[source][at, value_at]
            read = live[here, :].astype(jnp.float32) > 0.5
            keys[here, :] = jnp.where(read, key.astype(jnp.float32), spare_key).astype(keys.dtype)
            values[here, :width] = jnp.where(read, value.astype(jnp.float32), 0.0).astype(values.dtype)
            base += length
        for ref in ([fresh_ref] if with_fresh else []) + ([question_ref] if with_question else []):
            here = slice(base, base + ref.shape[0])
            keys[here, :] = ref[:, key_at]
            values[here, :width] = ref[:, value_at]
            base += ref.shape[0]
        plain = base - (question_len if with_question else 0)

        def query_columns(start):
            return pl.ds(pl.multiple_of(k * group_cols + start * width, width), width)

        def score(pair):
            query = jnp.concatenate(
                [query_ref[:, query_columns(pair * PAIR + h)] for h in range(PAIR)], axis=0
            )
            parts = [
                lax.dot_general(query, keys[:plain, :], contract, preferred_element_type=jnp.float32)
            ]
            if with_question:
                asked = lax.dot_general(
                    query, keys[plain:base, :], contract, preferred_element_type=jnp.float32
                )
                asked = asked.reshape(PAIR, question_len, question_len)
                q_place = lax.broadcasted_iota(jnp.int32, asked.shape, 1)
                k_place = lax.broadcasted_iota(jnp.int32, asked.shape, 2)
                asked = jnp.where(k_place <= q_place, asked, -jnp.inf)
                parts.append(asked.reshape(rows, question_len))
            return parts

        upcoming = score(0)
        for pair in range(pairs):
            scores = upcoming
            if pair + 1 < pairs:
                upcoming = score(pair + 1)
            highest = functools.reduce(
                jnp.maximum, [jnp.max(part, axis=1, keepdims=True) for part in scores]
            )
            highest = jnp.broadcast_to(highest, (rows, width))
            here = pl.ds(pl.multiple_of((k * pairs + pair) * rows, rows), rows)
            if not first:
                before = highest_in[here, :]
                highest = jnp.maximum(highest, before)
                fade = jnp.exp2((before - highest) * EXP_SCALE)
            blend = 0.0
            offset = 0
            for part in scores:
                length = part.shape[1]
                shift = jnp.concatenate([highest] * (length // width), axis=1)
                probs = jnp.exp2((part - shift) * EXP_SCALE).astype(jnp.bfloat16)
                blend = blend + jnp.dot(
                    probs, values[offset : offset + length, :], preferred_element_type=jnp.float32
                )
                offset += length
            total = blend[:, width:]
            blend = blend[:, :width]
            if not first:
                blend = blend + blend_in[here, :] * fade
                total = total + total_in[here, :] * fade
            if last:
                done = (blend / total).astype(out_ref.dtype)
                for h in range(PAIR):
                    out_stage[:, query_columns(pair * PAIR + h)] = done[
                        h * question_len : (h + 1) * question_len
                    ]
                out_copy(
                    k * pairs + pair,
                    pl.multiple_of(k * group_cols + pair * PAIR * width, PAIR * width),
                ).start()
            else:
                blend_out[here, :] = blend
                total_out[here, :] = total
                highest_out[here, :] = highest
        return carry

    lax.fori_loop(0, kv_heads, one_kv_head, 0)
    if last:
        for step in range(kv_heads * pairs):
            out_copy(step, step * PAIR * width).wait()


def attend(table, queries, question, parts, pieces, store, fresh, state, with_question, last):
    question_len, query_cols = queries.shape
    heads = query_cols // HEAD_WIDTH
    pairs = heads // PAIR
    first = state is None
    operands = [table, queries, question] + ([store] if store is not None else []) + list(pieces)
    held = sum(part[2] for part in parts)
    length = held + (question_len if with_question else 0)
    if fresh is not None:
        operands.append(fresh)
        length += fresh.shape[0]
    if not first:
        operands += list(state)
    scratch = [
        pltpu.VMEM((length, HEAD_WIDTH), jnp.bfloat16),
        pltpu.VMEM((length, 2 * HEAD_WIDTH), jnp.bfloat16),
        pltpu.VMEM((held, HEAD_WIDTH), jnp.bfloat16),
    ]
    if last:
        out_shape = jax.ShapeDtypeStruct(queries.shape, queries.dtype)
        out_specs = hbm_spec()
        scratch += [pltpu.VMEM(queries.shape, queries.dtype), pltpu.SemaphoreType.DMA((pairs,))]
    else:
        out_shape = [jax.ShapeDtypeStruct((heads * question_len, HEAD_WIDTH), jnp.float32)] * 3
        out_specs = [vmem_spec()] * 3
    return pl.pallas_call(
        functools.partial(
            attend_kernel, tuple(parts), len(pieces), store is not None, with_question,
            fresh is not None, first, last,
        ),
        out_shape=out_shape,
        in_specs=[smem_spec()] + [vmem_spec()] * (len(operands) - 1),
        out_specs=out_specs,
        scratch_shapes=scratch,
        compiler_params=pltpu.CompilerParams(vmem_limit_bytes=VMEM_LIMIT),
        cost_estimate=pl.CostEstimate(
            flops=heads * question_len * length * 8 * HEAD_WIDTH, bytes_accessed=0, transcendentals=0
        ),
        name="attend_spans",
    )(*operands)


def local(
    queries,
    question_kv,
    key_value_store,
    span_store_slot,
    retrieval,
    recompute_rows,
    recompute_hidden,
    kv_weight,
):
    n_store = lax.axis_size("store")
    n_tensor = lax.axis_size("tensor")
    slot_count, span_len, kv_cols = key_value_store.shape
    span_count = retrieval.shape[1]
    recomp = recompute_rows.shape[2]
    model_width = recompute_hidden.shape[3]
    shard_rows = span_count * recomp // n_tensor
    per_pair = max(1, span_count // n_store)
    fresh_rows = span_count * recomp
    hidden = recompute_hidden.reshape(fresh_rows, model_width)
    question = question_kv[0]
    query_rows = queries[0]

    def exchange(piece, distance, axis, content):
        size = lax.axis_size(axis)
        with jax.named_scope(content + str(distance)):
            return lax.ppermute(piece, axis, [(i, i ^ distance) for i in range(size)])

    shard = (shard_rows, model_width // n_store)

    def packed(messages, rows=None):
        return pack(
            span_store_slot, retrieval, key_value_store, hidden, rows, messages, shard,
            n_store * per_pair,
        )

    away = list(range(n_store - 1, 0, -1))
    half = span_len // 2

    def cuts(distance):
        if per_pair == 1:
            return [span_len]
        if distance == 1:
            return [span_len + half, 0, span_len + half] + [span_len] * (per_pair - 3)
        if distance % 2:
            return [half] + [span_len] * (per_pair - 2) + [half] * 3
        return [span_len] * (per_pair - 2) + [half] * 4

    def pieces_of(first, length):
        pieces = []
        while length:
            span, start = divmod(first, span_len)
            rows = min(span_len - start, length)
            pieces.append((span, start, rows))
            first, length = first + rows, length - rows
        return pieces

    messages = {}
    for d in away:
        first = 0
        for number, length in enumerate(cuts(d)):
            if length:
                messages[d, number] = (d, not number, pieces_of(first, length))
            first += length
    outbox, _ = packed([messages[d, 0] for d in away])
    coming = [exchange(piece, d, "store", "spans0_") for piece, d in zip(outbox, away)]
    count = 1 + max(number for _, number in messages)
    later = [(d, number) for number in range(1, count) for d in away if (d, number) in messages]
    (hidden_own, *outbox), table = packed(
        [(0, True, [])] + [messages[key] for key in later], recompute_rows[0]
    )
    outbox = dict(zip(later, outbox))

    def behind(pieces, state):
        return [after(piece, state[2]) for piece in pieces]

    def block(keys, state, fresh=None, last=False):
        parts = []
        for source, (d, number) in enumerate(keys):
            offset = 0
            for span, start, rows in messages[d, number][2]:
                parts.append((d * per_pair + span, start, rows, source, offset))
                offset += rows
        if not keys:
            parts = [(span, 0, span_len, 0, 0) for span in range(per_pair)]
        return attend(
            table, query_rows, question, parts, [arrived[key] for key in keys],
            None if keys else key_value_store, fresh, state, not keys, last,
        )

    def recomputed():
        blocks = [hidden_own]
        for d in away[::-1]:
            piece = arrived[d, 0]
            blocks.append(piece[piece.shape[0] - hidden_own.shape[0] :])
        distances = [0]
        for step, bit in enumerate(reversed(range(n_tensor.bit_length() - 1))):
            distances += [distance ^ (1 << bit) for distance in distances]
            if step and per_pair > 1:
                blocks[-1] = after(blocks[-1], *[arrived[d, 1] for d in away if d > 1])
            gathered = jnp.concatenate(blocks, axis=0)
            blocks = [gathered, exchange(gathered, 1 << bit, "tensor", "hidden")]
        partial, sent = project(blocks, kv_weight, n_store, shard_rows, distances)
        for bit in range(n_store.bit_length() - 1):
            if bit:
                sent = partial[1::2].astype(jnp.bfloat16)
            partial = partial[0::2] + exchange(sent, 1 << bit, "store", "partial").astype(jnp.float32)
        fresh = partial[0].astype(jnp.bfloat16)
        return fresh

    arrived = {}
    state = block([], None)
    arrived.update(zip([(d, 0) for d in away], behind(coming, state)))
    for number in range(1, count):
        keys = [key for key in later if key[1] == number]
        coming = [
            exchange(
                after(outbox[key], arrived[key[0] if key[0] > 1 else away[0], number - 1]),
                key[0], "store", "spans%d_" % number,
            )
            for key in keys
        ]
        keys_here = [(d, number - 1) for d in away if (d, number - 1) in arrived]
        joins = number == max(1, count - 2)
        if joins:
            fresh = recomputed()
        state = block(keys_here, state, fresh if joins else None)
        arrived.update(zip(keys, behind(coming, state)))

    keys = [(d, count - 1) for d in away if (d, count - 1) in arrived]
    size = 1 if per_pair > 1 else 6
    batches = [keys[i : i + size] for i in range(0, len(keys), size)]
    if count == 1:
        fresh = recomputed()
    for i, keys in enumerate(batches):
        joins, last = count == 1 and i == 0, i == len(batches) - 1
        if i:
            arrived.update(zip(keys, behind([arrived[key] for key in keys], state)))
        state = block(keys, state, fresh if joins else None, last)
    return (state[None], fresh.reshape(1, span_count, recomp, kv_cols))


def solution(mesh):
    in_specs = (
        P(("groups", "store"), None, "tensor"),
        P(("groups", "store"), None, "tensor"),
        P(("groups", "store"), None, "tensor"),
        P("groups"),
        P("groups", None),
        P(("groups", "store"), None, None),
        P(("groups", "store"), None, None, None),
        P("store", "tensor"),
    )
    out_specs = (
        P(("groups", "store"), None, "tensor"),
        P(("groups", "store"), None, None, "tensor"),
    )
    return jax.shard_map(local, mesh=mesh, in_specs=in_specs, out_specs=out_specs, check_vma=False)
```

```python
import functools
import math

import jax
import jax.numpy as jnp
from jax import lax
from jax.experimental import pallas as pl
from jax.experimental.pallas import tpu as pltpu
from jax.sharding import PartitionSpec as P

HEAD_WIDTH = 128
EXP_SCALE = math.log2(math.e) * HEAD_WIDTH ** (-0.5)
EXP_LIMIT = 64.0
PAIR = 2
VMEM_LIMIT = 28 * 1024 * 1024
FIRST_VMEM_LIMIT = 60 * 1024 * 1024


def hbm_spec():
    return pl.BlockSpec(memory_space=pltpu.HBM)


def smem_spec():
    return pl.BlockSpec(memory_space=pltpu.SMEM)


def vmem_spec():
    return pl.BlockSpec(memory_space=pltpu.VMEM)


def after(array, *others):
    return lax.optimization_barrier((array,) + others)[0]


def pack_kernel(messages, shard, with_table, *refs):
    slot_ref, retrieval_ref, store_ref, hidden_ref = refs[:4]
    refs = refs[4:]
    if with_table:
        rows_ref, refs = refs[0], refs[1:]
    outs, refs = refs[: len(messages)], refs[len(messages) :]
    if with_table:
        table_ref, refs = refs[0], refs[1:]
    sems = refs[0]
    myself = lax.axis_index("store")
    tensor = lax.axis_index("tensor")
    slot_count, _, kv_cols = store_ref.shape
    span_count = retrieval_ref.shape[1]
    shard_rows, shard_width = shard
    copies = []

    def send(source, target):
        copy = pltpu.make_async_copy(source, target, sems.at[len(copies)])
        copy.start()
        copies.append(copy)

    for target, (distance, with_hidden, pieces) in zip(outs, messages):
        if with_hidden:
            base = sum(rows for _, _, rows in pieces)
            first_row = pl.multiple_of(tensor * shard_rows, shard_rows)
            for i in range(shard_width // kv_cols):
                column = pl.multiple_of((myself ^ distance) * shard_width + i * kv_cols, kv_cols)
                send(
                    hidden_ref.at[pl.ds(first_row, shard_rows), pl.ds(column, kv_cols)],
                    target.at[pl.ds(base + i * shard_rows, shard_rows)],
                )
    for distance in sorted({message[0] for message in messages}, reverse=True):
        wanted = []
        for target, message in zip(outs, messages):
            base = 0
            for span, start, rows in message[2] if message[0] == distance else ():
                wanted.append((span, pl.ds(start, rows), target.at[pl.ds(base, rows)]))
                base += rows
        if not wanted:
            continue
        count = jnp.int32(0)
        chosen = [jnp.int32(0) for _ in wanted]
        for j in range(span_count):
            home = slot_ref[retrieval_ref[myself ^ distance, j]]
            mine = home // slot_count == myself
            for i, (span, _, _) in enumerate(wanted):
                chosen[i] = jnp.where(mine & (count == span), home - myself * slot_count, chosen[i])
            count = count + jnp.where(mine, 1, 0)
        for slot, (_, rows, target) in zip(chosen, wanted):
            send(store_ref.at[slot, rows], target)
    if with_table:
        lines, columns = table_ref.shape
        per_pair = lines >> (lax.axis_size("store").bit_length() - 1)

        def clear(line, carry):
            for column in range(columns):
                table_ref[line, column] = 0
            return carry

        def fill(j, carry):
            home = slot_ref[retrieval_ref[myself, j]]
            owner = home // slot_count
            first = (owner ^ myself) * per_pair
            taken = jnp.int32(0)
            for span in range(per_pair):
                taken = taken + table_ref[first + span, 0]
            line = first + jnp.minimum(taken, per_pair - 1)
            table_ref[line, 0] = 1
            for column in range(rows_ref.shape[1]):
                table_ref[line, 1 + column] = rows_ref[j, column]
            table_ref[line, columns - 1] = home - owner * slot_count
            return carry

        lax.fori_loop(0, lines, clear, 0)
        lax.fori_loop(0, span_count, fill, 0)
    for copy in copies:
        copy.wait()


def pack(slots, retrieval, store, hidden, rows, messages, shard, lines):
    kv_cols = store.shape[2]
    with_table = rows is not None
    blocks = shard[1] // kv_cols
    shapes, n_copies = [], 0
    for _, with_hidden, pieces in messages:
        length = sum(rows for _, _, rows in pieces) + (blocks * shard[0] if with_hidden else 0)
        shapes.append(jax.ShapeDtypeStruct((length, kv_cols), store.dtype))
        n_copies += len(pieces) + (blocks if with_hidden else 0)
    specs = [vmem_spec()] * len(shapes)
    operands = [slots, retrieval, store, hidden]
    in_specs = [smem_spec()] * 2 + [hbm_spec()] * 2
    if with_table:
        operands.append(rows)
        in_specs.append(smem_spec())
        shapes.append(jax.ShapeDtypeStruct((lines, rows.shape[1] + 2), jnp.int32))
        specs.append(smem_spec())
    outs = pl.pallas_call(
        functools.partial(pack_kernel, messages, shard, with_table),
        out_shape=shapes,
        in_specs=in_specs,
        out_specs=specs,
        scratch_shapes=[pltpu.SemaphoreType.DMA((n_copies,))],
        compiler_params=pltpu.CompilerParams(vmem_limit_bytes=VMEM_LIMIT if with_table else FIRST_VMEM_LIMIT),
        cost_estimate=pl.CostEstimate(flops=0, bytes_accessed=0, transcendentals=0),
        name="pack_spans",
    )(*operands)
    return list(outs[: len(messages)]), outs[-1] if with_table else None


def project_kernel(shard_rows, distances, *refs):
    block_refs, (weight_ref, partial_ref, sent_ref) = refs[:-3], refs[-3:]
    n_store, group_rows, kv_cols = partial_ref.shape
    pieces = weight_ref.shape[0] // kv_cols
    total = 0.0
    for piece in range(pieces):
        rows = []
        for d in range(n_store):
            for ref in block_refs:
                length = n_store * pieces * shard_rows
                for base in range(0, ref.shape[0], length):
                    start = base + (d * pieces + piece) * shard_rows
                    rows.append(ref[start : start + shard_rows, :])
        total = total + jnp.dot(
            jnp.concatenate(rows, axis=0),
            weight_ref[piece * kv_cols : (piece + 1) * kv_cols, :],
            preferred_element_type=jnp.float32,
        )
    tensor = lax.axis_index("tensor")
    for d in range(n_store):
        for i, distance in enumerate(distances):
            base = d * group_rows + i * shard_rows
            block = total[base : base + shard_rows, :]
            row = pl.multiple_of((tensor ^ distance) * shard_rows, shard_rows)
            partial_ref[d, pl.ds(row, shard_rows), :] = block
            if d % 2:
                sent_ref[d // 2, pl.ds(row, shard_rows), :] = block.astype(sent_ref.dtype)


def project(blocks, weight, n_store, shard_rows, distances):
    group_rows = sum(block.shape[0] for block in blocks) * weight.shape[1]
    group_rows = group_rows // (n_store * weight.shape[0])
    kv_cols = weight.shape[1]
    return pl.pallas_call(
        functools.partial(project_kernel, shard_rows, tuple(distances)),
        out_shape=[
            jax.ShapeDtypeStruct((n_store, group_rows, kv_cols), jnp.float32),
            jax.ShapeDtypeStruct((n_store // 2, group_rows, kv_cols), jnp.bfloat16),
        ],
        in_specs=[vmem_spec()] * (len(blocks) + 1),
        out_specs=[vmem_spec()] * 2,
        compiler_params=pltpu.CompilerParams(vmem_limit_bytes=VMEM_LIMIT),
        cost_estimate=pl.CostEstimate(flops=0, bytes_accessed=0, transcendentals=0),
        name="project_rows",
    )(*blocks, weight)


def attend_kernel(parts, n_pieces, with_store, with_question, with_fresh, first, last, *refs):
    table_ref, query_ref, question_ref = refs[:3]
    refs = refs[3:]
    if with_store:
        store_ref, refs = refs[0], refs[1:]
    piece_refs, refs = refs[:n_pieces], refs[n_pieces:]
    if with_fresh:
        own_ref, other_ref = refs[:2]
        refs = refs[2:]
    if not first:
        blend_in, total_in, shift_in = refs[:3]
        refs = refs[3:]
    if last:
        out_ref, refs = refs[0], refs[1:]
    else:
        blend_out, total_out, shift_out = refs[:3]
        refs = refs[3:]
    if with_fresh:
        fresh_out, refs = refs[0], refs[1:]
    keys, values, live, refs = refs[0], refs[1], refs[2], refs[3:]
    if with_fresh:
        fresh_ref, fresh_sem, refs = refs[0], refs[1], refs[2:]
    if last:
        out_stage, sems = refs
    width = HEAD_WIDTH
    question_len, query_cols = query_ref.shape
    kv_heads = question_ref.shape[1] // (2 * width)
    group_cols = query_cols // kv_heads
    group_size = group_cols // width
    rows = PAIR * question_len
    pairs = group_size // PAIR
    contract = (((1,), (1,)), ((), ()))

    def out_copy(step, column):
        columns = pl.ds(column, PAIR * width)
        return pltpu.make_async_copy(out_stage.at[:, columns], out_ref.at[:, columns], sems.at[step])

    def fresh_copy():
        return pltpu.make_async_copy(fresh_ref, fresh_out, fresh_sem)

    if with_fresh:
        fresh_ref[...] = (own_ref[...] + other_ref[...].astype(jnp.float32)).astype(fresh_ref.dtype)
        fresh_copy().start()
    base = 0
    for line, start, length, _, _ in parts:
        row = start + lax.broadcasted_iota(jnp.int32, (length, width), 0)
        stale = row < jnp.where(table_ref[line, 0] == 0, start + length, 0)
        for column in range(1, table_ref.shape[1] - 1):
            stale = stale | (row == table_ref[line, column])
        live[base : base + length, :] = jnp.where(stale, 0.0, 1.0).astype(live.dtype)
        base += length
    values[:base, width:] = live[:base, :]
    if values.shape[0] > base:
        values[base:, width:] = jnp.ones((values.shape[0] - base, width), values.dtype)
    plain = values.shape[0] - (question_len if with_question else 0)

    def load(k):
        key_at = pl.ds(pl.multiple_of(k * 2 * width, 2 * width), width)
        value_at = pl.ds(pl.multiple_of(k * 2 * width + width, width), width)
        spare_key = question_ref[0:8, key_at][0:1].astype(jnp.float32)
        base = 0
        for line, start, length, source, offset in parts:
            here = slice(base, base + length)
            if with_store:
                slot = table_ref[line, table_ref.shape[1] - 1]
                key, value = store_ref[slot, :, key_at], store_ref[slot, :, value_at]
            else:
                at = slice(offset, offset + length)
                key, value = piece_refs[source][at, key_at], piece_refs[source][at, value_at]
            read = live[here, :].astype(jnp.float32) > 0.5
            keys[here, :] = jnp.where(read, key.astype(jnp.float32), spare_key).astype(keys.dtype)
            values[here, :width] = jnp.where(read, value.astype(jnp.float32), 0.0).astype(values.dtype)
            base += length
        for ref in ([fresh_ref] if with_fresh else []) + ([question_ref] if with_question else []):
            here = slice(base, base + ref.shape[0])
            keys[here, :] = ref[:, key_at]
            values[here, :width] = ref[:, value_at]
            base += ref.shape[0]

    def query_columns(k, start):
        return pl.ds(pl.multiple_of(k * group_cols + start * width, width), width)

    def score(k, pair):
        query = jnp.concatenate(
            [query_ref[:, query_columns(k, pair * PAIR + h)] for h in range(PAIR)], axis=0
        )
        scores = [
            lax.dot_general(query, keys[:plain, :], contract, preferred_element_type=jnp.float32)
        ]
        if with_question:
            asked = lax.dot_general(
                query, keys[plain:, :], contract, preferred_element_type=jnp.float32
            )
            asked = asked.reshape(PAIR, question_len, question_len)
            q_place = lax.broadcasted_iota(jnp.int32, asked.shape, 1)
            k_place = lax.broadcasted_iota(jnp.int32, asked.shape, 2)
            asked = jnp.where(k_place <= q_place, asked, -jnp.inf)
            scores.append(asked.reshape(rows, question_len))
        return scores

    def over(scores, shift):
        return [
            part - jnp.concatenate([shift] * (part.shape[1] // width), axis=1) for part in scores
        ]

    def blended(apart):
        blend, offset = 0.0, 0
        for part in apart:
            probs = jnp.exp2(part * EXP_SCALE).astype(jnp.bfloat16)
            blend = blend + jnp.dot(
                probs, values[offset : offset + part.shape[1], :], preferred_element_type=jnp.float32
            )
            offset += part.shape[1]
        return blend[:, :width], blend[:, width:]

    def new_shift(scores):
        highest = functools.reduce(
            jnp.maximum, [jnp.max(part, axis=1, keepdims=True) for part in scores]
        )
        return jnp.broadcast_to(highest, (rows, width))

    def finish(k, pair, here, blend, total, shift):
        if last:
            done = (blend / total).astype(out_ref.dtype)
            for h in range(PAIR):
                out_stage[:, query_columns(k, pair * PAIR + h)] = done[
                    h * question_len : (h + 1) * question_len
                ]
            column = pl.multiple_of(k * group_cols + pair * PAIR * width, PAIR * width)
            out_copy(k * pairs + pair, column).start()
        else:
            blend_out[here, :] = blend
            total_out[here, :] = total
            shift_out[here, :] = shift

    def wait_out():
        for step in range(kv_heads * pairs if last else 0):
            out_copy(step, step * PAIR * width).wait()

    def one_kv_head(k, worst):
        load(k)
        upcoming = score(k, 0)
        for pair in range(pairs):
            scores = upcoming
            if pair + 1 < pairs:
                upcoming = score(k, pair + 1)
            here = pl.ds(pl.multiple_of((k * pairs + pair) * rows, rows), rows)
            shift = new_shift(scores) if first else shift_in[here, :]
            apart = over(scores, shift)
            blend, total = blended(apart)
            if not first:
                for part in apart:
                    most = jnp.max(part.reshape(rows // 8, 8, part.shape[1]), axis=0)
                    for column in range(0, part.shape[1], width):
                        worst = jnp.maximum(worst, most[:, column : column + width])
                blend = blend + blend_in[here, :]
                total = total + total_in[here, :]
            finish(k, pair, here, blend, total, shift)
        return worst

    worst = lax.fori_loop(0, kv_heads, one_kv_head, jnp.full((8, width), -jnp.inf, jnp.float32))
    wait_out()

    def again(k, carry):
        load(k)

        def one_pair(pair, carry):
            here = pl.ds(pl.multiple_of((k * pairs + pair) * rows, rows), rows)
            scores = score(k, pair)
            before = shift_in[here, :]
            shift = jnp.maximum(new_shift(scores), before)
            fade = jnp.exp2((before - shift) * EXP_SCALE)
            blend, total = blended(over(scores, shift))
            blend = blend + blend_in[here, :] * fade
            total = total + total_in[here, :] * fade
            finish(k, pair, here, blend, total, shift)
            return carry

        return lax.fori_loop(0, pairs, one_pair, carry)

    if not first:

        @pl.when(jnp.max(worst) * EXP_SCALE > EXP_LIMIT)
        def _():
            lax.fori_loop(0, kv_heads, again, 0)
            wait_out()

    if with_fresh:
        fresh_copy().wait()


def attend(table, queries, question, parts, pieces, store, fresh, state, with_question, last):
    question_len, query_cols = queries.shape
    heads = query_cols // HEAD_WIDTH
    pairs = heads // PAIR
    first = state is None
    operands = [table, queries, question] + ([store] if store is not None else []) + list(pieces)
    held = sum(part[2] for part in parts)
    length = held + (question_len if with_question else 0)
    if fresh is not None:
        operands += list(fresh)
        length += fresh[0].shape[0]
    if not first:
        operands += list(state)
    scratch = [
        pltpu.VMEM((length, HEAD_WIDTH), jnp.bfloat16),
        pltpu.VMEM((length, 2 * HEAD_WIDTH), jnp.bfloat16),
        pltpu.VMEM((held, HEAD_WIDTH), jnp.bfloat16),
    ]
    if last:
        out_shape = [jax.ShapeDtypeStruct(queries.shape, queries.dtype)]
        out_specs = [hbm_spec()]
    else:
        out_shape = [jax.ShapeDtypeStruct((heads * question_len, HEAD_WIDTH), jnp.float32)] * 3
        out_specs = [vmem_spec()] * 3
    if fresh is not None:
        out_shape.append(jax.ShapeDtypeStruct(fresh[0].shape, jnp.bfloat16))
        out_specs.append(hbm_spec())
        scratch += [pltpu.VMEM(fresh[0].shape, jnp.bfloat16), pltpu.SemaphoreType.DMA]
    if last:
        scratch += [pltpu.VMEM(queries.shape, queries.dtype), pltpu.SemaphoreType.DMA((pairs,))]
    outs = pl.pallas_call(
        functools.partial(
            attend_kernel, tuple(parts), len(pieces), store is not None, with_question,
            fresh is not None, first, last,
        ),
        out_shape=out_shape,
        in_specs=[smem_spec()] + [vmem_spec()] * (len(operands) - 1),
        out_specs=out_specs,
        scratch_shapes=scratch,
        compiler_params=pltpu.CompilerParams(vmem_limit_bytes=VMEM_LIMIT),
        cost_estimate=pl.CostEstimate(
            flops=64 * heads * question_len * length * HEAD_WIDTH, bytes_accessed=0, transcendentals=0
        ),
        name="attend_spans",
    )(*operands)
    rows = None
    if fresh is not None:
        *outs, rows = outs
    return outs, rows


def local(
    queries,
    question_kv,
    key_value_store,
    span_store_slot,
    retrieval,
    recompute_rows,
    recompute_hidden,
    kv_weight,
):
    n_store = lax.axis_size("store")
    n_tensor = lax.axis_size("tensor")
    slot_count, span_len, kv_cols = key_value_store.shape
    span_count = retrieval.shape[1]
    recomp = recompute_rows.shape[2]
    model_width = recompute_hidden.shape[3]
    shard_rows = span_count * recomp // n_tensor
    per_pair = max(1, span_count // n_store)
    fresh_rows = span_count * recomp
    hidden = recompute_hidden.reshape(fresh_rows, model_width)
    question = question_kv[0]
    query_rows = queries[0]

    def exchange(piece, distance, axis, content):
        size = lax.axis_size(axis)
        with jax.named_scope(content + str(distance)):
            return lax.ppermute(piece, axis, [(i, i ^ distance) for i in range(size)])

    shard = (shard_rows, model_width // n_store)

    def packed(messages, rows=None):
        return pack(
            span_store_slot, retrieval, key_value_store, hidden, rows, messages, shard,
            n_store * per_pair,
        )

    away = list(range(n_store - 1, 0, -1))
    half = span_len // 2

    def cuts(distance):
        if per_pair == 1:
            return [span_len]
        if distance == 1:
            return [2 * span_len, (per_pair - 2) * span_len]
        if distance % 2:
            return [span_len] * (per_pair - 2) + [span_len + half, half]
        return [span_len + half] + [span_len] * (per_pair - 2) + [half]

    def pieces_of(first, length):
        pieces = []
        while length:
            span, start = divmod(first, span_len)
            rows = min(span_len - start, length)
            pieces.append((span, start, rows))
            first, length = first + rows, length - rows
        return pieces

    messages = {}
    for d in away:
        first = 0
        for number, length in enumerate(cuts(d)):
            if length:
                messages[d, number] = (d, False, pieces_of(first, length))
            first += length
    count = 1 + max(number for _, number in messages)
    soon = [(d, 0) for d in away if d > 1]
    later = [key for number in range(count) for d in away for key in [(d, number)] if key in messages]
    later = [key for key in later if key not in soon]
    outbox, _ = packed([(d, True, []) for d in away] + [messages[key] for key in soon])
    hidden_in = {d: exchange(piece, d, "store", "columns") for d, piece in zip(away, outbox)}
    coming = [exchange(piece, key[0], "store", "spans0_") for key, piece in zip(soon, outbox[len(away) :])]
    (hidden_own, *outbox), table = packed(
        [(0, True, [])] + [messages[key] for key in later], recompute_rows[0]
    )
    outbox = dict(zip(later, outbox))
    coming.append(exchange(after(outbox[1, 0], hidden_in[1]), 1, "store", "spans0_"))

    def behind(pieces, state):
        return [after(piece, state[0]) for piece in pieces]

    def block(keys, state, own=(), with_question=False, fresh=None, last=False):
        parts = [(span, 0, span_len, 0, 0) for span in own]
        for source, (d, number) in enumerate(keys):
            offset = 0
            for span, start, rows in messages[d, number][2]:
                parts.append((d * per_pair + span, start, rows, source, offset))
                offset += rows
        return attend(
            table, query_rows, question, parts, [arrived[key] for key in keys],
            key_value_store if own else None, fresh, state, with_question, last,
        )

    def recomputed():
        blocks = [hidden_own] + behind([hidden_in[d] for d in away[::-1]], state)
        distances = [0]
        for step, bit in enumerate(reversed(range(n_tensor.bit_length() - 1))):
            distances += [distance ^ (1 << bit) for distance in distances]
            gathered = jnp.concatenate(blocks, axis=0)
            if not step:
                yield gathered
            blocks = [gathered, exchange(gathered, 1 << bit, "tensor", "hidden")]
        partial, sent = project(blocks, kv_weight, n_store, shard_rows, distances)
        bits = n_store.bit_length() - 1
        for bit in range(bits):
            if bit:
                sent = partial[1::2].astype(jnp.bfloat16)
            if bit == 1:
                yield sent
            other = exchange(sent, 1 << bit, "store", "partial")
            if bit + 1 < bits:
                partial = partial[0::2] + other.astype(jnp.float32)
        yield partial[0], other[0]

    arrived = {}
    steps = recomputed()
    middle = (per_pair + 1) // 2
    state, _ = block([], None, range(middle), True)
    state = [after(state[0], next(steps)), *state[1:]]
    if per_pair > 1:
        state, _ = block([], state, range(middle, per_pair))
    arrived.update(zip(soon + [(1, 0)], behind(coming, state)))
    fresh = rows = None
    for number in range(1, count):
        keys = [key for key in later if key[1] == number]
        coming = [
            exchange(after(outbox[key], arrived[key[0], number - 1]), key[0], "store", "spans%d_" % number)
            for key in keys
        ]
        if number == 2:
            state = [after(state[0], next(steps)), *state[1:]]
        if number == count - 1:
            *_, fresh = steps
        here = [(d, number - 1) for d in away if (d, number - 1) in arrived]
        state, rows = block(here, state, fresh=fresh)
        arrived.update(zip(keys, behind(coming, state)))
    keys = [(d, count - 1) for d in away[::-1] if (d, count - 1) in arrived]
    size = 6
    batches = [keys[i : i + size] for i in range(0, len(keys), size)]
    for i, keys in enumerate(batches):
        joins, last = rows is None, i == len(batches) - 1
        if joins:
            *_, fresh = steps
        state, now = block(keys, state, fresh=fresh if joins else None, last=last)
        rows = now if joins else rows
    return (state[0][None], rows.reshape(1, span_count, recomp, kv_cols))


def solution(mesh):
    in_specs = (
        P(("groups", "store"), None, "tensor"),
        P(("groups", "store"), None, "tensor"),
        P(("groups", "store"), None, "tensor"),
        P("groups"),
        P("groups", None),
        P(("groups", "store"), None, None),
        P(("groups", "store"), None, None, None),
        P("store", "tensor"),
    )
    out_specs = (
        P(("groups", "store"), None, "tensor"),
        P(("groups", "store"), None, None, "tensor"),
    )
    return jax.shard_map(local, mesh=mesh, in_specs=in_specs, out_specs=out_specs, check_vma=False)
```

```python
import functools
import math

import jax
import jax.numpy as jnp
from jax import lax
from jax.experimental import pallas as pl
from jax.experimental.pallas import tpu as pltpu
from jax.sharding import PartitionSpec as P

HEAD_WIDTH = 128
EXP_SCALE = math.log2(math.e) * HEAD_WIDTH ** (-0.5)
EXP_LIMIT = 64.0
PAIR = 2
VMEM_LIMIT = 28 * 1024 * 1024
FIRST_VMEM_LIMIT = 60 * 1024 * 1024


def hbm_spec():
    return pl.BlockSpec(memory_space=pltpu.HBM)


def smem_spec():
    return pl.BlockSpec(memory_space=pltpu.SMEM)


def vmem_spec():
    return pl.BlockSpec(memory_space=pltpu.VMEM)


def after(array, *others):
    return lax.optimization_barrier((array,) + others)[0]


def pack_kernel(messages, shard, with_table, *refs):
    slot_ref, retrieval_ref, store_ref, hidden_ref = refs[:4]
    refs = refs[4:]
    if with_table:
        rows_ref, refs = refs[0], refs[1:]
    outs, refs = refs[: len(messages)], refs[len(messages) :]
    if with_table:
        table_ref, refs = refs[0], refs[1:]
    sems = refs[0]
    myself = lax.axis_index("store")
    tensor = lax.axis_index("tensor")
    slot_count, _, kv_cols = store_ref.shape
    span_count = retrieval_ref.shape[1]
    shard_rows, shard_width = shard
    copies = []

    def send(source, target):
        copy = pltpu.make_async_copy(source, target, sems.at[len(copies)])
        copy.start()
        copies.append(copy)

    for target, (distance, with_hidden, pieces) in zip(outs, messages):
        if with_hidden:
            base = sum(rows for _, _, rows in pieces)
            first_row = pl.multiple_of(tensor * shard_rows, shard_rows)
            for i in range(shard_width // kv_cols):
                column = pl.multiple_of((myself ^ distance) * shard_width + i * kv_cols, kv_cols)
                send(
                    hidden_ref.at[pl.ds(first_row, shard_rows), pl.ds(column, kv_cols)],
                    target.at[pl.ds(base + i * shard_rows, shard_rows)],
                )
    for distance in sorted({message[0] for message in messages}, reverse=True):
        wanted = []
        for target, message in zip(outs, messages):
            base = 0
            for span, start, rows in message[2] if message[0] == distance else ():
                wanted.append((span, pl.ds(start, rows), target.at[pl.ds(base, rows)]))
                base += rows
        if not wanted:
            continue
        count = jnp.int32(0)
        chosen = [jnp.int32(0) for _ in wanted]
        for j in range(span_count):
            home = slot_ref[retrieval_ref[myself ^ distance, j]]
            mine = home // slot_count == myself
            for i, (span, _, _) in enumerate(wanted):
                chosen[i] = jnp.where(mine & (count == span), home - myself * slot_count, chosen[i])
            count = count + jnp.where(mine, 1, 0)
        for slot, (_, rows, target) in zip(chosen, wanted):
            send(store_ref.at[slot, rows], target)
    if with_table:
        lines, columns = table_ref.shape
        per_pair = lines >> (lax.axis_size("store").bit_length() - 1)

        def clear(line, carry):
            for column in range(columns):
                table_ref[line, column] = 0
            return carry

        def fill(j, carry):
            home = slot_ref[retrieval_ref[myself, j]]
            owner = home // slot_count
            first = (owner ^ myself) * per_pair
            taken = jnp.int32(0)
            for span in range(per_pair):
                taken = taken + table_ref[first + span, 0]
            line = first + jnp.minimum(taken, per_pair - 1)
            table_ref[line, 0] = 1
            for column in range(rows_ref.shape[1]):
                table_ref[line, 1 + column] = rows_ref[j, column]
            table_ref[line, columns - 1] = home - owner * slot_count
            return carry

        lax.fori_loop(0, lines, clear, 0)
        lax.fori_loop(0, span_count, fill, 0)
    for copy in copies:
        copy.wait()


def pack(slots, retrieval, store, hidden, rows, messages, shard, lines):
    kv_cols = store.shape[2]
    with_table = rows is not None
    blocks = shard[1] // kv_cols
    shapes, n_copies = [], 0
    for _, with_hidden, pieces in messages:
        length = sum(rows for _, _, rows in pieces) + (blocks * shard[0] if with_hidden else 0)
        shapes.append(jax.ShapeDtypeStruct((length, kv_cols), store.dtype))
        n_copies += len(pieces) + (blocks if with_hidden else 0)
    specs = [vmem_spec()] * len(shapes)
    operands = [slots, retrieval, store, hidden]
    in_specs = [smem_spec()] * 2 + [hbm_spec()] * 2
    if with_table:
        operands.append(rows)
        in_specs.append(smem_spec())
        shapes.append(jax.ShapeDtypeStruct((lines, rows.shape[1] + 2), jnp.int32))
        specs.append(smem_spec())
    outs = pl.pallas_call(
        functools.partial(pack_kernel, messages, shard, with_table),
        out_shape=shapes,
        in_specs=in_specs,
        out_specs=specs,
        scratch_shapes=[pltpu.SemaphoreType.DMA((n_copies,))],
        compiler_params=pltpu.CompilerParams(vmem_limit_bytes=VMEM_LIMIT if with_table else FIRST_VMEM_LIMIT),
        cost_estimate=pl.CostEstimate(flops=0, bytes_accessed=0, transcendentals=0),
        name="pack_spans",
    )(*operands)
    return list(outs[: len(messages)]), outs[-1] if with_table else None


def project_kernel(shard_rows, distances, *refs):
    block_refs, (weight_ref, partial_ref, sent_ref) = refs[:-3], refs[-3:]
    n_store, group_rows, kv_cols = partial_ref.shape
    pieces = weight_ref.shape[0] // kv_cols
    total = 0.0
    for piece in range(pieces):
        rows = []
        for d in range(n_store):
            for ref in block_refs:
                length = n_store * pieces * shard_rows
                for base in range(0, ref.shape[0], length):
                    start = base + (d * pieces + piece) * shard_rows
                    rows.append(ref[start : start + shard_rows, :])
        total = total + jnp.dot(
            jnp.concatenate(rows, axis=0),
            weight_ref[piece * kv_cols : (piece + 1) * kv_cols, :],
            preferred_element_type=jnp.float32,
        )
    tensor = lax.axis_index("tensor")
    for d in range(n_store):
        for i, distance in enumerate(distances):
            base = d * group_rows + i * shard_rows
            block = total[base : base + shard_rows, :]
            row = pl.multiple_of((tensor ^ distance) * shard_rows, shard_rows)
            partial_ref[d, pl.ds(row, shard_rows), :] = block
            if d % 2:
                sent_ref[d // 2, pl.ds(row, shard_rows), :] = block.astype(sent_ref.dtype)


def project(blocks, weight, n_store, shard_rows, distances):
    group_rows = sum(block.shape[0] for block in blocks) * weight.shape[1]
    group_rows = group_rows // (n_store * weight.shape[0])
    kv_cols = weight.shape[1]
    return pl.pallas_call(
        functools.partial(project_kernel, shard_rows, tuple(distances)),
        out_shape=[
            jax.ShapeDtypeStruct((n_store, group_rows, kv_cols), jnp.float32),
            jax.ShapeDtypeStruct((n_store // 2, group_rows, kv_cols), jnp.bfloat16),
        ],
        in_specs=[vmem_spec()] * (len(blocks) + 1),
        out_specs=[vmem_spec()] * 2,
        compiler_params=pltpu.CompilerParams(vmem_limit_bytes=VMEM_LIMIT),
        cost_estimate=pl.CostEstimate(flops=0, bytes_accessed=0, transcendentals=0),
        name="project_rows",
    )(*blocks, weight)


def attend_kernel(parts, n_pieces, with_store, with_question, with_fresh, first, last, *refs):
    table_ref, query_ref, question_ref = refs[:3]
    refs = refs[3:]
    if with_store:
        store_ref, refs = refs[0], refs[1:]
    piece_refs, refs = refs[:n_pieces], refs[n_pieces:]
    if with_fresh:
        own_ref, other_ref = refs[:2]
        refs = refs[2:]
    if not first:
        blend_in, total_in, shift_in = refs[:3]
        refs = refs[3:]
    if last:
        out_ref, refs = refs[0], refs[1:]
    else:
        blend_out, total_out, shift_out = refs[:3]
        refs = refs[3:]
    if with_fresh:
        fresh_out, refs = refs[0], refs[1:]
    keys, values, live, refs = refs[0], refs[1], refs[2], refs[3:]
    if with_fresh:
        fresh_ref, fresh_sem, refs = refs[0], refs[1], refs[2:]
    if last:
        out_stage, sems = refs
    width = HEAD_WIDTH
    question_len, query_cols = query_ref.shape
    kv_heads = question_ref.shape[1] // (2 * width)
    group_cols = query_cols // kv_heads
    group_size = group_cols // width
    rows = PAIR * question_len
    pairs = group_size // PAIR
    contract = (((1,), (1,)), ((), ()))

    def out_copy(step, column):
        columns = pl.ds(column, PAIR * width)
        return pltpu.make_async_copy(out_stage.at[:, columns], out_ref.at[:, columns], sems.at[step])

    def fresh_copy():
        return pltpu.make_async_copy(fresh_ref, fresh_out, fresh_sem)

    if with_fresh:
        fresh_ref[...] = (own_ref[...] + other_ref[...].astype(jnp.float32)).astype(fresh_ref.dtype)
        fresh_copy().start()
    base = 0
    for line, start, length, _, _ in parts:
        row = start + lax.broadcasted_iota(jnp.int32, (length, width), 0)
        stale = row < jnp.where(table_ref[line, 0] == 0, start + length, 0)
        for column in range(1, table_ref.shape[1] - 1):
            stale = stale | (row == table_ref[line, column])
        live[base : base + length, :] = jnp.where(stale, 0.0, 1.0).astype(live.dtype)
        base += length
    values[:base, width:] = live[:base, :]
    if values.shape[0] > base:
        values[base:, width:] = jnp.ones((values.shape[0] - base, width), values.dtype)
    plain = values.shape[0] - (question_len if with_question else 0)

    def load(k):
        key_at = pl.ds(pl.multiple_of(k * 2 * width, 2 * width), width)
        value_at = pl.ds(pl.multiple_of(k * 2 * width + width, width), width)
        spare_key = question_ref[0:8, key_at][0:1].astype(jnp.float32)
        base = 0
        for line, start, length, source, offset in parts:
            here = slice(base, base + length)
            if with_store:
                slot = table_ref[line, table_ref.shape[1] - 1]
                key, value = store_ref[slot, :, key_at], store_ref[slot, :, value_at]
            else:
                at = slice(offset, offset + length)
                key, value = piece_refs[source][at, key_at], piece_refs[source][at, value_at]
            read = live[here, :].astype(jnp.float32) > 0.5
            keys[here, :] = jnp.where(read, key.astype(jnp.float32), spare_key).astype(keys.dtype)
            values[here, :width] = jnp.where(read, value.astype(jnp.float32), 0.0).astype(values.dtype)
            base += length
        for ref in ([fresh_ref] if with_fresh else []) + ([question_ref] if with_question else []):
            here = slice(base, base + ref.shape[0])
            keys[here, :] = ref[:, key_at]
            values[here, :width] = ref[:, value_at]
            base += ref.shape[0]

    def query_columns(k, start):
        return pl.ds(pl.multiple_of(k * group_cols + start * width, width), width)

    def score(k, pair):
        query = jnp.concatenate(
            [query_ref[:, query_columns(k, pair * PAIR + h)] for h in range(PAIR)], axis=0
        )
        scores = [
            lax.dot_general(query, keys[:plain, :], contract, preferred_element_type=jnp.float32)
        ]
        if with_question:
            asked = lax.dot_general(
                query, keys[plain:, :], contract, preferred_element_type=jnp.float32
            )
            asked = asked.reshape(PAIR, question_len, question_len)
            q_place = lax.broadcasted_iota(jnp.int32, asked.shape, 1)
            k_place = lax.broadcasted_iota(jnp.int32, asked.shape, 2)
            asked = jnp.where(k_place <= q_place, asked, -jnp.inf)
            scores.append(asked.reshape(rows, question_len))
        return scores

    def over(scores, shift):
        return [
            part - jnp.concatenate([shift] * (part.shape[1] // width), axis=1) for part in scores
        ]

    def blended(apart):
        blend, offset = 0.0, 0
        for part in apart:
            probs = jnp.exp2(part * EXP_SCALE).astype(jnp.bfloat16)
            blend = blend + jnp.dot(
                probs, values[offset : offset + part.shape[1], :], preferred_element_type=jnp.float32
            )
            offset += part.shape[1]
        return blend[:, :width], blend[:, width:]

    def new_shift(scores):
        highest = functools.reduce(
            jnp.maximum, [jnp.max(part, axis=1, keepdims=True) for part in scores]
        )
        return jnp.broadcast_to(highest, (rows, width))

    def finish(k, pair, here, blend, total, shift):
        if last:
            done = (blend / total).astype(out_ref.dtype)
            for h in range(PAIR):
                out_stage[:, query_columns(k, pair * PAIR + h)] = done[
                    h * question_len : (h + 1) * question_len
                ]
            column = pl.multiple_of(k * group_cols + pair * PAIR * width, PAIR * width)
            out_copy(k * pairs + pair, column).start()
        else:
            blend_out[here, :] = blend
            total_out[here, :] = total
            shift_out[here, :] = shift

    def wait_out():
        for step in range(kv_heads * pairs if last else 0):
            out_copy(step, step * PAIR * width).wait()

    def one_kv_head(k, worst):
        load(k)
        upcoming = score(k, 0)
        for pair in range(pairs):
            scores = upcoming
            if pair + 1 < pairs:
                upcoming = score(k, pair + 1)
            here = pl.ds(pl.multiple_of((k * pairs + pair) * rows, rows), rows)
            shift = new_shift(scores) if first else shift_in[here, :]
            apart = over(scores, shift)
            blend, total = blended(apart)
            if not first:
                for part in apart:
                    most = jnp.max(part.reshape(rows // 8, 8, part.shape[1]), axis=0)
                    for column in range(0, part.shape[1], width):
                        worst = jnp.maximum(worst, most[:, column : column + width])
                blend = blend + blend_in[here, :]
                total = total + total_in[here, :]
            finish(k, pair, here, blend, total, shift)
        return worst

    worst = lax.fori_loop(0, kv_heads, one_kv_head, jnp.full((8, width), -jnp.inf, jnp.float32))
    wait_out()

    def again(k, carry):
        load(k)

        def one_pair(pair, carry):
            here = pl.ds(pl.multiple_of((k * pairs + pair) * rows, rows), rows)
            scores = score(k, pair)
            before = shift_in[here, :]
            shift = jnp.maximum(new_shift(scores), before)
            fade = jnp.exp2((before - shift) * EXP_SCALE)
            blend, total = blended(over(scores, shift))
            blend = blend + blend_in[here, :] * fade
            total = total + total_in[here, :] * fade
            finish(k, pair, here, blend, total, shift)
            return carry

        return lax.fori_loop(0, pairs, one_pair, carry)

    if not first:

        @pl.when(jnp.max(worst) * EXP_SCALE > EXP_LIMIT)
        def _():
            lax.fori_loop(0, kv_heads, again, 0)
            wait_out()

    if with_fresh:
        fresh_copy().wait()


def attend(table, queries, question, parts, pieces, store, fresh, state, with_question, last):
    question_len, query_cols = queries.shape
    heads = query_cols // HEAD_WIDTH
    pairs = heads // PAIR
    first = state is None
    operands = [table, queries, question] + ([store] if store is not None else []) + list(pieces)
    held = sum(part[2] for part in parts)
    length = held + (question_len if with_question else 0)
    if fresh is not None:
        operands += list(fresh)
        length += fresh[0].shape[0]
    if not first:
        operands += list(state)
    scratch = [
        pltpu.VMEM((length, HEAD_WIDTH), jnp.bfloat16),
        pltpu.VMEM((length, 2 * HEAD_WIDTH), jnp.bfloat16),
        pltpu.VMEM((held, HEAD_WIDTH), jnp.bfloat16),
    ]
    if last:
        out_shape = [jax.ShapeDtypeStruct(queries.shape, queries.dtype)]
        out_specs = [hbm_spec()]
    else:
        out_shape = [jax.ShapeDtypeStruct((heads * question_len, HEAD_WIDTH), jnp.float32)] * 3
        out_specs = [vmem_spec()] * 3
    if fresh is not None:
        out_shape.append(jax.ShapeDtypeStruct(fresh[0].shape, jnp.bfloat16))
        out_specs.append(hbm_spec())
        scratch += [pltpu.VMEM(fresh[0].shape, jnp.bfloat16), pltpu.SemaphoreType.DMA]
    if last:
        scratch += [pltpu.VMEM(queries.shape, queries.dtype), pltpu.SemaphoreType.DMA((pairs,))]
    outs = pl.pallas_call(
        functools.partial(
            attend_kernel, tuple(parts), len(pieces), store is not None, with_question,
            fresh is not None, first, last,
        ),
        out_shape=out_shape,
        in_specs=[smem_spec()] + [vmem_spec()] * (len(operands) - 1),
        out_specs=out_specs,
        scratch_shapes=scratch,
        compiler_params=pltpu.CompilerParams(vmem_limit_bytes=VMEM_LIMIT),
        cost_estimate=pl.CostEstimate(
            flops=64 * heads * question_len * length * HEAD_WIDTH, bytes_accessed=0, transcendentals=0
        ),
        name="attend_spans",
    )(*operands)
    rows = None
    if fresh is not None:
        *outs, rows = outs
    return outs, rows


def local(
    queries,
    question_kv,
    key_value_store,
    span_store_slot,
    retrieval,
    recompute_rows,
    recompute_hidden,
    kv_weight,
):
    n_store = lax.axis_size("store")
    n_tensor = lax.axis_size("tensor")
    slot_count, span_len, kv_cols = key_value_store.shape
    span_count = retrieval.shape[1]
    recomp = recompute_rows.shape[2]
    model_width = recompute_hidden.shape[3]
    shard_rows = span_count * recomp // n_tensor
    per_pair = max(1, span_count // n_store)
    fresh_rows = span_count * recomp
    hidden = recompute_hidden.reshape(fresh_rows, model_width)
    question = question_kv[0]
    query_rows = queries[0]

    def exchange(piece, distance, axis, content):
        size = lax.axis_size(axis)
        with jax.named_scope(content + str(distance)):
            return lax.ppermute(piece, axis, [(i, i ^ distance) for i in range(size)])

    shard = (shard_rows, model_width // n_store)

    def packed(messages, rows=None):
        return pack(
            span_store_slot, retrieval, key_value_store, hidden, rows, messages, shard,
            n_store * per_pair,
        )

    away = list(range(n_store - 1, 0, -1))
    half = span_len // 2

    def cuts(distance):
        if per_pair == 1:
            return [span_len]
        if distance == 1:
            return [2 * span_len, (per_pair - 2) * span_len]
        if distance % 2:
            return [span_len] * (per_pair - 2) + [span_len + half, half]
        return [span_len + half] + [span_len] * (per_pair - 2) + [half]

    def pieces_of(first, length):
        pieces = []
        while length:
            span, start = divmod(first, span_len)
            rows = min(span_len - start, length)
            pieces.append((span, start, rows))
            first, length = first + rows, length - rows
        return pieces

    messages = {}
    for d in away:
        first = 0
        for number, length in enumerate(cuts(d)):
            if length:
                messages[d, number] = (d, False, pieces_of(first, length))
            first += length
    count = 1 + max(number for _, number in messages)
    soon = [(d, 0) for d in away if d > 1]
    later = [key for number in range(count) for d in away for key in [(d, number)] if key in messages]
    later = [key for key in later if key not in soon]
    outbox, _ = packed([(d, True, []) for d in away] + [messages[key] for key in soon])
    hidden_in = {d: exchange(piece, d, "store", "columns") for d, piece in zip(away, outbox)}
    coming = [exchange(piece, key[0], "store", "spans0_") for key, piece in zip(soon, outbox[len(away) :])]
    (hidden_own, *outbox), table = packed(
        [(0, True, [])] + [messages[key] for key in later], recompute_rows[0]
    )
    outbox = dict(zip(later, outbox))
    coming.append(exchange(after(outbox[1, 0], hidden_in[1]), 1, "store", "spans0_"))

    def behind(pieces, state):
        return [after(piece, state[0]) for piece in pieces]

    def block(keys, state, own=(), with_question=False, fresh=None, last=False):
        parts = [(span, 0, span_len, 0, 0) for span in own]
        for source, (d, number) in enumerate(keys):
            offset = 0
            for span, start, rows in messages[d, number][2]:
                parts.append((d * per_pair + span, start, rows, source, offset))
                offset += rows
        return attend(
            table, query_rows, question, parts, [arrived[key] for key in keys],
            key_value_store if own else None, fresh, state, with_question, last,
        )

    def recomputed():
        blocks = [hidden_own] + [hidden_in[d] for d in away[::-1]]
        distances = [0]
        for step, bit in enumerate(reversed(range(n_tensor.bit_length() - 1))):
            distances += [distance ^ (1 << bit) for distance in distances]
            gathered = jnp.concatenate(blocks, axis=0)
            if not step:
                yield gathered
            blocks = [gathered, exchange(gathered, 1 << bit, "tensor", "hidden")]
        partial, sent = project(blocks, kv_weight, n_store, shard_rows, distances)
        bits = n_store.bit_length() - 1
        for bit in range(bits):
            if bit:
                sent = partial[1::2].astype(jnp.bfloat16)
            if bit == 1:
                yield sent
            other = exchange(sent, 1 << bit, "store", "partial")
            if bit + 1 < bits:
                partial = partial[0::2] + other.astype(jnp.float32)
        yield partial[0], other[0]

    arrived = {}
    steps = recomputed()
    middle = (per_pair + 1) // 2
    state, _ = block([], None, range(middle), True)
    state = [after(state[0], next(steps)), *state[1:]]
    if per_pair > 1:
        state, _ = block([], state, range(middle, per_pair))
    arrived.update(zip(soon + [(1, 0)], behind(coming, state)))
    fresh = rows = None
    for number in range(1, count):
        keys = [key for key in later if key[1] == number]
        coming = [
            exchange(after(outbox[key], arrived[key[0], number - 1]), key[0], "store", "spans%d_" % number)
            for key in keys
        ]
        if number == 2:
            state = [after(state[0], next(steps)), *state[1:]]
        if number == count - 1:
            *_, fresh = steps
        here = [(d, number - 1) for d in away if (d, number - 1) in arrived]
        state, rows = block(here, state, fresh=fresh)
        arrived.update(zip(keys, behind(coming, state)))
    keys = [(d, count - 1) for d in away[::-1] if (d, count - 1) in arrived]
    size = 6
    batches = [keys[i : i + size] for i in range(0, len(keys), size)]
    for i, keys in enumerate(batches):
        joins, last = rows is None, i == len(batches) - 1
        if joins:
            *_, fresh = steps
        state, now = block(keys, state, fresh=fresh if joins else None, last=last)
        rows = now if joins else rows
    return (state[0][None], rows.reshape(1, span_count, recomp, kv_cols))


def solution(mesh):
    in_specs = (
        P(("groups", "store"), None, "tensor"),
        P(("groups", "store"), None, "tensor"),
        P(("groups", "store"), None, "tensor"),
        P("groups"),
        P("groups", None),
        P(("groups", "store"), None, None),
        P(("groups", "store"), None, None, None),
        P("store", "tensor"),
    )
    out_specs = (
        P(("groups", "store"), None, "tensor"),
        P(("groups", "store"), None, None, "tensor"),
    )
    return jax.shard_map(local, mesh=mesh, in_specs=in_specs, out_specs=out_specs, check_vma=False)
```

```python
import functools
import math

import jax
import jax.numpy as jnp
from jax import lax
from jax.experimental import pallas as pl
from jax.experimental.pallas import tpu as pltpu
from jax.sharding import PartitionSpec as P

HEAD_WIDTH = 128
EXP_SCALE = math.log2(math.e) * HEAD_WIDTH ** (-0.5)
EXP_LIMIT = 64.0
PAIR = 2
WINDOW = 3
VMEM_LIMIT = 28 * 1024 * 1024
FIRST_VMEM_LIMIT = 60 * 1024 * 1024


def hbm_spec():
    return pl.BlockSpec(memory_space=pltpu.HBM)


def smem_spec():
    return pl.BlockSpec(memory_space=pltpu.SMEM)


def vmem_spec():
    return pl.BlockSpec(memory_space=pltpu.VMEM)


def after(array, *others):
    return lax.optimization_barrier((array,) + others)[0]


def pack_kernel(messages, shard, with_table, *refs):
    slot_ref, retrieval_ref, store_ref, hidden_ref = refs[:4]
    refs = refs[4:]
    if with_table:
        rows_ref, refs = refs[0], refs[1:]
    outs, refs = refs[: len(messages)], refs[len(messages) :]
    if with_table:
        table_ref, refs = refs[0], refs[1:]
    sems = refs[0]
    myself = lax.axis_index("store")
    tensor = lax.axis_index("tensor")
    slot_count, _, kv_cols = store_ref.shape
    span_count = retrieval_ref.shape[1]
    shard_rows, shard_width = shard
    copies = []

    def send(source, target):
        copy = pltpu.make_async_copy(source, target, sems.at[len(copies)])
        copy.start()
        copies.append(copy)

    for target, (distance, with_hidden, pieces) in zip(outs, messages):
        if with_hidden:
            base = sum(rows for _, _, rows in pieces)
            first_row = pl.multiple_of(tensor * shard_rows, shard_rows)
            for i in range(shard_width // kv_cols):
                column = pl.multiple_of((myself ^ distance) * shard_width + i * kv_cols, kv_cols)
                send(
                    hidden_ref.at[pl.ds(first_row, shard_rows), pl.ds(column, kv_cols)],
                    target.at[pl.ds(base + i * shard_rows, shard_rows)],
                )
    for distance in sorted({message[0] for message in messages}, reverse=True):
        wanted = []
        for target, message in zip(outs, messages):
            base = 0
            for span, start, rows in message[2] if message[0] == distance else ():
                wanted.append((span, pl.ds(start, rows), target.at[pl.ds(base, rows)]))
                base += rows
        if not wanted:
            continue
        count = jnp.int32(0)
        chosen = [jnp.int32(0) for _ in wanted]
        for j in range(span_count):
            home = slot_ref[retrieval_ref[myself ^ distance, j]]
            mine = home // slot_count == myself
            for i, (span, _, _) in enumerate(wanted):
                chosen[i] = jnp.where(mine & (count == span), home - myself * slot_count, chosen[i])
            count = count + jnp.where(mine, 1, 0)
        for slot, (_, rows, target) in zip(chosen, wanted):
            send(store_ref.at[slot, rows], target)
    if with_table:
        lines, columns = table_ref.shape
        per_pair = lines >> (lax.axis_size("store").bit_length() - 1)

        def clear(line, carry):
            for column in range(columns):
                table_ref[line, column] = 0
            return carry

        def fill(j, carry):
            home = slot_ref[retrieval_ref[myself, j]]
            owner = home // slot_count
            first = (owner ^ myself) * per_pair
            taken = jnp.int32(0)
            for span in range(per_pair):
                taken = taken + table_ref[first + span, 0]
            line = first + jnp.minimum(taken, per_pair - 1)
            table_ref[line, 0] = 1
            for column in range(rows_ref.shape[1]):
                table_ref[line, 1 + column] = rows_ref[j, column]
            table_ref[line, columns - 1] = home - owner * slot_count
            return carry

        lax.fori_loop(0, lines, clear, 0)
        lax.fori_loop(0, span_count, fill, 0)
    for copy in copies:
        copy.wait()


def pack(slots, retrieval, store, hidden, rows, messages, shard, lines):
    kv_cols = store.shape[2]
    with_table = rows is not None
    blocks = shard[1] // kv_cols
    shapes, n_copies = [], 0
    for _, with_hidden, pieces in messages:
        length = sum(rows for _, _, rows in pieces) + (blocks * shard[0] if with_hidden else 0)
        shapes.append(jax.ShapeDtypeStruct((length, kv_cols), store.dtype))
        n_copies += len(pieces) + (blocks if with_hidden else 0)
    specs = [vmem_spec()] * len(shapes)
    operands = [slots, retrieval, store, hidden]
    in_specs = [smem_spec()] * 2 + [hbm_spec()] * 2
    if with_table:
        operands.append(rows)
        in_specs.append(smem_spec())
        shapes.append(jax.ShapeDtypeStruct((lines, rows.shape[1] + 2), jnp.int32))
        specs.append(smem_spec())
    outs = pl.pallas_call(
        functools.partial(pack_kernel, messages, shard, with_table),
        out_shape=shapes,
        in_specs=in_specs,
        out_specs=specs,
        scratch_shapes=[pltpu.SemaphoreType.DMA((n_copies,))],
        compiler_params=pltpu.CompilerParams(vmem_limit_bytes=VMEM_LIMIT if with_table else FIRST_VMEM_LIMIT),
        cost_estimate=pl.CostEstimate(flops=0, bytes_accessed=0, transcendentals=0),
        name="pack_spans",
    )(*operands)
    return list(outs[: len(messages)]), outs[-1] if with_table else None


def project_kernel(shard_rows, distances, *refs):
    block_refs, (weight_ref, partial_ref, sent_ref) = refs[:-3], refs[-3:]
    n_store, group_rows, kv_cols = partial_ref.shape
    pieces = weight_ref.shape[0] // kv_cols
    total = 0.0
    for piece in range(pieces):
        rows = []
        for d in range(n_store):
            for ref in block_refs:
                length = n_store * pieces * shard_rows
                for base in range(0, ref.shape[0], length):
                    start = base + (d * pieces + piece) * shard_rows
                    rows.append(ref[start : start + shard_rows, :])
        total = total + jnp.dot(
            jnp.concatenate(rows, axis=0),
            weight_ref[piece * kv_cols : (piece + 1) * kv_cols, :],
            preferred_element_type=jnp.float32,
        )
    tensor = lax.axis_index("tensor")
    for d in range(n_store):
        for i, distance in enumerate(distances):
            base = d * group_rows + i * shard_rows
            block = total[base : base + shard_rows, :]
            row = pl.multiple_of((tensor ^ distance) * shard_rows, shard_rows)
            partial_ref[d, pl.ds(row, shard_rows), :] = block
            if d % 2:
                sent_ref[d // 2, pl.ds(row, shard_rows), :] = block.astype(sent_ref.dtype)


def project(blocks, weight, n_store, shard_rows, distances):
    group_rows = sum(block.shape[0] for block in blocks) * weight.shape[1]
    group_rows = group_rows // (n_store * weight.shape[0])
    kv_cols = weight.shape[1]
    return pl.pallas_call(
        functools.partial(project_kernel, shard_rows, tuple(distances)),
        out_shape=[
            jax.ShapeDtypeStruct((n_store, group_rows, kv_cols), jnp.float32),
            jax.ShapeDtypeStruct((n_store // 2, group_rows, kv_cols), jnp.bfloat16),
        ],
        in_specs=[vmem_spec()] * (len(blocks) + 1),
        out_specs=[vmem_spec()] * 2,
        compiler_params=pltpu.CompilerParams(vmem_limit_bytes=VMEM_LIMIT),
        cost_estimate=pl.CostEstimate(flops=0, bytes_accessed=0, transcendentals=0),
        name="project_rows",
    )(*blocks, weight)


def attend_kernel(parts, n_pieces, with_store, with_question, with_fresh, first, last, *refs):
    table_ref, query_ref, question_ref = refs[:3]
    refs = refs[3:]
    if with_store:
        store_ref, refs = refs[0], refs[1:]
    piece_refs, refs = refs[:n_pieces], refs[n_pieces:]
    if with_fresh:
        own_ref, other_ref = refs[:2]
        refs = refs[2:]
    if not first:
        blend_in, total_in, shift_in = refs[:3]
        refs = refs[3:]
    if last:
        out_ref, refs = refs[0], refs[1:]
    else:
        blend_out, total_out, shift_out = refs[:3]
        refs = refs[3:]
    if with_fresh:
        fresh_out, refs = refs[0], refs[1:]
    keys, values, live, refs = refs[0], refs[1], refs[2], refs[3:]
    if with_fresh:
        fresh_ref, fresh_sem, refs = refs[0], refs[1], refs[2:]
    if last:
        out_stage, sems = refs
    width = HEAD_WIDTH
    question_len, query_cols = query_ref.shape
    kv_heads = question_ref.shape[1] // (2 * width)
    group_cols = query_cols // kv_heads
    group_size = group_cols // width
    rows = PAIR * question_len
    pairs = group_size // PAIR
    contract = (((1,), (1,)), ((), ()))

    def out_copy(step, column):
        columns = pl.ds(column, PAIR * width)
        return pltpu.make_async_copy(out_stage.at[:, columns], out_ref.at[:, columns], sems.at[step])

    def fresh_copy():
        return pltpu.make_async_copy(fresh_ref, fresh_out, fresh_sem)

    if with_fresh:
        fresh_ref[...] = (own_ref[...] + other_ref[...].astype(jnp.float32)).astype(fresh_ref.dtype)
        fresh_copy().start()
    base = 0
    for line, start, length, _, _ in parts:
        row = start + lax.broadcasted_iota(jnp.int32, (length, width), 0)
        stale = row < jnp.where(table_ref[line, 0] == 0, start + length, 0)
        for column in range(1, table_ref.shape[1] - 1):
            stale = stale | (row == table_ref[line, column])
        live[base : base + length, :] = jnp.where(stale, 0.0, 1.0).astype(live.dtype)
        base += length
    values[:base, width:] = live[:base, :]
    if values.shape[0] > base:
        values[base:, width:] = jnp.ones((values.shape[0] - base, width), values.dtype)
    plain = values.shape[0] - (question_len if with_question else 0)

    def load(k):
        key_at = pl.ds(pl.multiple_of(k * 2 * width, 2 * width), width)
        value_at = pl.ds(pl.multiple_of(k * 2 * width + width, width), width)
        spare_key = question_ref[0:8, key_at][0:1].astype(jnp.float32)
        base = 0
        for line, start, length, source, offset in parts:
            here = slice(base, base + length)
            if with_store:
                slot = table_ref[line, table_ref.shape[1] - 1]
                key, value = store_ref[slot, :, key_at], store_ref[slot, :, value_at]
            else:
                at = slice(offset, offset + length)
                key, value = piece_refs[source][at, key_at], piece_refs[source][at, value_at]
            read = live[here, :].astype(jnp.float32) > 0.5
            keys[here, :] = jnp.where(read, key.astype(jnp.float32), spare_key).astype(keys.dtype)
            values[here, :width] = jnp.where(read, value.astype(jnp.float32), 0.0).astype(values.dtype)
            base += length
        for ref in ([fresh_ref] if with_fresh else []) + ([question_ref] if with_question else []):
            here = slice(base, base + ref.shape[0])
            keys[here, :] = ref[:, key_at]
            values[here, :width] = ref[:, value_at]
            base += ref.shape[0]

    def query_columns(k, start):
        return pl.ds(pl.multiple_of(k * group_cols + start * width, width), width)

    def score(k, pair):
        query = jnp.concatenate(
            [query_ref[:, query_columns(k, pair * PAIR + h)] for h in range(PAIR)], axis=0
        )
        scores = [
            lax.dot_general(query, keys[:plain, :], contract, preferred_element_type=jnp.float32)
        ]
        if with_question:
            asked = lax.dot_general(
                query, keys[plain:, :], contract, preferred_element_type=jnp.float32
            )
            asked = asked.reshape(PAIR, question_len, question_len)
            q_place = lax.broadcasted_iota(jnp.int32, asked.shape, 1)
            k_place = lax.broadcasted_iota(jnp.int32, asked.shape, 2)
            asked = jnp.where(k_place <= q_place, asked, -jnp.inf)
            scores.append(asked.reshape(rows, question_len))
        return scores

    def over(scores, shift):
        return [
            part - jnp.concatenate([shift] * (part.shape[1] // width), axis=1) for part in scores
        ]

    def blended(apart):
        blend, offset = 0.0, 0
        for part in apart:
            probs = jnp.exp2(part * EXP_SCALE).astype(jnp.bfloat16)
            blend = blend + jnp.dot(
                probs, values[offset : offset + part.shape[1], :], preferred_element_type=jnp.float32
            )
            offset += part.shape[1]
        return blend[:, :width], blend[:, width:]

    def new_shift(scores):
        highest = functools.reduce(
            jnp.maximum, [jnp.max(part, axis=1, keepdims=True) for part in scores]
        )
        return jnp.broadcast_to(highest, (rows, width))

    def finish(k, pair, here, blend, total, shift):
        if last:
            done = (blend / total).astype(out_ref.dtype)
            for h in range(PAIR):
                out_stage[:, query_columns(k, pair * PAIR + h)] = done[
                    h * question_len : (h + 1) * question_len
                ]
            column = pl.multiple_of(k * group_cols + pair * PAIR * width, PAIR * width)
            out_copy(k * pairs + pair, column).start()
        else:
            blend_out[here, :] = blend
            total_out[here, :] = total
            shift_out[here, :] = shift

    def wait_out():
        for step in range(kv_heads * pairs if last else 0):
            out_copy(step, step * PAIR * width).wait()

    def one_kv_head(k, worst):
        load(k)
        upcoming = score(k, 0)
        for pair in range(pairs):
            scores = upcoming
            if pair + 1 < pairs:
                upcoming = score(k, pair + 1)
            here = pl.ds(pl.multiple_of((k * pairs + pair) * rows, rows), rows)
            shift = new_shift(scores) if first else shift_in[here, :]
            apart = over(scores, shift)
            blend, total = blended(apart)
            if not first:
                for part in apart:
                    most = jnp.max(part.reshape(rows // 8, 8, part.shape[1]), axis=0)
                    for column in range(0, part.shape[1], width):
                        worst = jnp.maximum(worst, most[:, column : column + width])
                blend = blend + blend_in[here, :]
                total = total + total_in[here, :]
            finish(k, pair, here, blend, total, shift)
        return worst

    worst = lax.fori_loop(0, kv_heads, one_kv_head, jnp.full((8, width), -jnp.inf, jnp.float32))
    wait_out()

    def again(k, carry):
        load(k)

        def one_pair(pair, carry):
            here = pl.ds(pl.multiple_of((k * pairs + pair) * rows, rows), rows)
            scores = score(k, pair)
            before = shift_in[here, :]
            shift = jnp.maximum(new_shift(scores), before)
            fade = jnp.exp2((before - shift) * EXP_SCALE)
            blend, total = blended(over(scores, shift))
            blend = blend + blend_in[here, :] * fade
            total = total + total_in[here, :] * fade
            finish(k, pair, here, blend, total, shift)
            return carry

        return lax.fori_loop(0, pairs, one_pair, carry)

    if not first:

        @pl.when(jnp.max(worst) * EXP_SCALE > EXP_LIMIT)
        def _():
            lax.fori_loop(0, kv_heads, again, 0)
            wait_out()

    if with_fresh:
        fresh_copy().wait()


def attend(table, queries, question, parts, pieces, store, fresh, state, with_question, last):
    question_len, query_cols = queries.shape
    heads = query_cols // HEAD_WIDTH
    pairs = heads // PAIR
    first = state is None
    operands = [table, queries, question] + ([store] if store is not None else []) + list(pieces)
    held = sum(part[2] for part in parts)
    length = held + (question_len if with_question else 0)
    if fresh is not None:
        operands += list(fresh)
        length += fresh[0].shape[0]
    if not first:
        operands += list(state)
    scratch = [
        pltpu.VMEM((length, HEAD_WIDTH), jnp.bfloat16),
        pltpu.VMEM((length, 2 * HEAD_WIDTH), jnp.bfloat16),
        pltpu.VMEM((held, HEAD_WIDTH), jnp.bfloat16),
    ]
    if last:
        out_shape = [jax.ShapeDtypeStruct(queries.shape, queries.dtype)]
        out_specs = [hbm_spec()]
    else:
        out_shape = [jax.ShapeDtypeStruct((heads * question_len, HEAD_WIDTH), jnp.float32)] * 3
        out_specs = [vmem_spec()] * 3
    if fresh is not None:
        out_shape.append(jax.ShapeDtypeStruct(fresh[0].shape, jnp.bfloat16))
        out_specs.append(hbm_spec())
        scratch += [pltpu.VMEM(fresh[0].shape, jnp.bfloat16), pltpu.SemaphoreType.DMA]
    if last:
        scratch += [pltpu.VMEM(queries.shape, queries.dtype), pltpu.SemaphoreType.DMA((pairs,))]
    outs = pl.pallas_call(
        functools.partial(
            attend_kernel, tuple(parts), len(pieces), store is not None, with_question,
            fresh is not None, first, last,
        ),
        out_shape=out_shape,
        in_specs=[smem_spec()] + [vmem_spec()] * (len(operands) - 1),
        out_specs=out_specs,
        scratch_shapes=scratch,
        compiler_params=pltpu.CompilerParams(vmem_limit_bytes=VMEM_LIMIT),
        cost_estimate=pl.CostEstimate(
            flops=64 * heads * question_len * length * HEAD_WIDTH, bytes_accessed=0, transcendentals=0
        ),
        name="attend_spans",
    )(*operands)
    rows = None
    if fresh is not None:
        *outs, rows = outs
    return outs, rows


def local(
    queries,
    question_kv,
    key_value_store,
    span_store_slot,
    retrieval,
    recompute_rows,
    recompute_hidden,
    kv_weight,
):
    n_store = lax.axis_size("store")
    n_tensor = lax.axis_size("tensor")
    slot_count, span_len, kv_cols = key_value_store.shape
    span_count = retrieval.shape[1]
    recomp = recompute_rows.shape[2]
    model_width = recompute_hidden.shape[3]
    shard_rows = span_count * recomp // n_tensor
    per_pair = max(1, span_count // n_store)
    fresh_rows = span_count * recomp
    hidden = recompute_hidden.reshape(fresh_rows, model_width)
    question = question_kv[0]
    query_rows = queries[0]

    def exchange(piece, distance, axis, content):
        size = lax.axis_size(axis)
        with jax.named_scope(content + str(distance)):
            return lax.ppermute(piece, axis, [(i, i ^ distance) for i in range(size)])

    shard = (shard_rows, model_width // n_store)

    def packed(messages, rows=None):
        return pack(
            span_store_slot, retrieval, key_value_store, hidden, rows, messages, shard,
            n_store * per_pair,
        )

    away = list(range(n_store - 1, 0, -1))
    half = span_len // 2

    def cuts(distance):
        if per_pair == 1:
            return [span_len]
        if distance == 1:
            return [2 * span_len, (per_pair - 2) * span_len]
        return [span_len] * (per_pair - 1) + [half] * 2

    def pieces_of(first, length):
        pieces = []
        while length:
            span, start = divmod(first, span_len)
            rows = min(span_len - start, length)
            pieces.append((span, start, rows))
            first, length = first + rows, length - rows
        return pieces

    messages = {}
    for d in away:
        first = 0
        for number, length in enumerate(cuts(d)):
            if length:
                messages[d, number] = (d, not number, pieces_of(first, length))
            first += length
    outbox, _ = packed([messages[d, 0] for d in away])
    coming = [exchange(piece, d, "store", "spans0_") for piece, d in zip(outbox, away)]
    count = 1 + max(number for _, number in messages)
    later = [(d, number) for number in range(1, count) for d in away if (d, number) in messages]
    (hidden_own, *outbox), table = packed(
        [(0, True, [])] + [messages[key] for key in later], recompute_rows[0]
    )
    outbox = dict(zip(later, outbox))

    def behind(pieces, state):
        return [after(piece, state[0]) for piece in pieces]

    def block(keys, state, fresh=None, last=False):
        parts = []
        for source, (d, number) in enumerate(keys):
            offset = 0
            for span, start, rows in messages[d, number][2]:
                parts.append((d * per_pair + span, start, rows, source, offset))
                offset += rows
        if not keys:
            parts = [(span, 0, span_len, 0, 0) for span in range(per_pair)]
        return attend(
            table, query_rows, question, parts, [arrived[key] for key in keys],
            None if keys else key_value_store, fresh, state, not keys, last,
        )

    def recomputed():
        blocks = [hidden_own]
        for d in away[::-1]:
            piece = arrived[d, 0]
            blocks.append(piece[piece.shape[0] - hidden_own.shape[0] :])
        distances = [0]
        for step, bit in enumerate(reversed(range(n_tensor.bit_length() - 1))):
            distances += [distance ^ (1 << bit) for distance in distances]
            gathered = jnp.concatenate(blocks, axis=0)
            blocks = [gathered, exchange(gathered, 1 << bit, "tensor", "hidden")]
        partial, sent = project(blocks, kv_weight, n_store, shard_rows, distances)
        bits = n_store.bit_length() - 1
        for bit in range(bits):
            if bit:
                sent = partial[1::2].astype(jnp.bfloat16)
            yield sent
            other = exchange(sent, 1 << bit, "store", "partial")
            if bit + 1 < bits:
                partial = partial[0::2] + other.astype(jnp.float32)
        yield partial[0], other[0]

    arrived = {}
    state, _ = block([], None)
    arrived.update(zip([(d, 0) for d in away], behind(coming, state)))
    steps = recomputed()
    turns = [(d, number) for number in range(count) for d in away if d > 1]

    def leave(key):
        piece, (d, number) = outbox[key], key
        turn = turns.index(key if d > 1 else (away[0], number)) - WINDOW
        if turn >= 0:
            piece = after(piece, arrived[turns[turn]])
        return exchange(piece, d, "store", "spans%d_" % number)

    for number in range(1, count):
        keys = [key for key in later if key[1] == number]
        coming = [leave(key) for key in keys]
        here = [(d, number - 1) for d in away if (d, number - 1) in arrived]
        if 2 <= number < n_store.bit_length() + 1:
            state = [after(state[0], next(steps)), *state[1:]]
        state, _ = block(here, state)
        arrived.update(zip(keys, behind(coming, state)))

    keys = [(d, count - 1) for d in away[::-1] if (d, count - 1) in arrived]
    size = 6
    batches = [keys[i : i + size] for i in range(0, len(keys), size)]
    *_, fresh = steps
    for i, keys in enumerate(batches):
        last = i == len(batches) - 1
        if i:
            arrived.update(zip(keys, behind([arrived[key] for key in keys], state)))
            fresh = behind(fresh, state)
        state, rows = block(keys, state, fresh if last else None, last)
    return (state[0][None], rows.reshape(1, span_count, recomp, kv_cols))


def solution(mesh):
    in_specs = (
        P(("groups", "store"), None, "tensor"),
        P(("groups", "store"), None, "tensor"),
        P(("groups", "store"), None, "tensor"),
        P("groups"),
        P("groups", None),
        P(("groups", "store"), None, None),
        P(("groups", "store"), None, None, None),
        P("store", "tensor"),
    )
    out_specs = (
        P(("groups", "store"), None, "tensor"),
        P(("groups", "store"), None, None, "tensor"),
    )
    return jax.shard_map(local, mesh=mesh, in_specs=in_specs, out_specs=out_specs, check_vma=False)
```

```python
import functools
import math

import jax
import jax.numpy as jnp
from jax import lax
from jax.experimental import pallas as pl
from jax.experimental.pallas import tpu as pltpu
from jax.sharding import PartitionSpec as P

HEAD_WIDTH = 128
EXP_SCALE = math.log2(math.e) * HEAD_WIDTH ** (-0.5)
EXP_LIMIT = 64.0
PAIR = 2
WINDOW = 3
VMEM_LIMIT = 28 * 1024 * 1024
FIRST_VMEM_LIMIT = 60 * 1024 * 1024


def hbm_spec():
    return pl.BlockSpec(memory_space=pltpu.HBM)


def smem_spec():
    return pl.BlockSpec(memory_space=pltpu.SMEM)


def vmem_spec():
    return pl.BlockSpec(memory_space=pltpu.VMEM)


def after(array, *others):
    return lax.optimization_barrier((array,) + others)[0]


def pack_kernel(messages, shard, with_table, *refs):
    slot_ref, retrieval_ref, store_ref, hidden_ref = refs[:4]
    refs = refs[4:]
    if with_table:
        rows_ref, refs = refs[0], refs[1:]
    outs, refs = refs[: len(messages)], refs[len(messages) :]
    if with_table:
        table_ref, refs = refs[0], refs[1:]
    sems = refs[0]
    myself = lax.axis_index("store")
    tensor = lax.axis_index("tensor")
    slot_count, _, kv_cols = store_ref.shape
    span_count = retrieval_ref.shape[1]
    shard_rows, shard_width = shard
    copies = []

    def send(source, target):
        copy = pltpu.make_async_copy(source, target, sems.at[len(copies)])
        copy.start()
        copies.append(copy)

    for target, (distance, with_hidden, pieces) in zip(outs, messages):
        if with_hidden:
            base = sum(rows for _, _, rows in pieces)
            first_row = pl.multiple_of(tensor * shard_rows, shard_rows)
            for i in range(shard_width // kv_cols):
                column = pl.multiple_of((myself ^ distance) * shard_width + i * kv_cols, kv_cols)
                send(
                    hidden_ref.at[pl.ds(first_row, shard_rows), pl.ds(column, kv_cols)],
                    target.at[pl.ds(base + i * shard_rows, shard_rows)],
                )
    for distance in sorted({message[0] for message in messages}, reverse=True):
        wanted = []
        for target, message in zip(outs, messages):
            base = 0
            for span, start, rows in message[2] if message[0] == distance else ():
                wanted.append((span, pl.ds(start, rows), target.at[pl.ds(base, rows)]))
                base += rows
        if not wanted:
            continue
        count = jnp.int32(0)
        chosen = [jnp.int32(0) for _ in wanted]
        for j in range(span_count):
            home = slot_ref[retrieval_ref[myself ^ distance, j]]
            mine = home // slot_count == myself
            for i, (span, _, _) in enumerate(wanted):
                chosen[i] = jnp.where(mine & (count == span), home - myself * slot_count, chosen[i])
            count = count + jnp.where(mine, 1, 0)
        for slot, (_, rows, target) in zip(chosen, wanted):
            send(store_ref.at[slot, rows], target)
    if with_table:
        lines, columns = table_ref.shape
        per_pair = lines >> (lax.axis_size("store").bit_length() - 1)

        def clear(line, carry):
            for column in range(columns):
                table_ref[line, column] = 0
            return carry

        def fill(j, carry):
            home = slot_ref[retrieval_ref[myself, j]]
            owner = home // slot_count
            first = (owner ^ myself) * per_pair
            taken = jnp.int32(0)
            for span in range(per_pair):
                taken = taken + table_ref[first + span, 0]
            line = first + jnp.minimum(taken, per_pair - 1)
            table_ref[line, 0] = 1
            for column in range(rows_ref.shape[1]):
                table_ref[line, 1 + column] = rows_ref[j, column]
            table_ref[line, columns - 1] = home - owner * slot_count
            return carry

        lax.fori_loop(0, lines, clear, 0)
        lax.fori_loop(0, span_count, fill, 0)
    for copy in copies:
        copy.wait()


def pack(slots, retrieval, store, hidden, rows, messages, shard, lines):
    kv_cols = store.shape[2]
    with_table = rows is not None
    blocks = shard[1] // kv_cols
    shapes, n_copies = [], 0
    for _, with_hidden, pieces in messages:
        length = sum(rows for _, _, rows in pieces) + (blocks * shard[0] if with_hidden else 0)
        shapes.append(jax.ShapeDtypeStruct((length, kv_cols), store.dtype))
        n_copies += len(pieces) + (blocks if with_hidden else 0)
    specs = [vmem_spec()] * len(shapes)
    operands = [slots, retrieval, store, hidden]
    in_specs = [smem_spec()] * 2 + [hbm_spec()] * 2
    if with_table:
        operands.append(rows)
        in_specs.append(smem_spec())
        shapes.append(jax.ShapeDtypeStruct((lines, rows.shape[1] + 2), jnp.int32))
        specs.append(smem_spec())
    outs = pl.pallas_call(
        functools.partial(pack_kernel, messages, shard, with_table),
        out_shape=shapes,
        in_specs=in_specs,
        out_specs=specs,
        scratch_shapes=[pltpu.SemaphoreType.DMA((n_copies,))],
        compiler_params=pltpu.CompilerParams(vmem_limit_bytes=VMEM_LIMIT if with_table else FIRST_VMEM_LIMIT),
        cost_estimate=pl.CostEstimate(flops=0, bytes_accessed=0, transcendentals=0),
        name="pack_spans",
    )(*operands)
    return list(outs[: len(messages)]), outs[-1] if with_table else None


def project_kernel(shard_rows, distances, *refs):
    block_refs, (weight_ref, partial_ref, sent_ref) = refs[:-3], refs[-3:]
    n_store, group_rows, kv_cols = partial_ref.shape
    pieces = weight_ref.shape[0] // kv_cols
    total = 0.0
    for piece in range(pieces):
        rows = []
        for d in range(n_store):
            for ref in block_refs:
                length = n_store * pieces * shard_rows
                for base in range(0, ref.shape[0], length):
                    start = base + (d * pieces + piece) * shard_rows
                    rows.append(ref[start : start + shard_rows, :])
        total = total + jnp.dot(
            jnp.concatenate(rows, axis=0),
            weight_ref[piece * kv_cols : (piece + 1) * kv_cols, :],
            preferred_element_type=jnp.float32,
        )
    tensor = lax.axis_index("tensor")
    for d in range(n_store):
        for i, distance in enumerate(distances):
            base = d * group_rows + i * shard_rows
            block = total[base : base + shard_rows, :]
            row = pl.multiple_of((tensor ^ distance) * shard_rows, shard_rows)
            partial_ref[d, pl.ds(row, shard_rows), :] = block
            if d % 2:
                sent_ref[d // 2, pl.ds(row, shard_rows), :] = block.astype(sent_ref.dtype)


def project(blocks, weight, n_store, shard_rows, distances):
    group_rows = sum(block.shape[0] for block in blocks) * weight.shape[1]
    group_rows = group_rows // (n_store * weight.shape[0])
    kv_cols = weight.shape[1]
    return pl.pallas_call(
        functools.partial(project_kernel, shard_rows, tuple(distances)),
        out_shape=[
            jax.ShapeDtypeStruct((n_store, group_rows, kv_cols), jnp.float32),
            jax.ShapeDtypeStruct((n_store // 2, group_rows, kv_cols), jnp.bfloat16),
        ],
        in_specs=[vmem_spec()] * (len(blocks) + 1),
        out_specs=[vmem_spec()] * 2,
        compiler_params=pltpu.CompilerParams(vmem_limit_bytes=VMEM_LIMIT),
        cost_estimate=pl.CostEstimate(flops=0, bytes_accessed=0, transcendentals=0),
        name="project_rows",
    )(*blocks, weight)


def attend_kernel(parts, n_pieces, with_store, with_question, with_fresh, first, last, *refs):
    table_ref, query_ref, question_ref = refs[:3]
    refs = refs[3:]
    if with_store:
        store_ref, refs = refs[0], refs[1:]
    piece_refs, refs = refs[:n_pieces], refs[n_pieces:]
    if with_fresh:
        own_ref, other_ref = refs[:2]
        refs = refs[2:]
    if not first:
        blend_in, total_in, shift_in = refs[:3]
        refs = refs[3:]
    if last:
        out_ref, refs = refs[0], refs[1:]
    else:
        blend_out, total_out, shift_out = refs[:3]
        refs = refs[3:]
    if with_fresh:
        fresh_out, refs = refs[0], refs[1:]
    keys, values, live, refs = refs[0], refs[1], refs[2], refs[3:]
    if with_fresh:
        fresh_ref, fresh_sem, refs = refs[0], refs[1], refs[2:]
    if last:
        out_stage, sems = refs
    width = HEAD_WIDTH
    question_len, query_cols = query_ref.shape
    kv_heads = question_ref.shape[1] // (2 * width)
    group_cols = query_cols // kv_heads
    group_size = group_cols // width
    rows = PAIR * question_len
    pairs = group_size // PAIR
    contract = (((1,), (1,)), ((), ()))

    def out_copy(step, column):
        columns = pl.ds(column, PAIR * width)
        return pltpu.make_async_copy(out_stage.at[:, columns], out_ref.at[:, columns], sems.at[step])

    def fresh_copy():
        return pltpu.make_async_copy(fresh_ref, fresh_out, fresh_sem)

    if with_fresh:
        fresh_ref[...] = (own_ref[...] + other_ref[...].astype(jnp.float32)).astype(fresh_ref.dtype)
        fresh_copy().start()
    base = 0
    for line, start, length, _, _ in parts:
        row = start + lax.broadcasted_iota(jnp.int32, (length, width), 0)
        stale = row < jnp.where(table_ref[line, 0] == 0, start + length, 0)
        for column in range(1, table_ref.shape[1] - 1):
            stale = stale | (row == table_ref[line, column])
        live[base : base + length, :] = jnp.where(stale, 0.0, 1.0).astype(live.dtype)
        base += length
    values[:base, width:] = live[:base, :]
    if values.shape[0] > base:
        values[base:, width:] = jnp.ones((values.shape[0] - base, width), values.dtype)
    plain = values.shape[0] - (question_len if with_question else 0)

    def load(k):
        key_at = pl.ds(pl.multiple_of(k * 2 * width, 2 * width), width)
        value_at = pl.ds(pl.multiple_of(k * 2 * width + width, width), width)
        spare_key = question_ref[0:8, key_at][0:1].astype(jnp.float32)
        base = 0
        for line, start, length, source, offset in parts:
            here = slice(base, base + length)
            if with_store:
                slot = table_ref[line, table_ref.shape[1] - 1]
                key, value = store_ref[slot, :, key_at], store_ref[slot, :, value_at]
            else:
                at = slice(offset, offset + length)
                key, value = piece_refs[source][at, key_at], piece_refs[source][at, value_at]
            read = live[here, :].astype(jnp.float32) > 0.5
            keys[here, :] = jnp.where(read, key.astype(jnp.float32), spare_key).astype(keys.dtype)
            values[here, :width] = jnp.where(read, value.astype(jnp.float32), 0.0).astype(values.dtype)
            base += length
        for ref in ([fresh_ref] if with_fresh else []) + ([question_ref] if with_question else []):
            here = slice(base, base + ref.shape[0])
            keys[here, :] = ref[:, key_at]
            values[here, :width] = ref[:, value_at]
            base += ref.shape[0]

    def query_columns(k, start):
        return pl.ds(pl.multiple_of(k * group_cols + start * width, width), width)

    def score(k, pair):
        query = jnp.concatenate(
            [query_ref[:, query_columns(k, pair * PAIR + h)] for h in range(PAIR)], axis=0
        )
        scores = [
            lax.dot_general(query, keys[:plain, :], contract, preferred_element_type=jnp.float32)
        ]
        if with_question:
            asked = lax.dot_general(
                query, keys[plain:, :], contract, preferred_element_type=jnp.float32
            )
            asked = asked.reshape(PAIR, question_len, question_len)
            q_place = lax.broadcasted_iota(jnp.int32, asked.shape, 1)
            k_place = lax.broadcasted_iota(jnp.int32, asked.shape, 2)
            asked = jnp.where(k_place <= q_place, asked, -jnp.inf)
            scores.append(asked.reshape(rows, question_len))
        return scores

    def over(scores, shift):
        return [
            part - jnp.concatenate([shift] * (part.shape[1] // width), axis=1) for part in scores
        ]

    def blended(apart):
        blend, offset = 0.0, 0
        for part in apart:
            probs = jnp.exp2(part * EXP_SCALE).astype(jnp.bfloat16)
            blend = blend + jnp.dot(
                probs, values[offset : offset + part.shape[1], :], preferred_element_type=jnp.float32
            )
            offset += part.shape[1]
        return blend[:, :width], blend[:, width:]

    def new_shift(scores):
        highest = functools.reduce(
            jnp.maximum, [jnp.max(part, axis=1, keepdims=True) for part in scores]
        )
        return jnp.broadcast_to(highest, (rows, width))

    def finish(k, pair, here, blend, total, shift):
        if last:
            done = (blend / total).astype(out_ref.dtype)
            for h in range(PAIR):
                out_stage[:, query_columns(k, pair * PAIR + h)] = done[
                    h * question_len : (h + 1) * question_len
                ]
            column = pl.multiple_of(k * group_cols + pair * PAIR * width, PAIR * width)
            out_copy(k * pairs + pair, column).start()
        else:
            blend_out[here, :] = blend
            total_out[here, :] = total
            shift_out[here, :] = shift

    def wait_out():
        for step in range(kv_heads * pairs if last else 0):
            out_copy(step, step * PAIR * width).wait()

    def one_kv_head(k, worst):
        load(k)
        upcoming = score(k, 0)
        for pair in range(pairs):
            scores = upcoming
            if pair + 1 < pairs:
                upcoming = score(k, pair + 1)
            here = pl.ds(pl.multiple_of((k * pairs + pair) * rows, rows), rows)
            shift = new_shift(scores) if first else shift_in[here, :]
            apart = over(scores, shift)
            blend, total = blended(apart)
            if not first:
                for part in apart:
                    most = jnp.max(part.reshape(rows // 8, 8, part.shape[1]), axis=0)
                    for column in range(0, part.shape[1], width):
                        worst = jnp.maximum(worst, most[:, column : column + width])
                blend = blend + blend_in[here, :]
                total = total + total_in[here, :]
            finish(k, pair, here, blend, total, shift)
        return worst

    worst = lax.fori_loop(0, kv_heads, one_kv_head, jnp.full((8, width), -jnp.inf, jnp.float32))
    wait_out()

    def again(k, carry):
        load(k)

        def one_pair(pair, carry):
            here = pl.ds(pl.multiple_of((k * pairs + pair) * rows, rows), rows)
            scores = score(k, pair)
            before = shift_in[here, :]
            shift = jnp.maximum(new_shift(scores), before)
            fade = jnp.exp2((before - shift) * EXP_SCALE)
            blend, total = blended(over(scores, shift))
            blend = blend + blend_in[here, :] * fade
            total = total + total_in[here, :] * fade
            finish(k, pair, here, blend, total, shift)
            return carry

        return lax.fori_loop(0, pairs, one_pair, carry)

    if not first:

        @pl.when(jnp.max(worst) * EXP_SCALE > EXP_LIMIT)
        def _():
            lax.fori_loop(0, kv_heads, again, 0)
            wait_out()

    if with_fresh:
        fresh_copy().wait()


def attend(table, queries, question, parts, pieces, store, fresh, state, with_question, last):
    question_len, query_cols = queries.shape
    heads = query_cols // HEAD_WIDTH
    pairs = heads // PAIR
    first = state is None
    operands = [table, queries, question] + ([store] if store is not None else []) + list(pieces)
    held = sum(part[2] for part in parts)
    length = held + (question_len if with_question else 0)
    if fresh is not None:
        operands += list(fresh)
        length += fresh[0].shape[0]
    if not first:
        operands += list(state)
    scratch = [
        pltpu.VMEM((length, HEAD_WIDTH), jnp.bfloat16),
        pltpu.VMEM((length, 2 * HEAD_WIDTH), jnp.bfloat16),
        pltpu.VMEM((held, HEAD_WIDTH), jnp.bfloat16),
    ]
    if last:
        out_shape = [jax.ShapeDtypeStruct(queries.shape, queries.dtype)]
        out_specs = [hbm_spec()]
    else:
        out_shape = [jax.ShapeDtypeStruct((heads * question_len, HEAD_WIDTH), jnp.float32)] * 3
        out_specs = [vmem_spec()] * 3
    if fresh is not None:
        out_shape.append(jax.ShapeDtypeStruct(fresh[0].shape, jnp.bfloat16))
        out_specs.append(hbm_spec())
        scratch += [pltpu.VMEM(fresh[0].shape, jnp.bfloat16), pltpu.SemaphoreType.DMA]
    if last:
        scratch += [pltpu.VMEM(queries.shape, queries.dtype), pltpu.SemaphoreType.DMA((pairs,))]
    outs = pl.pallas_call(
        functools.partial(
            attend_kernel, tuple(parts), len(pieces), store is not None, with_question,
            fresh is not None, first, last,
        ),
        out_shape=out_shape,
        in_specs=[smem_spec()] + [vmem_spec()] * (len(operands) - 1),
        out_specs=out_specs,
        scratch_shapes=scratch,
        compiler_params=pltpu.CompilerParams(vmem_limit_bytes=VMEM_LIMIT),
        cost_estimate=pl.CostEstimate(
            flops=64 * heads * question_len * length * HEAD_WIDTH, bytes_accessed=0, transcendentals=0
        ),
        name="attend_spans",
    )(*operands)
    rows = None
    if fresh is not None:
        *outs, rows = outs
    return outs, rows


def local(
    queries,
    question_kv,
    key_value_store,
    span_store_slot,
    retrieval,
    recompute_rows,
    recompute_hidden,
    kv_weight,
):
    n_store = lax.axis_size("store")
    n_tensor = lax.axis_size("tensor")
    slot_count, span_len, kv_cols = key_value_store.shape
    span_count = retrieval.shape[1]
    recomp = recompute_rows.shape[2]
    model_width = recompute_hidden.shape[3]
    shard_rows = span_count * recomp // n_tensor
    per_pair = max(1, span_count // n_store)
    fresh_rows = span_count * recomp
    hidden = recompute_hidden.reshape(fresh_rows, model_width)
    question = question_kv[0]
    query_rows = queries[0]

    def exchange(piece, distance, axis, content):
        size = lax.axis_size(axis)
        with jax.named_scope(content + str(distance)):
            return lax.ppermute(piece, axis, [(i, i ^ distance) for i in range(size)])

    shard = (shard_rows, model_width // n_store)

    def packed(messages, rows=None):
        return pack(
            span_store_slot, retrieval, key_value_store, hidden, rows, messages, shard,
            n_store * per_pair,
        )

    away = list(range(n_store - 1, 0, -1))
    half = span_len // 2

    def cuts(distance):
        if per_pair == 1:
            return [span_len]
        if distance == 1:
            return [2 * span_len + half, 0, 0, (per_pair - 3) * span_len + half]
        return [span_len] * (per_pair - 1) + [span_len - half // 2, half // 2]

    def pieces_of(first, length):
        pieces = []
        while length:
            span, start = divmod(first, span_len)
            rows = min(span_len - start, length)
            pieces.append((span, start, rows))
            first, length = first + rows, length - rows
        return pieces

    messages = {}
    for d in away:
        first = 0
        for number, length in enumerate(cuts(d)):
            if length:
                messages[d, number] = (d, not number, pieces_of(first, length))
            first += length
    outbox, _ = packed([messages[d, 0] for d in away])
    coming = [exchange(piece, d, "store", "spans0_") for piece, d in zip(outbox, away)]
    count = 1 + max(number for _, number in messages)
    later = [(d, number) for number in range(1, count) for d in away if (d, number) in messages]
    (hidden_own, *outbox), table = packed(
        [(0, True, [])] + [messages[key] for key in later], recompute_rows[0]
    )
    outbox = dict(zip(later, outbox))

    def behind(pieces, state):
        return [after(piece, state[0]) for piece in pieces]

    def block(keys, state, fresh=None, last=False):
        parts = []
        for source, (d, number) in enumerate(keys):
            offset = 0
            for span, start, rows in messages[d, number][2]:
                parts.append((d * per_pair + span, start, rows, source, offset))
                offset += rows
        if not keys:
            parts = [(span, 0, span_len, 0, 0) for span in range(per_pair)]
        return attend(
            table, query_rows, question, parts, [arrived[key] for key in keys],
            None if keys else key_value_store, fresh, state, not keys, last,
        )

    def recomputed():
        blocks = [hidden_own]
        for d in away[::-1]:
            piece = arrived[d, 0]
            blocks.append(piece[piece.shape[0] - hidden_own.shape[0] :])
        distances = [0]
        for step, bit in enumerate(reversed(range(n_tensor.bit_length() - 1))):
            distances += [distance ^ (1 << bit) for distance in distances]
            gathered = jnp.concatenate(blocks, axis=0)
            blocks = [gathered, exchange(gathered, 1 << bit, "tensor", "hidden")]
        partial, sent = project(blocks, kv_weight, n_store, shard_rows, distances)
        bits = n_store.bit_length() - 1
        for bit in range(bits):
            if bit:
                sent = partial[1::2].astype(jnp.bfloat16)
            yield sent
            other = exchange(sent, 1 << bit, "store", "partial")
            if bit + 1 < bits:
                partial = partial[0::2] + other.astype(jnp.float32)
        yield partial[0], other[0]

    arrived, fresh, rows = {}, None, None
    state, _ = block([], None)
    arrived.update(zip([(d, 0) for d in away], behind(coming, state)))
    steps = recomputed()
    turns = [(d, number) for number in range(count) for d in away if d > 1]

    def leave(key):
        piece, (d, number) = outbox[key], key
        turn = turns.index(key if d > 1 else (away[-2], number)) - WINDOW
        if d == 1:
            turn += 1
        if turn >= 0:
            piece = after(piece, arrived[turns[turn]])
        return exchange(piece, d, "store", "spans%d_" % number)

    for number in range(1, count):
        keys = [key for key in later if key[1] == number]
        coming = [leave(key) for key in keys]
        here = [(d, number - 1) for d in away if (d, number - 1) in arrived]
        if 2 <= number < n_store.bit_length() + 1:
            state = [after(state[0], next(steps)), *state[1:]]
        if number == count - 1:
            *_, fresh = steps
        state, rows = block(here, state, fresh)
        arrived.update(zip(keys, behind(coming, state)))

    keys = [(d, count - 1) for d in away[::-1] if (d, count - 1) in arrived]
    size = 6
    batches = [keys[i : i + size] for i in range(0, len(keys), size)]
    for i, keys in enumerate(batches):
        joins, last = rows is None, i == len(batches) - 1
        if joins:
            *_, fresh = steps
        state, now = block(keys, state, fresh if joins else None, last)
        rows = now if joins else rows
    return (state[0][None], rows.reshape(1, span_count, recomp, kv_cols))


def solution(mesh):
    in_specs = (
        P(("groups", "store"), None, "tensor"),
        P(("groups", "store"), None, "tensor"),
        P(("groups", "store"), None, "tensor"),
        P("groups"),
        P("groups", None),
        P(("groups", "store"), None, None),
        P(("groups", "store"), None, None, None),
        P("store", "tensor"),
    )
    out_specs = (
        P(("groups", "store"), None, "tensor"),
        P(("groups", "store"), None, None, "tensor"),
    )
    return jax.shard_map(local, mesh=mesh, in_specs=in_specs, out_specs=out_specs, check_vma=False)
```

```python
import functools
import math

import jax
import jax.numpy as jnp
from jax import lax
from jax.experimental import pallas as pl
from jax.experimental.pallas import tpu as pltpu
from jax.sharding import PartitionSpec as P

HEAD_WIDTH = 128
EXP_SCALE = math.log2(math.e) * HEAD_WIDTH ** (-0.5)
EXP_LIMIT = 64.0
PAIR = 2
WINDOW = 3
VMEM_LIMIT = 28 * 1024 * 1024
FIRST_VMEM_LIMIT = 60 * 1024 * 1024


def hbm_spec():
    return pl.BlockSpec(memory_space=pltpu.HBM)


def smem_spec():
    return pl.BlockSpec(memory_space=pltpu.SMEM)


def vmem_spec():
    return pl.BlockSpec(memory_space=pltpu.VMEM)


def after(array, *others):
    return lax.optimization_barrier((array,) + others)[0]


def pack_kernel(messages, shard, with_table, *refs):
    slot_ref, retrieval_ref, store_ref, hidden_ref = refs[:4]
    refs = refs[4:]
    if with_table:
        rows_ref, refs = refs[0], refs[1:]
    outs, refs = refs[: len(messages)], refs[len(messages) :]
    if with_table:
        table_ref, refs = refs[0], refs[1:]
    sems = refs[0]
    myself = lax.axis_index("store")
    tensor = lax.axis_index("tensor")
    slot_count, _, kv_cols = store_ref.shape
    span_count = retrieval_ref.shape[1]
    shard_rows, shard_width = shard
    copies = []

    def send(source, target):
        copy = pltpu.make_async_copy(source, target, sems.at[len(copies)])
        copy.start()
        copies.append(copy)

    for target, (distance, with_hidden, pieces) in zip(outs, messages):
        if with_hidden:
            base = sum(rows for _, _, rows in pieces)
            first_row = pl.multiple_of(tensor * shard_rows, shard_rows)
            for i in range(shard_width // kv_cols):
                column = pl.multiple_of((myself ^ distance) * shard_width + i * kv_cols, kv_cols)
                send(
                    hidden_ref.at[pl.ds(first_row, shard_rows), pl.ds(column, kv_cols)],
                    target.at[pl.ds(base + i * shard_rows, shard_rows)],
                )
    for distance in sorted({message[0] for message in messages}, reverse=True):
        wanted = []
        for target, message in zip(outs, messages):
            base = 0
            for span, start, rows in message[2] if message[0] == distance else ():
                wanted.append((span, pl.ds(start, rows), target.at[pl.ds(base, rows)]))
                base += rows
        if not wanted:
            continue
        count = jnp.int32(0)
        chosen = [jnp.int32(0) for _ in wanted]
        for j in range(span_count):
            home = slot_ref[retrieval_ref[myself ^ distance, j]]
            mine = home // slot_count == myself
            for i, (span, _, _) in enumerate(wanted):
                chosen[i] = jnp.where(mine & (count == span), home - myself * slot_count, chosen[i])
            count = count + jnp.where(mine, 1, 0)
        for slot, (_, rows, target) in zip(chosen, wanted):
            send(store_ref.at[slot, rows], target)
    if with_table:
        lines, columns = table_ref.shape
        per_pair = lines >> (lax.axis_size("store").bit_length() - 1)

        def clear(line, carry):
            for column in range(columns):
                table_ref[line, column] = 0
            return carry

        def fill(j, carry):
            home = slot_ref[retrieval_ref[myself, j]]
            owner = home // slot_count
            first = (owner ^ myself) * per_pair
            taken = jnp.int32(0)
            for span in range(per_pair):
                taken = taken + table_ref[first + span, 0]
            line = first + jnp.minimum(taken, per_pair - 1)
            table_ref[line, 0] = 1
            for column in range(rows_ref.shape[1]):
                table_ref[line, 1 + column] = rows_ref[j, column]
            table_ref[line, columns - 1] = home - owner * slot_count
            return carry

        lax.fori_loop(0, lines, clear, 0)
        lax.fori_loop(0, span_count, fill, 0)
    for copy in copies:
        copy.wait()


def pack(slots, retrieval, store, hidden, rows, messages, shard, lines):
    kv_cols = store.shape[2]
    with_table = rows is not None
    blocks = shard[1] // kv_cols
    shapes, n_copies = [], 0
    for _, with_hidden, pieces in messages:
        length = sum(rows for _, _, rows in pieces) + (blocks * shard[0] if with_hidden else 0)
        shapes.append(jax.ShapeDtypeStruct((length, kv_cols), store.dtype))
        n_copies += len(pieces) + (blocks if with_hidden else 0)
    specs = [vmem_spec()] * len(shapes)
    operands = [slots, retrieval, store, hidden]
    in_specs = [smem_spec()] * 2 + [hbm_spec()] * 2
    if with_table:
        operands.append(rows)
        in_specs.append(smem_spec())
        shapes.append(jax.ShapeDtypeStruct((lines, rows.shape[1] + 2), jnp.int32))
        specs.append(smem_spec())
    outs = pl.pallas_call(
        functools.partial(pack_kernel, messages, shard, with_table),
        out_shape=shapes,
        in_specs=in_specs,
        out_specs=specs,
        scratch_shapes=[pltpu.SemaphoreType.DMA((n_copies,))],
        compiler_params=pltpu.CompilerParams(vmem_limit_bytes=VMEM_LIMIT if with_table else FIRST_VMEM_LIMIT),
        cost_estimate=pl.CostEstimate(flops=0, bytes_accessed=0, transcendentals=0),
        name="pack_spans",
    )(*operands)
    return list(outs[: len(messages)]), outs[-1] if with_table else None


def project_kernel(shard_rows, distances, *refs):
    block_refs, (weight_ref, partial_ref, sent_ref) = refs[:-3], refs[-3:]
    n_store, group_rows, kv_cols = partial_ref.shape
    pieces = weight_ref.shape[0] // kv_cols
    total = 0.0
    for piece in range(pieces):
        rows = []
        for d in range(n_store):
            for ref in block_refs:
                length = n_store * pieces * shard_rows
                for base in range(0, ref.shape[0], length):
                    start = base + (d * pieces + piece) * shard_rows
                    rows.append(ref[start : start + shard_rows, :])
        total = total + jnp.dot(
            jnp.concatenate(rows, axis=0),
            weight_ref[piece * kv_cols : (piece + 1) * kv_cols, :],
            preferred_element_type=jnp.float32,
        )
    tensor = lax.axis_index("tensor")
    for d in range(n_store):
        for i, distance in enumerate(distances):
            base = d * group_rows + i * shard_rows
            block = total[base : base + shard_rows, :]
            row = pl.multiple_of((tensor ^ distance) * shard_rows, shard_rows)
            partial_ref[d, pl.ds(row, shard_rows), :] = block
            if d % 2:
                sent_ref[d // 2, pl.ds(row, shard_rows), :] = block.astype(sent_ref.dtype)


def project(blocks, weight, n_store, shard_rows, distances):
    group_rows = sum(block.shape[0] for block in blocks) * weight.shape[1]
    group_rows = group_rows // (n_store * weight.shape[0])
    kv_cols = weight.shape[1]
    return pl.pallas_call(
        functools.partial(project_kernel, shard_rows, tuple(distances)),
        out_shape=[
            jax.ShapeDtypeStruct((n_store, group_rows, kv_cols), jnp.float32),
            jax.ShapeDtypeStruct((n_store // 2, group_rows, kv_cols), jnp.bfloat16),
        ],
        in_specs=[vmem_spec()] * (len(blocks) + 1),
        out_specs=[vmem_spec()] * 2,
        compiler_params=pltpu.CompilerParams(vmem_limit_bytes=VMEM_LIMIT),
        cost_estimate=pl.CostEstimate(flops=0, bytes_accessed=0, transcendentals=0),
        name="project_rows",
    )(*blocks, weight)


def attend_kernel(parts, n_pieces, with_store, with_question, with_fresh, first, last, *refs):
    table_ref, query_ref, question_ref = refs[:3]
    refs = refs[3:]
    if with_store:
        store_ref, refs = refs[0], refs[1:]
    piece_refs, refs = refs[:n_pieces], refs[n_pieces:]
    if with_fresh:
        own_ref, other_ref = refs[:2]
        refs = refs[2:]
    if not first:
        blend_in, total_in, shift_in = refs[:3]
        refs = refs[3:]
    if last:
        out_ref, refs = refs[0], refs[1:]
    else:
        blend_out, total_out, shift_out = refs[:3]
        refs = refs[3:]
    if with_fresh:
        fresh_out, refs = refs[0], refs[1:]
    keys, values, live, refs = refs[0], refs[1], refs[2], refs[3:]
    if with_fresh:
        fresh_ref, fresh_sem, refs = refs[0], refs[1], refs[2:]
    if last:
        out_stage, sems = refs
    width = HEAD_WIDTH
    question_len, query_cols = query_ref.shape
    kv_heads = question_ref.shape[1] // (2 * width)
    group_cols = query_cols // kv_heads
    group_size = group_cols // width
    rows = PAIR * question_len
    pairs = group_size // PAIR
    contract = (((1,), (1,)), ((), ()))

    def out_copy(step, column):
        columns = pl.ds(column, PAIR * width)
        return pltpu.make_async_copy(out_stage.at[:, columns], out_ref.at[:, columns], sems.at[step])

    def fresh_copy():
        return pltpu.make_async_copy(fresh_ref, fresh_out, fresh_sem)

    if with_fresh:
        fresh_ref[...] = (own_ref[...] + other_ref[...].astype(jnp.float32)).astype(fresh_ref.dtype)
        fresh_copy().start()
    base = 0
    for line, start, length, _, _ in parts:
        row = start + lax.broadcasted_iota(jnp.int32, (length, width), 0)
        stale = row < jnp.where(table_ref[line, 0] == 0, start + length, 0)
        for column in range(1, table_ref.shape[1] - 1):
            stale = stale | (row == table_ref[line, column])
        live[base : base + length, :] = jnp.where(stale, 0.0, 1.0).astype(live.dtype)
        base += length
    values[:base, width:] = live[:base, :]
    if values.shape[0] > base:
        values[base:, width:] = jnp.ones((values.shape[0] - base, width), values.dtype)
    plain = values.shape[0] - (question_len if with_question else 0)

    def load(k):
        key_at = pl.ds(pl.multiple_of(k * 2 * width, 2 * width), width)
        value_at = pl.ds(pl.multiple_of(k * 2 * width + width, width), width)
        spare_key = question_ref[0:8, key_at][0:1].astype(jnp.float32)
        base = 0
        for line, start, length, source, offset in parts:
            here = slice(base, base + length)
            if with_store:
                slot = table_ref[line, table_ref.shape[1] - 1]
                key, value = store_ref[slot, :, key_at], store_ref[slot, :, value_at]
            else:
                at = slice(offset, offset + length)
                key, value = piece_refs[source][at, key_at], piece_refs[source][at, value_at]
            read = live[here, :].astype(jnp.float32) > 0.5
            keys[here, :] = jnp.where(read, key.astype(jnp.float32), spare_key).astype(keys.dtype)
            values[here, :width] = jnp.where(read, value.astype(jnp.float32), 0.0).astype(values.dtype)
            base += length
        for ref in ([fresh_ref] if with_fresh else []) + ([question_ref] if with_question else []):
            here = slice(base, base + ref.shape[0])
            keys[here, :] = ref[:, key_at]
            values[here, :width] = ref[:, value_at]
            base += ref.shape[0]

    def query_columns(k, start):
        return pl.ds(pl.multiple_of(k * group_cols + start * width, width), width)

    def score(k, pair):
        query = jnp.concatenate(
            [query_ref[:, query_columns(k, pair * PAIR + h)] for h in range(PAIR)], axis=0
        )
        scores = [
            lax.dot_general(query, keys[:plain, :], contract, preferred_element_type=jnp.float32)
        ]
        if with_question:
            asked = lax.dot_general(
                query, keys[plain:, :], contract, preferred_element_type=jnp.float32
            )
            asked = asked.reshape(PAIR, question_len, question_len)
            q_place = lax.broadcasted_iota(jnp.int32, asked.shape, 1)
            k_place = lax.broadcasted_iota(jnp.int32, asked.shape, 2)
            asked = jnp.where(k_place <= q_place, asked, -jnp.inf)
            scores.append(asked.reshape(rows, question_len))
        return scores

    def over(scores, shift):
        return [
            part - jnp.concatenate([shift] * (part.shape[1] // width), axis=1) for part in scores
        ]

    def blended(apart):
        blend, offset = 0.0, 0
        for part in apart:
            probs = jnp.exp2(part * EXP_SCALE).astype(jnp.bfloat16)
            blend = blend + jnp.dot(
                probs, values[offset : offset + part.shape[1], :], preferred_element_type=jnp.float32
            )
            offset += part.shape[1]
        return blend[:, :width], blend[:, width:]

    def new_shift(scores):
        highest = functools.reduce(
            jnp.maximum, [jnp.max(part, axis=1, keepdims=True) for part in scores]
        )
        return jnp.broadcast_to(highest, (rows, width))

    def finish(k, pair, here, blend, total, shift):
        if last:
            done = (blend / total).astype(out_ref.dtype)
            for h in range(PAIR):
                out_stage[:, query_columns(k, pair * PAIR + h)] = done[
                    h * question_len : (h + 1) * question_len
                ]
            column = pl.multiple_of(k * group_cols + pair * PAIR * width, PAIR * width)
            out_copy(k * pairs + pair, column).start()
        else:
            blend_out[here, :] = blend
            total_out[here, :] = total
            shift_out[here, :] = shift

    def wait_out():
        for step in range(kv_heads * pairs if last else 0):
            out_copy(step, step * PAIR * width).wait()

    def one_kv_head(k, worst):
        load(k)
        upcoming = score(k, 0)
        for pair in range(pairs):
            scores = upcoming
            if pair + 1 < pairs:
                upcoming = score(k, pair + 1)
            here = pl.ds(pl.multiple_of((k * pairs + pair) * rows, rows), rows)
            shift = new_shift(scores) if first else shift_in[here, :]
            apart = over(scores, shift)
            blend, total = blended(apart)
            if not first:
                for part in apart:
                    most = jnp.max(part.reshape(rows // 8, 8, part.shape[1]), axis=0)
                    for column in range(0, part.shape[1], width):
                        worst = jnp.maximum(worst, most[:, column : column + width])
                blend = blend + blend_in[here, :]
                total = total + total_in[here, :]
            finish(k, pair, here, blend, total, shift)
        return worst

    worst = lax.fori_loop(0, kv_heads, one_kv_head, jnp.full((8, width), -jnp.inf, jnp.float32))
    wait_out()

    def again(k, carry):
        load(k)

        def one_pair(pair, carry):
            here = pl.ds(pl.multiple_of((k * pairs + pair) * rows, rows), rows)
            scores = score(k, pair)
            before = shift_in[here, :]
            shift = jnp.maximum(new_shift(scores), before)
            fade = jnp.exp2((before - shift) * EXP_SCALE)
            blend, total = blended(over(scores, shift))
            blend = blend + blend_in[here, :] * fade
            total = total + total_in[here, :] * fade
            finish(k, pair, here, blend, total, shift)
            return carry

        return lax.fori_loop(0, pairs, one_pair, carry)

    if not first:

        @pl.when(jnp.max(worst) * EXP_SCALE > EXP_LIMIT)
        def _():
            lax.fori_loop(0, kv_heads, again, 0)
            wait_out()

    if with_fresh:
        fresh_copy().wait()


def attend(table, queries, question, parts, pieces, store, fresh, state, with_question, last):
    question_len, query_cols = queries.shape
    heads = query_cols // HEAD_WIDTH
    pairs = heads // PAIR
    first = state is None
    operands = [table, queries, question] + ([store] if store is not None else []) + list(pieces)
    held = sum(part[2] for part in parts)
    length = held + (question_len if with_question else 0)
    if fresh is not None:
        operands += list(fresh)
        length += fresh[0].shape[0]
    if not first:
        operands += list(state)
    scratch = [
        pltpu.VMEM((length, HEAD_WIDTH), jnp.bfloat16),
        pltpu.VMEM((length, 2 * HEAD_WIDTH), jnp.bfloat16),
        pltpu.VMEM((held, HEAD_WIDTH), jnp.bfloat16),
    ]
    if last:
        out_shape = [jax.ShapeDtypeStruct(queries.shape, queries.dtype)]
        out_specs = [hbm_spec()]
    else:
        out_shape = [jax.ShapeDtypeStruct((heads * question_len, HEAD_WIDTH), jnp.float32)] * 3
        out_specs = [vmem_spec()] * 3
    if fresh is not None:
        out_shape.append(jax.ShapeDtypeStruct(fresh[0].shape, jnp.bfloat16))
        out_specs.append(hbm_spec())
        scratch += [pltpu.VMEM(fresh[0].shape, jnp.bfloat16), pltpu.SemaphoreType.DMA]
    if last:
        scratch += [pltpu.VMEM(queries.shape, queries.dtype), pltpu.SemaphoreType.DMA((pairs,))]
    outs = pl.pallas_call(
        functools.partial(
            attend_kernel, tuple(parts), len(pieces), store is not None, with_question,
            fresh is not None, first, last,
        ),
        out_shape=out_shape,
        in_specs=[smem_spec()] + [vmem_spec()] * (len(operands) - 1),
        out_specs=out_specs,
        scratch_shapes=scratch,
        compiler_params=pltpu.CompilerParams(vmem_limit_bytes=VMEM_LIMIT),
        cost_estimate=pl.CostEstimate(
            flops=64 * heads * question_len * length * HEAD_WIDTH, bytes_accessed=0, transcendentals=0
        ),
        name="attend_spans",
    )(*operands)
    rows = None
    if fresh is not None:
        *outs, rows = outs
    return outs, rows


def local(
    queries,
    question_kv,
    key_value_store,
    span_store_slot,
    retrieval,
    recompute_rows,
    recompute_hidden,
    kv_weight,
):
    n_store = lax.axis_size("store")
    n_tensor = lax.axis_size("tensor")
    slot_count, span_len, kv_cols = key_value_store.shape
    span_count = retrieval.shape[1]
    recomp = recompute_rows.shape[2]
    model_width = recompute_hidden.shape[3]
    shard_rows = span_count * recomp // n_tensor
    per_pair = max(1, span_count // n_store)
    fresh_rows = span_count * recomp
    hidden = recompute_hidden.reshape(fresh_rows, model_width)
    question = question_kv[0]
    query_rows = queries[0]

    def exchange(piece, distance, axis, content):
        size = lax.axis_size(axis)
        with jax.named_scope(content + str(distance)):
            return lax.ppermute(piece, axis, [(i, i ^ distance) for i in range(size)])

    shard = (shard_rows, model_width // n_store)

    def packed(messages, rows=None):
        return pack(
            span_store_slot, retrieval, key_value_store, hidden, rows, messages, shard,
            n_store * per_pair,
        )

    away = list(range(n_store - 1, 0, -1))
    half = span_len // 2

    def cuts(distance):
        if per_pair == 1:
            return [span_len]
        if distance == 1:
            return [2 * span_len, (per_pair - 2) * span_len]
        return [span_len] * (per_pair - 1) + [span_len - half // 2, half // 2]

    def pieces_of(first, length):
        pieces = []
        while length:
            span, start = divmod(first, span_len)
            rows = min(span_len - start, length)
            pieces.append((span, start, rows))
            first, length = first + rows, length - rows
        return pieces

    messages = {}
    for d in away:
        first = 0
        for number, length in enumerate(cuts(d)):
            if length:
                messages[d, number] = (d, not number, pieces_of(first, length))
            first += length
    outbox, _ = packed([messages[d, 0] for d in away])
    coming = [exchange(piece, d, "store", "spans0_") for piece, d in zip(outbox, away)]
    count = 1 + max(number for _, number in messages)
    later = [(d, number) for number in range(1, count) for d in away if (d, number) in messages]
    (hidden_own, *outbox), table = packed(
        [(0, True, [])] + [messages[key] for key in later], recompute_rows[0]
    )
    outbox = dict(zip(later, outbox))

    def behind(pieces, state):
        return [after(piece, state[0]) for piece in pieces]

    def block(keys, state, fresh=None, last=False):
        parts = []
        for source, (d, number) in enumerate(keys):
            offset = 0
            for span, start, rows in messages[d, number][2]:
                parts.append((d * per_pair + span, start, rows, source, offset))
                offset += rows
        if not keys:
            parts = [(span, 0, span_len, 0, 0) for span in range(per_pair)]
        return attend(
            table, query_rows, question, parts, [arrived[key] for key in keys],
            None if keys else key_value_store, fresh, state, not keys, last,
        )

    def recomputed():
        blocks = [hidden_own]
        for d in away[::-1]:
            piece = arrived[d, 0]
            blocks.append(piece[piece.shape[0] - hidden_own.shape[0] :])
        distances = [0]
        for step, bit in enumerate(reversed(range(n_tensor.bit_length() - 1))):
            distances += [distance ^ (1 << bit) for distance in distances]
            gathered = jnp.concatenate(blocks, axis=0)
            blocks = [gathered, exchange(gathered, 1 << bit, "tensor", "hidden")]
        partial, sent = project(blocks, kv_weight, n_store, shard_rows, distances)
        bits = n_store.bit_length() - 1
        for bit in range(bits):
            if bit:
                sent = partial[1::2].astype(jnp.bfloat16)
            yield sent
            other = exchange(sent, 1 << bit, "store", "partial")
            if bit + 1 < bits:
                partial = partial[0::2] + other.astype(jnp.float32)
        yield partial[0], other[0]

    arrived, fresh, rows = {}, None, None
    state, _ = block([], None)
    arrived.update(zip([(d, 0) for d in away], behind(coming, state)))
    steps = recomputed()
    turns = [(d, number) for number in range(count) for d in away if d > 1]

    def leave(key):
        piece, (d, number) = outbox[key], key
        if d == 1:
            before = (away[0], number - 1)
        else:
            turn = turns.index(key) - WINDOW
            before = turns[turn] if turn >= 0 else None
        if before in arrived:
            piece = after(piece, arrived[before])
        return exchange(piece, d, "store", "spans%d_" % number)

    for number in range(1, count):
        keys = [key for key in later if key[1] == number]
        coming = [leave(key) for key in keys]
        here = [(d, number - 1) for d in away if (d, number - 1) in arrived]
        if number == 2:
            state, _ = block([key for key in here if key[0] > 1], state)
            here = [key for key in here if key[0] == 1]
        if 2 <= number < n_store.bit_length() + 1:
            state = [after(state[0], next(steps)), *state[1:]]
        if number == count - 1:
            *_, fresh = steps
        state, rows = block(here, state, fresh)
        arrived.update(zip(keys, behind(coming, state)))

    keys = [(d, count - 1) for d in away[::-1] if (d, count - 1) in arrived]
    size = 6
    batches = [keys[i : i + size] for i in range(0, len(keys), size)]
    for i, keys in enumerate(batches):
        joins, last = rows is None, i == len(batches) - 1
        if joins:
            *_, fresh = steps
        state, now = block(keys, state, fresh if joins else None, last)
        rows = now if joins else rows
    return (state[0][None], rows.reshape(1, span_count, recomp, kv_cols))


def solution(mesh):
    in_specs = (
        P(("groups", "store"), None, "tensor"),
        P(("groups", "store"), None, "tensor"),
        P(("groups", "store"), None, "tensor"),
        P("groups"),
        P("groups", None),
        P(("groups", "store"), None, None),
        P(("groups", "store"), None, None, None),
        P("store", "tensor"),
    )
    out_specs = (
        P(("groups", "store"), None, "tensor"),
        P(("groups", "store"), None, None, "tensor"),
    )
    return jax.shard_map(local, mesh=mesh, in_specs=in_specs, out_specs=out_specs, check_vma=False)
```

```python
import functools
import math

import jax
import jax.numpy as jnp
from jax import lax
from jax.experimental import pallas as pl
from jax.experimental.pallas import tpu as pltpu
from jax.sharding import PartitionSpec as P

HEAD_WIDTH = 128
EXP_SCALE = math.log2(math.e) * HEAD_WIDTH ** (-0.5)
EXP_LIMIT = 64.0
PAIR = 2
WINDOW = 3
VMEM_LIMIT = 28 * 1024 * 1024
FIRST_VMEM_LIMIT = 60 * 1024 * 1024


def hbm_spec():
    return pl.BlockSpec(memory_space=pltpu.HBM)


def smem_spec():
    return pl.BlockSpec(memory_space=pltpu.SMEM)


def vmem_spec():
    return pl.BlockSpec(memory_space=pltpu.VMEM)


def after(array, *others):
    return lax.optimization_barrier((array,) + others)[0]


def pack_kernel(messages, shard, with_table, *refs):
    slot_ref, retrieval_ref, store_ref, hidden_ref = refs[:4]
    refs = refs[4:]
    if with_table:
        rows_ref, refs = refs[0], refs[1:]
    outs, refs = refs[: len(messages)], refs[len(messages) :]
    if with_table:
        table_ref, refs = refs[0], refs[1:]
    sems = refs[0]
    myself = lax.axis_index("store")
    tensor = lax.axis_index("tensor")
    slot_count, _, kv_cols = store_ref.shape
    span_count = retrieval_ref.shape[1]
    shard_rows, shard_width = shard
    copies = []

    def send(source, target):
        copy = pltpu.make_async_copy(source, target, sems.at[len(copies)])
        copy.start()
        copies.append(copy)

    for target, (distance, with_hidden, pieces) in zip(outs, messages):
        if with_hidden:
            base = sum(rows for _, _, rows in pieces)
            first_row = pl.multiple_of(tensor * shard_rows, shard_rows)
            for i in range(shard_width // kv_cols):
                column = pl.multiple_of((myself ^ distance) * shard_width + i * kv_cols, kv_cols)
                send(
                    hidden_ref.at[pl.ds(first_row, shard_rows), pl.ds(column, kv_cols)],
                    target.at[pl.ds(base + i * shard_rows, shard_rows)],
                )
    for distance in sorted({message[0] for message in messages}, reverse=True):
        wanted = []
        for target, message in zip(outs, messages):
            base = 0
            for span, start, rows in message[2] if message[0] == distance else ():
                wanted.append((span, pl.ds(start, rows), target.at[pl.ds(base, rows)]))
                base += rows
        if not wanted:
            continue
        count = jnp.int32(0)
        chosen = [jnp.int32(0) for _ in wanted]
        for j in range(span_count):
            home = slot_ref[retrieval_ref[myself ^ distance, j]]
            mine = home // slot_count == myself
            for i, (span, _, _) in enumerate(wanted):
                chosen[i] = jnp.where(mine & (count == span), home - myself * slot_count, chosen[i])
            count = count + jnp.where(mine, 1, 0)
        for slot, (_, rows, target) in zip(chosen, wanted):
            send(store_ref.at[slot, rows], target)
    if with_table:
        lines, columns = table_ref.shape
        per_pair = lines >> (lax.axis_size("store").bit_length() - 1)

        def clear(line, carry):
            for column in range(columns):
                table_ref[line, column] = 0
            return carry

        def fill(j, carry):
            home = slot_ref[retrieval_ref[myself, j]]
            owner = home // slot_count
            first = (owner ^ myself) * per_pair
            taken = jnp.int32(0)
            for span in range(per_pair):
                taken = taken + table_ref[first + span, 0]
            line = first + jnp.minimum(taken, per_pair - 1)
            table_ref[line, 0] = 1
            for column in range(rows_ref.shape[1]):
                table_ref[line, 1 + column] = rows_ref[j, column]
            table_ref[line, columns - 1] = home - owner * slot_count
            return carry

        lax.fori_loop(0, lines, clear, 0)
        lax.fori_loop(0, span_count, fill, 0)
    for copy in copies:
        copy.wait()


def pack(slots, retrieval, store, hidden, rows, messages, shard, lines):
    kv_cols = store.shape[2]
    with_table = rows is not None
    blocks = shard[1] // kv_cols
    shapes, n_copies = [], 0
    for _, with_hidden, pieces in messages:
        length = sum(rows for _, _, rows in pieces) + (blocks * shard[0] if with_hidden else 0)
        shapes.append(jax.ShapeDtypeStruct((length, kv_cols), store.dtype))
        n_copies += len(pieces) + (blocks if with_hidden else 0)
    specs = [vmem_spec()] * len(shapes)
    operands = [slots, retrieval, store, hidden]
    in_specs = [smem_spec()] * 2 + [hbm_spec()] * 2
    if with_table:
        operands.append(rows)
        in_specs.append(smem_spec())
        shapes.append(jax.ShapeDtypeStruct((lines, rows.shape[1] + 2), jnp.int32))
        specs.append(smem_spec())
    outs = pl.pallas_call(
        functools.partial(pack_kernel, messages, shard, with_table),
        out_shape=shapes,
        in_specs=in_specs,
        out_specs=specs,
        scratch_shapes=[pltpu.SemaphoreType.DMA((n_copies,))],
        compiler_params=pltpu.CompilerParams(vmem_limit_bytes=VMEM_LIMIT if with_table else FIRST_VMEM_LIMIT),
        cost_estimate=pl.CostEstimate(flops=0, bytes_accessed=0, transcendentals=0),
        name="pack_spans",
    )(*operands)
    return list(outs[: len(messages)]), outs[-1] if with_table else None


def project_kernel(shard_rows, distances, *refs):
    block_refs, (weight_ref, partial_ref, sent_ref) = refs[:-3], refs[-3:]
    n_store, group_rows, kv_cols = partial_ref.shape
    pieces = weight_ref.shape[0] // kv_cols
    total = 0.0
    for piece in range(pieces):
        rows = []
        for d in range(n_store):
            for ref in block_refs:
                length = n_store * pieces * shard_rows
                for base in range(0, ref.shape[0], length):
                    start = base + (d * pieces + piece) * shard_rows
                    rows.append(ref[start : start + shard_rows, :])
        total = total + jnp.dot(
            jnp.concatenate(rows, axis=0),
            weight_ref[piece * kv_cols : (piece + 1) * kv_cols, :],
            preferred_element_type=jnp.float32,
        )
    tensor = lax.axis_index("tensor")
    for d in range(n_store):
        for i, distance in enumerate(distances):
            base = d * group_rows + i * shard_rows
            block = total[base : base + shard_rows, :]
            row = pl.multiple_of((tensor ^ distance) * shard_rows, shard_rows)
            partial_ref[d, pl.ds(row, shard_rows), :] = block
            if d % 2:
                sent_ref[d // 2, pl.ds(row, shard_rows), :] = block.astype(sent_ref.dtype)


def project(blocks, weight, n_store, shard_rows, distances):
    group_rows = sum(block.shape[0] for block in blocks) * weight.shape[1]
    group_rows = group_rows // (n_store * weight.shape[0])
    kv_cols = weight.shape[1]
    return pl.pallas_call(
        functools.partial(project_kernel, shard_rows, tuple(distances)),
        out_shape=[
            jax.ShapeDtypeStruct((n_store, group_rows, kv_cols), jnp.float32),
            jax.ShapeDtypeStruct((n_store // 2, group_rows, kv_cols), jnp.bfloat16),
        ],
        in_specs=[vmem_spec()] * (len(blocks) + 1),
        out_specs=[vmem_spec()] * 2,
        compiler_params=pltpu.CompilerParams(vmem_limit_bytes=VMEM_LIMIT),
        cost_estimate=pl.CostEstimate(flops=0, bytes_accessed=0, transcendentals=0),
        name="project_rows",
    )(*blocks, weight)


def attend_kernel(parts, n_pieces, with_store, with_question, with_fresh, first, last, *refs):
    table_ref, query_ref, question_ref = refs[:3]
    refs = refs[3:]
    if with_store:
        store_ref, refs = refs[0], refs[1:]
    piece_refs, refs = refs[:n_pieces], refs[n_pieces:]
    if with_fresh:
        own_ref, other_ref = refs[:2]
        refs = refs[2:]
    if not first:
        blend_in, total_in, shift_in = refs[:3]
        refs = refs[3:]
    if last:
        out_ref, refs = refs[0], refs[1:]
    else:
        blend_out, total_out, shift_out = refs[:3]
        refs = refs[3:]
    if with_fresh:
        fresh_out, refs = refs[0], refs[1:]
    keys, values, live, refs = refs[0], refs[1], refs[2], refs[3:]
    if with_fresh:
        fresh_ref, fresh_sem, refs = refs[0], refs[1], refs[2:]
    if last:
        out_stage, sems = refs
    width = HEAD_WIDTH
    question_len, query_cols = query_ref.shape
    kv_heads = question_ref.shape[1] // (2 * width)
    group_cols = query_cols // kv_heads
    group_size = group_cols // width
    rows = PAIR * question_len
    pairs = group_size // PAIR
    contract = (((1,), (1,)), ((), ()))

    def out_copy(step, column):
        columns = pl.ds(column, PAIR * width)
        return pltpu.make_async_copy(out_stage.at[:, columns], out_ref.at[:, columns], sems.at[step])

    def fresh_copy():
        return pltpu.make_async_copy(fresh_ref, fresh_out, fresh_sem)

    if with_fresh:
        fresh_ref[...] = (own_ref[...] + other_ref[...].astype(jnp.float32)).astype(fresh_ref.dtype)
        fresh_copy().start()
    base = 0
    for line, start, length, _, _ in parts:
        row = start + lax.broadcasted_iota(jnp.int32, (length, width), 0)
        stale = row < jnp.where(table_ref[line, 0] == 0, start + length, 0)
        for column in range(1, table_ref.shape[1] - 1):
            stale = stale | (row == table_ref[line, column])
        live[base : base + length, :] = jnp.where(stale, 0.0, 1.0).astype(live.dtype)
        base += length
    values[:base, width:] = live[:base, :]
    if values.shape[0] > base:
        values[base:, width:] = jnp.ones((values.shape[0] - base, width), values.dtype)
    plain = values.shape[0] - (question_len if with_question else 0)

    def load(k):
        key_at = pl.ds(pl.multiple_of(k * 2 * width, 2 * width), width)
        value_at = pl.ds(pl.multiple_of(k * 2 * width + width, width), width)
        spare_key = question_ref[0:8, key_at][0:1].astype(jnp.float32)
        base = 0
        for line, start, length, source, offset in parts:
            here = slice(base, base + length)
            if with_store:
                slot = table_ref[line, table_ref.shape[1] - 1]
                key, value = store_ref[slot, :, key_at], store_ref[slot, :, value_at]
            else:
                at = slice(offset, offset + length)
                key, value = piece_refs[source][at, key_at], piece_refs[source][at, value_at]
            read = live[here, :].astype(jnp.float32) > 0.5
            keys[here, :] = jnp.where(read, key.astype(jnp.float32), spare_key).astype(keys.dtype)
            values[here, :width] = jnp.where(read, value.astype(jnp.float32), 0.0).astype(values.dtype)
            base += length
        for ref in ([fresh_ref] if with_fresh else []) + ([question_ref] if with_question else []):
            here = slice(base, base + ref.shape[0])
            keys[here, :] = ref[:, key_at]
            values[here, :width] = ref[:, value_at]
            base += ref.shape[0]

    def query_columns(k, start):
        return pl.ds(pl.multiple_of(k * group_cols + start * width, width), width)

    def score(k, pair):
        query = jnp.concatenate(
            [query_ref[:, query_columns(k, pair * PAIR + h)] for h in range(PAIR)], axis=0
        )
        scores = [
            lax.dot_general(query, keys[:plain, :], contract, preferred_element_type=jnp.float32)
        ]
        if with_question:
            asked = lax.dot_general(
                query, keys[plain:, :], contract, preferred_element_type=jnp.float32
            )
            asked = asked.reshape(PAIR, question_len, question_len)
            q_place = lax.broadcasted_iota(jnp.int32, asked.shape, 1)
            k_place = lax.broadcasted_iota(jnp.int32, asked.shape, 2)
            asked = jnp.where(k_place <= q_place, asked, -jnp.inf)
            scores.append(asked.reshape(rows, question_len))
        return scores

    def over(scores, shift):
        return [
            part - jnp.concatenate([shift] * (part.shape[1] // width), axis=1) for part in scores
        ]

    def blended(apart):
        blend, offset = 0.0, 0
        for part in apart:
            probs = jnp.exp2(part * EXP_SCALE).astype(jnp.bfloat16)
            blend = blend + jnp.dot(
                probs, values[offset : offset + part.shape[1], :], preferred_element_type=jnp.float32
            )
            offset += part.shape[1]
        return blend[:, :width], blend[:, width:]

    def new_shift(scores):
        highest = functools.reduce(
            jnp.maximum, [jnp.max(part, axis=1, keepdims=True) for part in scores]
        )
        return jnp.broadcast_to(highest, (rows, width))

    def finish(k, pair, here, blend, total, shift):
        if last:
            done = (blend / total).astype(out_ref.dtype)
            for h in range(PAIR):
                out_stage[:, query_columns(k, pair * PAIR + h)] = done[
                    h * question_len : (h + 1) * question_len
                ]
            column = pl.multiple_of(k * group_cols + pair * PAIR * width, PAIR * width)
            out_copy(k * pairs + pair, column).start()
        else:
            blend_out[here, :] = blend
            total_out[here, :] = total
            shift_out[here, :] = shift

    def wait_out():
        for step in range(kv_heads * pairs if last else 0):
            out_copy(step, step * PAIR * width).wait()

    def one_kv_head(k, worst):
        load(k)
        upcoming = score(k, 0)
        for pair in range(pairs):
            scores = upcoming
            if pair + 1 < pairs:
                upcoming = score(k, pair + 1)
            here = pl.ds(pl.multiple_of((k * pairs + pair) * rows, rows), rows)
            shift = new_shift(scores) if first else shift_in[here, :]
            apart = over(scores, shift)
            blend, total = blended(apart)
            if not first:
                for part in apart:
                    most = jnp.max(part.reshape(rows // 8, 8, part.shape[1]), axis=0)
                    for column in range(0, part.shape[1], width):
                        worst = jnp.maximum(worst, most[:, column : column + width])
                blend = blend + blend_in[here, :]
                total = total + total_in[here, :]
            finish(k, pair, here, blend, total, shift)
        return worst

    worst = lax.fori_loop(0, kv_heads, one_kv_head, jnp.full((8, width), -jnp.inf, jnp.float32))
    wait_out()

    def again(k, carry):
        load(k)

        def one_pair(pair, carry):
            here = pl.ds(pl.multiple_of((k * pairs + pair) * rows, rows), rows)
            scores = score(k, pair)
            before = shift_in[here, :]
            shift = jnp.maximum(new_shift(scores), before)
            fade = jnp.exp2((before - shift) * EXP_SCALE)
            blend, total = blended(over(scores, shift))
            blend = blend + blend_in[here, :] * fade
            total = total + total_in[here, :] * fade
            finish(k, pair, here, blend, total, shift)
            return carry

        return lax.fori_loop(0, pairs, one_pair, carry)

    if not first:

        @pl.when(jnp.max(worst) * EXP_SCALE > EXP_LIMIT)
        def _():
            lax.fori_loop(0, kv_heads, again, 0)
            wait_out()

    if with_fresh:
        fresh_copy().wait()


def attend(table, queries, question, parts, pieces, store, fresh, state, with_question, last):
    question_len, query_cols = queries.shape
    heads = query_cols // HEAD_WIDTH
    pairs = heads // PAIR
    first = state is None
    operands = [table, queries, question] + ([store] if store is not None else []) + list(pieces)
    held = sum(part[2] for part in parts)
    length = held + (question_len if with_question else 0)
    if fresh is not None:
        operands += list(fresh)
        length += fresh[0].shape[0]
    if not first:
        operands += list(state)
    scratch = [
        pltpu.VMEM((length, HEAD_WIDTH), jnp.bfloat16),
        pltpu.VMEM((length, 2 * HEAD_WIDTH), jnp.bfloat16),
        pltpu.VMEM((held, HEAD_WIDTH), jnp.bfloat16),
    ]
    if last:
        out_shape = [jax.ShapeDtypeStruct(queries.shape, queries.dtype)]
        out_specs = [hbm_spec()]
    else:
        out_shape = [jax.ShapeDtypeStruct((heads * question_len, HEAD_WIDTH), jnp.float32)] * 3
        out_specs = [vmem_spec()] * 3
    if fresh is not None:
        out_shape.append(jax.ShapeDtypeStruct(fresh[0].shape, jnp.bfloat16))
        out_specs.append(hbm_spec())
        scratch += [pltpu.VMEM(fresh[0].shape, jnp.bfloat16), pltpu.SemaphoreType.DMA]
    if last:
        scratch += [pltpu.VMEM(queries.shape, queries.dtype), pltpu.SemaphoreType.DMA((pairs,))]
    outs = pl.pallas_call(
        functools.partial(
            attend_kernel, tuple(parts), len(pieces), store is not None, with_question,
            fresh is not None, first, last,
        ),
        out_shape=out_shape,
        in_specs=[smem_spec()] + [vmem_spec()] * (len(operands) - 1),
        out_specs=out_specs,
        scratch_shapes=scratch,
        compiler_params=pltpu.CompilerParams(vmem_limit_bytes=VMEM_LIMIT),
        cost_estimate=pl.CostEstimate(
            flops=64 * heads * question_len * length * HEAD_WIDTH, bytes_accessed=0, transcendentals=0
        ),
        name="attend_spans",
    )(*operands)
    rows = None
    if fresh is not None:
        *outs, rows = outs
    return outs, rows


def local(
    queries,
    question_kv,
    key_value_store,
    span_store_slot,
    retrieval,
    recompute_rows,
    recompute_hidden,
    kv_weight,
):
    n_store = lax.axis_size("store")
    n_tensor = lax.axis_size("tensor")
    slot_count, span_len, kv_cols = key_value_store.shape
    span_count = retrieval.shape[1]
    recomp = recompute_rows.shape[2]
    model_width = recompute_hidden.shape[3]
    shard_rows = span_count * recomp // n_tensor
    per_pair = max(1, span_count // n_store)
    fresh_rows = span_count * recomp
    hidden = recompute_hidden.reshape(fresh_rows, model_width)
    question = question_kv[0]
    query_rows = queries[0]

    def exchange(piece, distance, axis, content):
        size = lax.axis_size(axis)
        with jax.named_scope(content + str(distance)):
            return lax.ppermute(piece, axis, [(i, i ^ distance) for i in range(size)])

    shard = (shard_rows, model_width // n_store)

    def packed(messages, rows=None):
        return pack(
            span_store_slot, retrieval, key_value_store, hidden, rows, messages, shard,
            n_store * per_pair,
        )

    away = list(range(n_store - 1, 0, -1))
    half = span_len // 2

    def cuts(distance):
        if per_pair == 1:
            return [span_len]
        if distance == 1:
            return [2 * span_len, (per_pair - 2) * span_len]
        return [span_len] * (per_pair - 1) + [span_len - half // 2, half // 2]

    def pieces_of(first, length):
        pieces = []
        while length:
            span, start = divmod(first, span_len)
            rows = min(span_len - start, length)
            pieces.append((span, start, rows))
            first, length = first + rows, length - rows
        return pieces

    messages = {}
    for d in away:
        first = 0
        for number, length in enumerate(cuts(d)):
            if length:
                messages[d, number] = (d, not number, pieces_of(first, length))
            first += length
    outbox, _ = packed([messages[d, 0] for d in away])
    coming = [exchange(piece, d, "store", "spans0_") for piece, d in zip(outbox, away)]
    count = 1 + max(number for _, number in messages)
    later = [(d, number) for number in range(1, count) for d in away if (d, number) in messages]
    (hidden_own, *outbox), table = packed(
        [(0, True, [])] + [messages[key] for key in later], recompute_rows[0]
    )
    outbox = dict(zip(later, outbox))

    def behind(pieces, state):
        return [after(piece, state[0]) for piece in pieces]

    def block(keys, state, fresh=None, last=False):
        parts = []
        for source, (d, number) in enumerate(keys):
            offset = 0
            for span, start, rows in messages[d, number][2]:
                parts.append((d * per_pair + span, start, rows, source, offset))
                offset += rows
        if not keys:
            parts = [(span, 0, span_len, 0, 0) for span in range(per_pair)]
        return attend(
            table, query_rows, question, parts, [arrived[key] for key in keys],
            None if keys else key_value_store, fresh, state, not keys, last,
        )

    def recomputed():
        blocks = [hidden_own]
        for d in away[::-1]:
            piece = arrived[d, 0]
            blocks.append(piece[piece.shape[0] - hidden_own.shape[0] :])
        distances = [0]
        for step, bit in enumerate(reversed(range(n_tensor.bit_length() - 1))):
            distances += [distance ^ (1 << bit) for distance in distances]
            gathered = jnp.concatenate(blocks, axis=0)
            blocks = [gathered, exchange(gathered, 1 << bit, "tensor", "hidden")]
        partial, sent = project(blocks, kv_weight, n_store, shard_rows, distances)
        bits = n_store.bit_length() - 1
        for bit in range(bits):
            if bit:
                sent = partial[1::2].astype(jnp.bfloat16)
            yield sent
            other = exchange(sent, 1 << bit, "store", "partial")
            if bit + 1 < bits:
                partial = partial[0::2] + other.astype(jnp.float32)
        yield partial[0], other[0]

    arrived = {}
    state, _ = block([], None)
    arrived.update(zip([(d, 0) for d in away], behind(coming, state)))
    steps = recomputed()
    turns = [(d, number) for number in range(count) for d in away if d > 1]

    def leave(key):
        piece, (d, number) = outbox[key], key
        if d == 1:
            before = (away[0], number - 1)
        else:
            turn = turns.index(key) - WINDOW
            before = turns[turn] if turn >= 0 else None
        if before in arrived:
            piece = after(piece, arrived[before])
        return exchange(piece, d, "store", "spans%d_" % number)

    for number in range(1, count):
        keys = [key for key in later if key[1] == number]
        coming = [leave(key) for key in keys]
        here = [(d, number - 1) for d in away if (d, number - 1) in arrived]
        if number == 2:
            state, _ = block([key for key in here if key[0] > 1], state)
            here = [key for key in here if key[0] == 1]
        if 2 <= number < n_store.bit_length() + 1:
            state = [after(state[0], next(steps)), *state[1:]]
        state, _ = block(here, state)
        arrived.update(zip(keys, behind(coming, state)))

    keys = [(d, count - 1) for d in away[::-1] if (d, count - 1) in arrived]
    size = 6
    batches = [keys[i : i + size] for i in range(0, len(keys), size)]
    *_, fresh = steps
    for i, keys in enumerate(batches):
        last = i == len(batches) - 1
        state, rows = block(keys, state, fresh if last else None, last)
    return (state[0][None], rows.reshape(1, span_count, recomp, kv_cols))


def solution(mesh):
    in_specs = (
        P(("groups", "store"), None, "tensor"),
        P(("groups", "store"), None, "tensor"),
        P(("groups", "store"), None, "tensor"),
        P("groups"),
        P("groups", None),
        P(("groups", "store"), None, None),
        P(("groups", "store"), None, None, None),
        P("store", "tensor"),
    )
    out_specs = (
        P(("groups", "store"), None, "tensor"),
        P(("groups", "store"), None, None, "tensor"),
    )
    return jax.shard_map(local, mesh=mesh, in_specs=in_specs, out_specs=out_specs, check_vma=False)
```
